32 devices in a mesh: seq: 16 (over z, y, x), wa: 2 (over core).
Axes of the slice: x: 2, y: 2, z: 4, core: 2. Of those that a mesh axis runs over, the one named last changes fastest.
Arguments:
- stream: bfloat16 [2, 49152, 800], P('wa', 'seq'), may hold values from -6 to 6
- doc_start: int32 [2, 49152], P('wa', 'seq'), may hold values from 0 to 49151, as said below
- doc_end: int32 [2, 49152], P('wa', 'seq'), may hold values from 1 to 49152, as said below
- cotangent: bfloat16 [2, 49152, 800], P('wa', 'seq'), may hold values from -6 to 6
- encoder_first_gain: bfloat16 [800], P('wa'), may hold values from 0.25 to 1.75
- encoder_first_bias: bfloat16 [800], P('wa'), may hold values from -3 to 3
- encoder_reduce_weight: bfloat16 [800, 400], P(None, 'wa'), may hold values from -0.21875 to 0.21875
- encoder_reduce_bias: bfloat16 [400], P('wa'), may hold values from -3 to 3
- encoder_middle_gain: bfloat16 [400], P('wa'), may hold values from 0.25 to 1.75
- encoder_middle_bias: bfloat16 [400], P('wa'), may hold values from -3 to 3
- encoder_conv_kernel: bfloat16 [5, 400, 400], P(None, 'wa'), may hold values from -0.125 to 0.125
- encoder_conv_bias: bfloat16 [400], P('wa'), may hold values from -3 to 3
- encoder_last_gain: bfloat16 [400], P('wa'), may hold values from 0.25 to 1.75
- encoder_last_bias: bfloat16 [400], P('wa'), may hold values from -3 to 3
- encoder_expand_weight: bfloat16 [400, 800], P('wa'), may hold values from -0.3125 to 0.3125
- encoder_expand_bias: bfloat16 [800], P('wa'), may hold values from -3 to 3
- decoder_first_gain: bfloat16 [800], P('wa'), may hold values from 0.25 to 1.75
- decoder_first_bias: bfloat16 [800], P('wa'), may hold values from -3 to 3
- decoder_reduce_weight: bfloat16 [800, 400], P(None, 'wa'), may hold values from -0.21875 to 0.21875
- decoder_reduce_bias: bfloat16 [400], P('wa'), may hold values from -3 to 3
- decoder_middle_gain: bfloat16 [400], P('wa'), may hold values from 0.25 to 1.75
- decoder_middle_bias: bfloat16 [400], P('wa'), may hold values from -3 to 3
- decoder_conv_kernel: bfloat16 [3, 400, 400], P(None, 'wa'), may hold values from -0.1875 to 0.1875
- decoder_conv_bias: bfloat16 [400], P('wa'), may hold values from -3 to 3
- decoder_last_gain: bfloat16 [400], P('wa'), may hold values from 0.25 to 1.75
- decoder_last_bias: bfloat16 [400], P('wa'), may hold values from -3 to 3
- decoder_expand_weight: bfloat16 [400, 800], P('wa'), may hold values from -0.3125 to 0.3125
- decoder_expand_bias: bfloat16 [800], P('wa'), may hold values from -3 to 3
Outputs:
- block_out: float32 [2, 49152, 800], P('wa', 'seq')
- stream_grad: float32 [2, 49152, 800], P('wa', 'seq')
- encoder_first_gain_grad: float32 [800], P('wa')
- encoder_first_bias_grad: float32 [800], P('wa')
- encoder_reduce_weight_grad: float32 [800, 400], P(None, 'wa')
- encoder_reduce_bias_grad: float32 [400], P('wa')
- encoder_middle_gain_grad: float32 [400], P('wa')
- encoder_middle_bias_grad: float32 [400], P('wa')
- encoder_conv_kernel_grad: float32 [5, 400, 400], P(None, 'wa')
- encoder_conv_bias_grad: float32 [400], P('wa')
- encoder_last_gain_grad: float32 [400], P('wa')
- encoder_last_bias_grad: float32 [400], P('wa')
- encoder_expand_weight_grad: float32 [400, 800], P('wa')
- encoder_expand_bias_grad: float32 [800], P('wa')
- decoder_first_gain_grad: float32 [800], P('wa')
- decoder_first_bias_grad: float32 [800], P('wa')
- decoder_reduce_weight_grad: float32 [800, 400], P(None, 'wa')
- decoder_reduce_bias_grad: float32 [400], P('wa')
- decoder_middle_gain_grad: float32 [400], P('wa')
- decoder_middle_bias_grad: float32 [400], P('wa')
- decoder_conv_kernel_grad: float32 [3, 400, 400], P(None, 'wa')
- decoder_conv_bias_grad: float32 [400], P('wa')
- decoder_last_gain_grad: float32 [400], P('wa')
- decoder_last_bias_grad: float32 [400], P('wa')
- decoder_expand_weight_grad: float32 [400, 800], P('wa')
- decoder_expand_bias_grad: float32 [800], P('wa')
The draws below stay inside these ranges and needn't reach their ends.
Inputs may be any that keep to these rules, and one draw needn't show every extreme that they name: Documents are contiguous runs of positions within a stream; every position's doc_start is the first position of its run. Each stream holds two documents of exactly 4096 characters and otherwise short ones; positions 0 and 49151 are each a document of one character. doc_end is one past the last position of the same run as doc_start, so doc_start[p] <= p < doc_end[p].
All inputs are finite; a program needn't handle non-finite values.
Results may differ from the reference program's by a relative error of at most 0.014.
Values may be sent and summed in bfloat16 or wider, within the bound.
A program may use at most 256 MiB of HBM per device.

```python
import jax
import jax.numpy as jnp
from jax import lax

D = 800
INNER = 400
ENCODER_TAPS = 5
ENCODER_DILATION = 8
DECODER_TAPS = 3
DECODER_DILATION = 16
ROWS = 49152
STREAMS = 2
LONG = 4096


def document_spans(key):

    def one_stream(stream_key):
        first_key, flag_key = jax.random.split(stream_key, 2)
        places = jnp.arange(ROWS, dtype=jnp.int32)
        half = ROWS // 2
        longs = jax.random.randint(first_key, (2,), 2, half - LONG).astype(jnp.int32)
        longs = longs + jnp.array([0, half], dtype=jnp.int32)
        flags = jax.random.randint(flag_key, (ROWS,), 0, 48) == 0
        flags = flags | (places == 0) | (places == 1) | (places == ROWS - 1)
        for index in range(2):
            inside = (places > longs[index]) & (places < longs[index] + LONG)
            flags = flags & jnp.logical_not(inside) | (places == longs[index]) | (places == longs[index] + LONG)
        starts = lax.cummax(jnp.where(flags, places, 0), axis=0)
        marks = jnp.where(flags, places, ROWS)
        marks = jnp.concatenate([marks[1:], jnp.array([ROWS], dtype=jnp.int32)])
        ends = lax.cummin(marks, axis=0, reverse=True)
        return (starts.astype(jnp.int32), ends.astype(jnp.int32))
    return jax.vmap(one_stream)(jax.random.split(key, STREAMS))


def draw_doc_start(key, part):
    spans = document_spans(key)
    return spans[0]


def draw_doc_end(key, part):
    spans = document_spans(key)
    return spans[1]


def block_levels(own_key, extent, shards, least, top_value):
    loudness, own = 1.0, jax.random.fold_in(own_key, 6)
    for axis_at, blocks in shards:
        draws = jnp.exp(jax.random.uniform(jax.random.fold_in(own, axis_at), (blocks,), jnp.float32, least / len(shards), top_value / len(shards)))
        loudness = loudness * jnp.repeat(draws, extent[axis_at] // blocks).reshape([-1 if axis == axis_at else 1 for axis in range(len(extent))])
    return loudness


def gaussian(own_key, dims, scale, bound, shards=(), held_as=jnp.bfloat16):
    values = jax.random.normal(own_key, dims, jnp.float32) * scale
    if len(shards) > 0:
        values = block_levels(own_key, dims, shards, -0.22, 0.18) * values
    return jnp.clip(values, min=-bound, max=bound).astype(held_as)


def setup_inputs(seed: int = 0) -> dict:
    seeds = jax.random.split(jax.random.key(seed), 29)
    stream = gaussian(seeds[0], (STREAMS, ROWS, D), 1.0, 6.0, ((0, 2), (1, 16)))
    doc_start = draw_doc_start(jax.random.fold_in(seeds[28], 71), 0)
    doc_end = draw_doc_end(jax.random.fold_in(seeds[28], 71), 0)
    cotangent = gaussian(seeds[3], (STREAMS, ROWS, D), 1.0, 6.0, ((0, 2), (1, 16)))
    encoder_first_gain = jnp.clip(1.0 + 0.15 * jax.random.normal(seeds[4], (D,), jnp.float32), 0.25, 1.75).astype(jnp.bfloat16)
    encoder_first_bias = gaussian(seeds[5], (D,), 0.3, 3.0, ((0, 2),))
    encoder_reduce_weight = gaussian(seeds[6], (D, INNER), D ** -0.5, 0.21875, ((1, 2),))
    encoder_reduce_bias = gaussian(seeds[7], (INNER,), 0.3, 3.0, ((0, 2),))
    encoder_middle_gain = jnp.clip(1.0 + 0.15 * jax.random.normal(seeds[8], (INNER,), jnp.float32), 0.25, 1.75).astype(jnp.bfloat16)
    encoder_middle_bias = gaussian(seeds[9], (INNER,), 0.3, 3.0, ((0, 2),))
    encoder_conv_kernel = gaussian(seeds[10], (ENCODER_TAPS, INNER, INNER), (ENCODER_TAPS * INNER) ** -0.5, 0.125, ((1, 2),))
    encoder_conv_bias = gaussian(seeds[11], (INNER,), 0.3, 3.0, ((0, 2),))
    encoder_last_gain = jnp.clip(1.0 + 0.15 * jax.random.normal(seeds[12], (INNER,), jnp.float32), 0.25, 1.75).astype(jnp.bfloat16)
    encoder_last_bias = gaussian(seeds[13], (INNER,), 0.3, 3.0, ((0, 2),))
    encoder_expand_weight = gaussian(seeds[14], (INNER, D), INNER ** -0.5, 0.3125, ((0, 2),))
    encoder_expand_bias = gaussian(seeds[15], (D,), 0.3, 3.0, ((0, 2),))
    decoder_first_gain = jnp.clip(1.0 + 0.15 * jax.random.normal(seeds[16], (D,), jnp.float32), 0.25, 1.75).astype(jnp.bfloat16)
    decoder_first_bias = gaussian(seeds[17], (D,), 0.3, 3.0, ((0, 2),))
    decoder_reduce_weight = gaussian(seeds[18], (D, INNER), D ** -0.5, 0.21875, ((1, 2),))
    decoder_reduce_bias = gaussian(seeds[19], (INNER,), 0.3, 3.0, ((0, 2),))
    decoder_middle_gain = jnp.clip(1.0 + 0.15 * jax.random.normal(seeds[20], (INNER,), jnp.float32), 0.25, 1.75).astype(jnp.bfloat16)
    decoder_middle_bias = gaussian(seeds[21], (INNER,), 0.3, 3.0, ((0, 2),))
    decoder_conv_kernel = gaussian(seeds[22], (DECODER_TAPS, INNER, INNER), (DECODER_TAPS * INNER) ** -0.5, 0.1875, ((1, 2),))
    decoder_conv_bias = gaussian(seeds[23], (INNER,), 0.3, 3.0, ((0, 2),))
    decoder_last_gain = jnp.clip(1.0 + 0.15 * jax.random.normal(seeds[24], (INNER,), jnp.float32), 0.25, 1.75).astype(jnp.bfloat16)
    decoder_last_bias = gaussian(seeds[25], (INNER,), 0.3, 3.0, ((0, 2),))
    decoder_expand_weight = gaussian(seeds[26], (INNER, D), INNER ** -0.5, 0.3125, ((0, 2),))
    decoder_expand_bias = gaussian(seeds[27], (D,), 0.3, 3.0, ((0, 2),))
    return dict(stream=stream, doc_start=doc_start, doc_end=doc_end, cotangent=cotangent, encoder_first_gain=encoder_first_gain, encoder_first_bias=encoder_first_bias, encoder_reduce_weight=encoder_reduce_weight, encoder_reduce_bias=encoder_reduce_bias, encoder_middle_gain=encoder_middle_gain, encoder_middle_bias=encoder_middle_bias, encoder_conv_kernel=encoder_conv_kernel, encoder_conv_bias=encoder_conv_bias, encoder_last_gain=encoder_last_gain, encoder_last_bias=encoder_last_bias, encoder_expand_weight=encoder_expand_weight, encoder_expand_bias=encoder_expand_bias, decoder_first_gain=decoder_first_gain, decoder_first_bias=decoder_first_bias, decoder_reduce_weight=decoder_reduce_weight, decoder_reduce_bias=decoder_reduce_bias, decoder_middle_gain=decoder_middle_gain, decoder_middle_bias=decoder_middle_bias, decoder_conv_kernel=decoder_conv_kernel, decoder_conv_bias=decoder_conv_bias, decoder_last_gain=decoder_last_gain, decoder_last_bias=decoder_last_bias, decoder_expand_weight=decoder_expand_weight, decoder_expand_bias=decoder_expand_bias)


@jax.custom_vjp
def low(v):
    return lax.optimization_barrier(v.astype(jnp.bfloat16)).astype(jnp.float32)

@jax.custom_vjp
def low_back(v):
    return v

def low_keep(v):
    return (low(v), None)

def low_pass(kept, grad):
    return (grad,)

def back_keep(v):
    return (v, None)

def back_low(kept, grad):
    return (low(grad),)
low.defvjp(low_keep, low_pass)
low_back.defvjp(back_keep, back_low)
EPS = 1e-05

def norm_act(value, gain, bias):
    centre = value - lax.optimization_barrier(jnp.mean(value, axis=-1, keepdims=True))
    spread = lax.optimization_barrier(jnp.mean(centre * centre, axis=-1, keepdims=True))
    return jax.nn.gelu(centre * lax.rsqrt(spread + EPS) * gain + bias)

def matmul(left, right):
    return jnp.einsum('srd,de->sre', left, right, precision=lax.Precision.HIGHEST)

def dilated(hidden, kernel, starts, ends, offsets):
    length = hidden.shape[1]
    margin = 64
    padded = jnp.pad(hidden, ((0, 0), (margin, margin), (0, 0)))
    places = jnp.arange(length, dtype=jnp.int32)[None, :]
    total = jnp.zeros((hidden.shape[0], length, kernel.shape[2]), jnp.float32)
    for index, offset in enumerate(offsets):
        tapped = padded[:, margin + offset:margin + offset + length]
        source = places + offset
        usable = (source >= starts) & (source < ends)
        tapped = jnp.where(usable[..., None], tapped, 0.0)
        total = total + matmul(tapped, kernel[index])
    return total

def block(value, params, starts, ends, offsets):
    first_gain, first_bias, reduce_weight, reduce_bias, middle_gain, middle_bias, conv_kernel, conv_bias, last_gain, last_bias, expand_weight, expand_bias = params
    first = low(norm_act(value, first_gain, first_bias))
    inner = low_back(matmul(first, reduce_weight) + reduce_bias)
    middle = low(norm_act(inner, middle_gain, middle_bias))
    mixed = low_back(dilated(middle, conv_kernel, starts, ends, offsets) + conv_bias)
    last = low(norm_act(mixed, last_gain, last_bias))
    branch = low_back(matmul(last, expand_weight) + expand_bias)
    return value + branch

def reference(stream, doc_start, doc_end, cotangent, encoder_first_gain, encoder_first_bias, encoder_reduce_weight, encoder_reduce_bias, encoder_middle_gain, encoder_middle_bias, encoder_conv_kernel, encoder_conv_bias, encoder_last_gain, encoder_last_bias, encoder_expand_weight, encoder_expand_bias, decoder_first_gain, decoder_first_bias, decoder_reduce_weight, decoder_reduce_bias, decoder_middle_gain, decoder_middle_bias, decoder_conv_kernel, decoder_conv_bias, decoder_last_gain, decoder_last_bias, decoder_expand_weight, decoder_expand_bias):
    params = [encoder_first_gain, encoder_first_bias, encoder_reduce_weight, encoder_reduce_bias, encoder_middle_gain, encoder_middle_bias, encoder_conv_kernel, encoder_conv_bias, encoder_last_gain, encoder_last_bias, encoder_expand_weight, encoder_expand_bias, decoder_first_gain, decoder_first_bias, decoder_reduce_weight, decoder_reduce_bias, decoder_middle_gain, decoder_middle_bias, decoder_conv_kernel, decoder_conv_bias, decoder_last_gain, decoder_last_bias, decoder_expand_weight, decoder_expand_bias]
    params = [item.astype(jnp.float32) for item in params]
    encoder_tap_offsets = [ENCODER_DILATION * (tap_index - ENCODER_TAPS // 2) for tap_index in range(ENCODER_TAPS)]
    decoder_tap_offsets = [-DECODER_DILATION * (DECODER_TAPS - 1 - tap_index) for tap_index in range(DECODER_TAPS)]

    def forward(value, *weights):
        middle = block(value, weights[:12], doc_start, doc_end, encoder_tap_offsets)
        return block(middle, weights[12:], doc_start, doc_end, decoder_tap_offsets)
    result, pull = jax.vjp(forward, stream.astype(jnp.float32), *params)
    grads = pull(cotangent.astype(jnp.float32))
    return (result, grads[0], grads[1], grads[2], grads[3], grads[4], grads[5], grads[6], grads[7], grads[8], grads[9], grads[10], grads[11], grads[12], grads[13], grads[14], grads[15], grads[16], grads[17], grads[18], grads[19], grads[20], grads[21], grads[22], grads[23], grads[24])
```

```python
import functools

import jax
import jax.numpy as jnp
from jax import lax
from jax.experimental import pallas as pl
from jax.experimental.pallas import tpu as pltpu
from jax.sharding import PartitionSpec as P

ENCODER_TAPS = 5
ENCODER_DILATION = 8
DECODER_TAPS = 3
DECODER_DILATION = 16
EPS = 1e-05

MESH = pl.DeviceIdType.MESH
BF = jnp.bfloat16
F32 = jnp.float32
LANES = 128
TILE = 512
HALF = 256
AUG = 16
VMEM_LIMIT = 56 * 1024 * 1024
GELU_1 = 2.0 * 0.7978845608028654
GELU_3 = 8.0 * 0.7978845608028654 * 0.044715

ENCODER_SHIFTS = tuple(ENCODER_DILATION * (j - ENCODER_TAPS // 2) for j in range(ENCODER_TAPS))
DECODER_SHIFTS = tuple(-DECODER_DILATION * (DECODER_TAPS - 1 - j) for j in range(DECODER_TAPS))


def params(collective=None):
    if collective is None:
        return pltpu.CompilerParams(vmem_limit_bytes=VMEM_LIMIT)
    return pltpu.CompilerParams(
        vmem_limit_bytes=VMEM_LIMIT, collective_id=collective, has_side_effects=True
    )


def whole(shape):
    return pl.BlockSpec(shape, lambda *_: (0,) * len(shape))


def nt_dot(left, right):
    return lax.dot_general(left, right, (((1,), (1,)), ((), ())), preferred_element_type=F32)


def nn_dot(left, right):
    return jnp.dot(left, right, preferred_element_type=F32)


def lanes_of(column, width):
    return jnp.concatenate([column] * (width // LANES), axis=1)


def fold(value):
    total = value[:, :LANES]
    for at in range(LANES, value.shape[1], LANES):
        total = total + value[:, at : at + LANES]
    return total


def weights_kernel(dims, *refs):
    d, inner, taps = dims
    n_in = 24
    ins, refs = refs[:n_in], refs[n_in:]
    outs, refs = refs[:24], refs[24:]
    (small_own, small_got, k_own0, k_own1, e_own0, e_own1, r_own0, r_own1, *rest) = refs
    (r_got0, r_got1, k_got0, k_got1, e_got0, e_got1, send, recv) = rest
    me = lax.axis_index("wa")
    other = 1 - me
    barrier = pltpu.get_barrier_semaphore()
    pl.semaphore_signal(barrier, inc=1, device_id={"wa": other}, device_id_type=MESH)
    pl.semaphore_wait(barrier, 1)

    half = inner // 2
    pad = k_own0.shape[1]
    small_own[...] = jnp.zeros_like(small_own)
    small_at = []
    for side in range(2):
        for at in (0, 1, 3, 4, 5, 7, 8, 9, 11):
            small_at.append(12 * side + at)
    for row, at in enumerate(small_at):
        n = ins[at].shape[0]
        small_own[row : row + 1, 0:n] = ins[at][...].astype(F32).reshape(1, n)
    owns, gots = [], []
    for side, (k_own, e_own, r_own) in enumerate(((k_own0, e_own0, r_own0), (k_own1, e_own1, r_own1))):
        base = 12 * side
        k_own[:, half - 8 : pad, :] = jnp.zeros((taps[side], pad - half + 8, inner), BF)
        k_own[:, 0:half, :] = ins[base + 6][...]
        e_own[half - 8 : pad, :] = jnp.zeros((pad - half + 8, d), BF)
        e_own[0:half, :] = ins[base + 10][...]
        r_own[half - 8 : pad, :] = jnp.zeros((pad - half + 8, d), BF)
        r_own[0:half, :] = ins[base + 2][...]
        owns += [r_own, k_own, e_own]
    owns.append(small_own)
    gots = [r_got0, k_got0, e_got0, r_got1, k_got1, e_got1, small_got]
    copies = []
    for at, (own, got) in enumerate(zip(owns, gots)):
        copies.append(
            pltpu.make_async_remote_copy(
                src_ref=own,
                dst_ref=got,
                send_sem=send.at[at],
                recv_sem=recv.at[at],
                device_id={"wa": other},
                device_id_type=MESH,
            )
        )
        copies[-1].start()
    for copy in copies:
        copy.wait()

    first_core = me == 0

    def ordered(own, got):
        own, got = own.astype(F32), got.astype(F32)
        return jnp.where(first_core, own, got), jnp.where(first_core, got, own)

    small0, small1 = ordered(small_own[...], small_got[...])

    def column(row, n):
        line = jnp.concatenate([small0[row : row + 1, 0 : n // 2], small1[row : row + 1, 0 : n // 2]], axis=1)
        return jnp.broadcast_to(line, (LANES, n)).T

    def bias_columns(value):
        where = lax.broadcasted_iota(jnp.int32, (value.shape[0], AUG), 1) == 0
        return jnp.where(where, value[:, :AUG], 0.0).astype(BF)

    for side in range(2):
        o = outs[12 * side : 12 * side + 12]
        wrt, kt, wet, we, kb, wr, g1, b1, g2, b2, g3, b3 = o
        base = 9 * side
        g1[...] = column(base + 0, d)
        b1[...] = column(base + 1, d)
        g2[...] = column(base + 3, inner)
        b2[...] = column(base + 4, inner)
        g3[...] = column(base + 6, inner)
        b3[...] = column(base + 7, inner)
        n = taps[side]
        r0, r1 = ordered(owns[3 * side][0:half, :], gots[3 * side][0:half, :])
        r = jnp.concatenate([r0, r1], axis=0)
        wr[...] = r.T.astype(BF)
        wrt[:, 0:d] = r.astype(BF)
        wrt[:, d : d + AUG] = bias_columns(column(base + 2, inner))
        e0, e1 = ordered(owns[3 * side + 2][0:half, :], gots[3 * side + 2][0:half, :])
        e = jnp.concatenate([e0, e1], axis=0)
        we[...] = e.astype(BF)
        wet[:, 0:inner] = e.T.astype(BF)
        wet[:, inner : inner + AUG] = bias_columns(column(base + 8, d))
        for j in range(n):
            k0, k1 = ordered(owns[3 * side + 1][j, 0:half, :], gots[3 * side + 1][j, 0:half, :])
            k = jnp.concatenate([k0, k1], axis=0)
            kb[:, j * inner : (j + 1) * inner] = k.astype(BF)
            kt[:, j * inner : (j + 1) * inner] = k.T.astype(BF)
        kt[:, n * inner : n * inner + AUG] = bias_columns(column(base + 5, inner))


def gather_weights(args, d, inner):
    taps = (ENCODER_TAPS, DECODER_TAPS)
    half = inner // 2
    pad = -(-half // 16) * 16
    shapes = []
    for n in taps:
        shapes += [
            ((inner, d + AUG), BF),
            ((inner, n * inner + AUG), BF),
            ((d, inner + AUG), BF),
            ((inner, d), BF),
            ((inner, n * inner), BF),
            ((d, inner), BF),
            ((d, LANES), F32),
            ((d, LANES), F32),
            ((inner, LANES), F32),
            ((inner, LANES), F32),
            ((inner, LANES), F32),
            ((inner, LANES), F32),
        ]
    vm = pl.BlockSpec(memory_space=pltpu.VMEM)
    small = pltpu.VMEM((24, 512), F32)
    kk = [pltpu.VMEM((n, pad, inner), BF) for n in taps]
    ee = [pltpu.VMEM((pad, d), BF)] * 2
    outs = pl.pallas_call(
        functools.partial(weights_kernel, (d, inner, taps)),
        out_shape=[jax.ShapeDtypeStruct(*s) for s in shapes],
        in_specs=[vm] * 24,
        out_specs=[vm] * 24,
        scratch_shapes=[small, small, *kk, *ee, *ee, *ee, *kk, *ee]
        + [pltpu.SemaphoreType.DMA((7,)), pltpu.SemaphoreType.DMA((7,))],
        compiler_params=params(0),
        name="gather_weights",
    )(*args)
    return outs[:12], outs[12:]


def statistics(src, lanes, channels):
    width = lanes.stop - lanes.start
    total = [jnp.zeros((8, width), F32) for _ in range(4)]
    for g in range(channels // 8):
        total[g % 4] = total[g % 4] + src[8 * g : 8 * g + 8, lanes]
    mean = jnp.sum((total[0] + total[1]) + (total[2] + total[3]), axis=0, keepdims=True) * (1.0 / channels)
    wide = jnp.broadcast_to(mean, (8, width))
    total = [jnp.zeros((8, width), F32) for _ in range(4)]
    for g in range(channels // 8):
        centre = src[8 * g : 8 * g + 8, lanes] - wide
        total[g % 4] = total[g % 4] + centre * centre
    spread = jnp.sum((total[0] + total[1]) + (total[2] + total[3]), axis=0, keepdims=True) * (1.0 / channels)
    return mean, lax.rsqrt(spread + EPS)


def norm_forward(src, lanes, channels, gain, bias, h_out, z_out, d_out, r_out):
    width = lanes.stop - lanes.start
    mean, r = statistics(src, lanes, channels)
    if r_out is not None:
        r_out[:, lanes] = jnp.broadcast_to(r, (8, width))
    rw = jnp.broadcast_to(r, (16, width))
    mw = jnp.broadcast_to(mean * r, (16, width))
    for c in range(0, channels, 16):
        rows = slice(c, c + 16)
        z = src[rows, lanes] * rw - mw
        half = z * lanes_of(gain[rows, :] * 0.5, width) + lanes_of(bias[rows, :] * 0.5, width)
        sq = half * half
        t = jnp.tanh(half * (sq * GELU_3 + GELU_1))
        h_out[rows, lanes] = (half + half * t).astype(BF)
        slope = (1.0 + t) * (0.5 + (half * (sq * (1.5 * GELU_3) + 0.5 * GELU_1)) * (1.0 - t))
        z_out[rows, lanes] = z.astype(BF)
        d_out[rows, lanes] = slope.astype(BF)


def norm_backward(grad, lanes, channels, gain, z_in, d_in, r_in, gain_sum, bias_sum, emit):
    width = lanes.stop - lanes.start
    one = [jnp.zeros((8, width), F32) for _ in range(2)]
    two = [jnp.zeros((8, width), F32) for _ in range(2)]
    for c in range(0, channels, 16):
        rows = slice(c, c + 16)
        da = grad[rows, lanes] * d_in[rows, lanes].astype(F32)
        p = da * z_in[rows, lanes].astype(F32)
        bias_sum[rows, :] += fold(da)
        gain_sum[rows, :] += fold(p)
        wide = lanes_of(gain[rows, :], width)
        dz = da * wide
        q = p * wide
        grad[rows, lanes] = dz
        for at in range(2):
            one[at] = one[at] + dz[8 * at : 8 * at + 8]
            two[at] = two[at] + q[8 * at : 8 * at + 8]
    r = r_in[0:1, lanes]
    scale = r * (1.0 / channels)
    m1 = jnp.broadcast_to(jnp.sum(one[0] + one[1], axis=0, keepdims=True) * scale, (16, width))
    m2 = jnp.broadcast_to(jnp.sum(two[0] + two[1], axis=0, keepdims=True) * scale, (16, width))
    rw = jnp.broadcast_to(r, (16, width))
    for c in range(0, channels, 16):
        rows = slice(c, c + 16)
        emit(rows, grad[rows, lanes] * rw - m1 - z_in[rows, lanes].astype(F32) * m2)


def tap_mask(starts, ends, first, shift):
    place = first + shift + lax.broadcasted_iota(jnp.int32, (8, TILE), 1)
    usable = (place >= jnp.broadcast_to(starts[...], (8, TILE))) & (place < jnp.broadcast_to(ends[...], (8, TILE)))
    one = jnp.where(usable, 1.0, 0.0)
    return jnp.concatenate([one, one], axis=0).astype(BF)


def stack_taps(stack, shifts, before, main, after, starts, ends, first, inner):
    for j, shift in enumerate(shifts):
        if not shift:
            stack[j * inner : (j + 1) * inner, :] = main[0:inner, :]
            continue
        mask = tap_mask(starts, ends, first, shift)
        for c in range(0, inner, 16):
            rows = slice(c, c + 16)
            if shift < 0:
                span = jnp.concatenate([before[rows, :], main[rows, :]], axis=1)
                span = pltpu.roll(span, -shift, 1)[:, LANES:]
            else:
                span = jnp.concatenate([main[rows, :], after[rows, :]], axis=1)
                span = pltpu.roll(span, TILE + LANES - shift, 1)[:, :TILE]
            stack[j * inner + c : j * inner + c + 16, :] = span * mask


def ones_rows(width):
    where = lax.broadcasted_iota(jnp.int32, (AUG, width), 0) == 0
    return jnp.where(where, 1.0, 0.0).astype(BF)


def neighbours():
    me = lax.axis_index("seq")
    n = lax.axis_size("seq")
    return lax.rem(me + n - 1, n), lax.rem(me + 1, n)


def greet(left, right):
    barrier = pltpu.get_barrier_semaphore()
    for device in (left, right):
        pl.semaphore_signal(barrier, inc=1, device_id={"seq": device}, device_id_type=MESH)
    pl.semaphore_wait(barrier, 2)


def send_copy(src, dst, sems, device):
    return pltpu.make_async_remote_copy(
        src_ref=src,
        dst_ref=dst,
        send_sem=sems.at[0],
        recv_sem=sems.at[1],
        device_id={"seq": device},
        device_id_type=MESH,
    )


def share_edges(kind, step, steps, inner, source, edges, scratch):
    left, right = neighbours()
    own_r = got_r = own_l = got_l = None
    if kind == "both":
        own_r, got_r, sem_r, own_l, got_l, sem_l = scratch
    elif kind == "right":
        own_r, got_r, sem_r = scratch
    else:
        own_l, got_l, sem_l = scratch

    @pl.when(step == 0)
    def _():
        greet(left, right)
        if own_r is not None:
            own_r[...] = source[0:inner, TILE - LANES : TILE]
            send_copy(own_r, got_r, sem_r, right).start()

    if own_l is not None:

        @pl.when(step == 1)
        def _():
            own_l[...] = source[0:inner, 0:LANES]
            send_copy(own_l, got_l, sem_l, left).start()

    @pl.when(step == steps - 1)
    def _():
        at = 0
        if own_r is not None:
            send_copy(own_r, got_r, sem_r, right).wait()
            edges[at][...] = got_r[...]
            at += 1
        if own_l is not None:
            send_copy(own_l, got_l, sem_l, left).wait()
            edges[at][...] = got_l[...]


def edge_scratch(kind, inner):
    one = [pltpu.VMEM((inner, LANES), BF), pltpu.VMEM((inner, LANES), BF), pltpu.SemaphoreType.DMA((2,))]
    return one * 2 if kind == "both" else one


def first_place(step, steps):
    return lax.axis_index("seq") * (steps * TILE) + lax.rem(step + steps - 1, steps) * TILE


CHAINS = (slice(0, HALF), slice(HALF, TILE))


def enc_in_kernel(steps, x, wrt, g1, b1, g2, b2, h1, z1, d1, r1, h2, z2, d2, r2, e_l, e_r, xt, u, *edge):
    step = pl.program_id(0)
    d, inner = x.shape[0], wrt.shape[0]
    h1[d : d + AUG, :] = ones_rows(TILE)
    h2[inner : inner + AUG, :] = ones_rows(TILE)
    for lanes in CHAINS:
        xt[:, lanes] = x[:, lanes].astype(F32)
        norm_forward(xt, lanes, d, g1, b1, h1, z1, d1, r1)
    for lanes in CHAINS:
        u[:, lanes] = nn_dot(wrt[...], h1[:, lanes])
    for lanes in CHAINS:
        norm_forward(u, lanes, inner, g2, b2, h2, z2, d2, r2)
    share_edges("both", step, steps, inner, h2, (e_l, e_r), edge)


def enc_out_kernel(
    steps, starts, ends, before, main, after, e_l, e_r, xt, kt, wet, wrt, g3, b3, g1, b1, g2, b2,
    h3, z3, d3, r3, x1, h1, z1, d1, r1, h2, z2, d2, r2, edge_o,
    stack, win_b, win_a, v, y, u, *edge,
):
    step = pl.program_id(0)
    d, inner = xt.shape[0], v.shape[0]
    win_b[...] = jnp.where(step == 1, e_l[...], before[0:inner, :])
    win_a[...] = jnp.where(step == 0, e_r[...], after[0:inner, :])
    stack_taps(stack, ENCODER_SHIFTS, win_b, main, win_a, starts, ends, first_place(step, steps), inner)
    stack[len(ENCODER_SHIFTS) * inner :, :] = ones_rows(TILE)
    h3[inner : inner + AUG, :] = ones_rows(TILE)
    h1[d : d + AUG, :] = ones_rows(TILE)
    h2[inner : inner + AUG, :] = ones_rows(TILE)
    for lanes in CHAINS:
        v[:, lanes] = nn_dot(kt[...], stack[:, lanes])
    for lanes in CHAINS:
        norm_forward(v, lanes, inner, g3, b3, h3, z3, d3, r3)
    for lanes in CHAINS:
        y[:, lanes] = nn_dot(wet[...], h3[:, lanes])
    for lanes in CHAINS:
        for c in range(0, d, 16):
            rows = slice(c, c + 16)
            total = y[rows, lanes] + xt[rows, lanes].astype(F32)
            y[rows, lanes] = total
            x1[rows, lanes] = total.astype(BF)
        norm_forward(y, lanes, d, g1, b1, h1, z1, d1, r1)
    for lanes in CHAINS:
        u[:, lanes] = nn_dot(wrt[...], h1[:, lanes])
    for lanes in CHAINS:
        norm_forward(u, lanes, inner, g2, b2, h2, z2, d2, r2)
    share_edges("right", step, steps, inner, h2, (edge_o,), edge)


def dec_out_kernel(
    steps, starts, ends, before, main, e_l, cot_t, kt, we, g3, b3,
    h3, evr, edge_o, dwe, dg3, db3,
    stack, win_b, v, z3, d3, r3, g, *edge,
):
    step = pl.program_id(0)
    inner = v.shape[0]

    @pl.when(step == 0)
    def _():
        dwe[...] = jnp.zeros_like(dwe)
        dg3[...] = jnp.zeros_like(dg3)
        db3[...] = jnp.zeros_like(db3)

    win_b[...] = jnp.where(step == 1, e_l[...], before[0:inner, :])
    stack_taps(stack, DECODER_SHIFTS, win_b, main, None, starts, ends, first_place(step, steps), inner)
    stack[len(DECODER_SHIFTS) * inner :, :] = ones_rows(TILE)
    h3[inner : inner + AUG, :] = ones_rows(TILE)
    for lanes in CHAINS:
        v[:, lanes] = nn_dot(kt[...], stack[:, lanes])
    for lanes in CHAINS:
        g[:, lanes] = nn_dot(we[...], cot_t[:, lanes])
    for lanes in CHAINS:
        norm_forward(v, lanes, inner, g3, b3, h3, z3, d3, r3)
    dwe[...] += nt_dot(h3[...], cot_t[...])

    for lanes in CHAINS:

        def emit(rows, value):
            evr[rows, lanes] = value.astype(BF)

        norm_backward(g, lanes, inner, g3, z3, d3, r3, dg3, db3, emit)
    share_edges("left", step, steps, inner, evr, (edge_o,), edge)


def dec_back_kernel(
    steps, starts, ends, main, after, e_r, kb, wr, we, g2, g1, g3,
    h2, z2, d2, r2, h1, z1, d1, r1, cot_t, h3, z3, d3, r3,
    ey, evr, e_l2, e_r2, dk, dwrt, dwe, dg2, db2, dg1, db1, dg3, db3,
    stack, win_a, g, big, eur, *edge,
):
    step = pl.program_id(0)
    d, inner = cot_t.shape[0], g.shape[0]

    @pl.when(step == 0)
    def _():
        for ref in (dk, dwrt, dwe, dg2, db2, dg1, db1, dg3, db3):
            ref[...] = jnp.zeros_like(ref)

    win_a[...] = jnp.where(step == 0, e_r[...], after[0:inner, :])
    back = tuple(-s for s in DECODER_SHIFTS)
    stack_taps(stack, back, None, main, win_a, starts, ends, first_place(step, steps), inner)
    for lanes in CHAINS:
        g[:, lanes] = nn_dot(kb[...], stack[:, lanes])
    dk[...] += nt_dot(h2[...], stack[...])
    for lanes in CHAINS:

        def emit_u(rows, value):
            eur[rows, lanes] = value.astype(BF)

        norm_backward(g, lanes, inner, g2, z2, d2, r2, dg2, db2, emit_u)
    for lanes in CHAINS:
        big[:, lanes] = nn_dot(wr[...], eur[:, lanes])
    dwrt[...] += nt_dot(eur[...], h1[...])
    for lanes in CHAINS:

        def emit_x(rows, value):
            ey[rows, lanes] = (value + cot_t[rows, lanes].astype(F32)).astype(BF)

        norm_backward(big, lanes, d, g1, z1, d1, r1, dg1, db1, emit_x)
    for lanes in CHAINS:
        g[:, lanes] = nn_dot(we[...], ey[:, lanes])
    dwe[...] += nt_dot(h3[...], ey[...])
    for lanes in CHAINS:

        def emit_v(rows, value):
            evr[rows, lanes] = value.astype(BF)

        norm_backward(g, lanes, inner, g3, z3, d3, r3, dg3, db3, emit_v)
    share_edges("both", step, steps, inner, evr, (e_l2, e_r2), edge)


def enc_back_kernel(
    steps, starts, ends, before, main, after, e_l, e_r, kb, wr, wet, g2, g1,
    h2, z2, d2, r2, h1, z1, d1, r1, ey, x1, h3,
    out, grad, dk, dwrt, dg2, db2, dg1, db1,
    stack, win_b, win_a, g, big, eur,
):
    step = pl.program_id(0)
    d, inner = ey.shape[0], g.shape[0]

    @pl.when(step == 0)
    def _():
        for ref in (dk, dwrt, dg2, db2, dg1, db1):
            ref[...] = jnp.zeros_like(ref)

    win_b[...] = jnp.where(step == 1, e_l[...], before[0:inner, :])
    win_a[...] = jnp.where(step == 0, e_r[...], after[0:inner, :])
    back = tuple(-s for s in ENCODER_SHIFTS)
    stack_taps(stack, back, win_b, main, win_a, starts, ends, first_place(step, steps), inner)
    for lanes in CHAINS:
        g[:, lanes] = nn_dot(kb[...], stack[:, lanes])
    for lanes in CHAINS:
        out[:, lanes] = nn_dot(wet[...], h3[:, lanes]) + x1[:, lanes].astype(F32)
    dk[...] += nt_dot(h2[...], stack[...])
    for lanes in CHAINS:

        def emit_u(rows, value):
            eur[rows, lanes] = value.astype(BF)

        norm_backward(g, lanes, inner, g2, z2, d2, r2, dg2, db2, emit_u)
    for lanes in CHAINS:
        big[:, lanes] = nn_dot(wr[...], eur[:, lanes])
    dwrt[...] += nt_dot(eur[...], h1[...])
    for lanes in CHAINS:

        def emit_x(rows, value):
            grad[rows, lanes] = value + ey[rows, lanes].astype(F32)

        norm_backward(big, lanes, d, g1, z1, d1, r1, dg1, db1, emit_x)


def sections(d, inner):
    return (
        ("e_we", d),
        ("e_k", ENCODER_TAPS * inner),
        ("e_wr", d + AUG),
        ("d_we", d),
        ("d_k", DECODER_TAPS * inner),
        ("d_wr", d + AUG),
    )


def section_blocks(d, inner):
    starts, at = {}, 0
    for name, used in sections(d, inner):
        starts[name] = at
        at += -(-used // LANES)
    starts["vec"] = at
    return starts, at + 1


def reduce_kernel(plan, *refs):
    d, inner, n, streams, per = plan
    half = inner // 2
    starts, blocks = section_blocks(d, inner)
    mats, vecs, refs = refs[:6], refs[6:18], refs[18:]
    out, pack, got, rs_got, wa_sem, rs_send, rs_recv, ag_send, ag_recv = refs
    me = lax.axis_index("wa")
    seq = lax.axis_index("seq")
    bits = []
    bit = 1
    while bit < n:
        bits.append(bit)
        bit *= 2

    barrier = pltpu.get_barrier_semaphore()
    pl.semaphore_signal(barrier, inc=1, device_id={"wa": 1 - me}, device_id_type=MESH)
    partners = []
    for b in bits:
        low = lax.rem(lax.div(seq, b), 2)
        partners.append(seq + b - 2 * b * low)
        pl.semaphore_signal(barrier, inc=1, device_id={"seq": partners[-1]}, device_id_type=MESH)
    pl.semaphore_wait(barrier, 1 + len(bits))

    rows_of = 13

    def put(w, tile, value):
        pack[w, tile] = value.astype(BF)

    def rows16(ref, w, r, lanes):
        base = half * w
        if r < rows_of - 1:
            return ref[base + 16 * r : base + 16 * r + 16, lanes]
        top = ref[base + 16 * r : base + 16 * r + 8, lanes]
        if ref.shape[0] > inner:
            return jnp.concatenate([top, ref[inner : inner + 8, lanes]], axis=0)
        return jnp.concatenate([top, jnp.zeros_like(top)], axis=0)

    for w in range(2):
        for (name, used), ref in zip(sections(d, inner), mats):
            count = -(-used // LANES)
            for b in range(count):
                stop = min(used, LANES * (b + 1))
                width = stop - LANES * b
                for r in range(rows_of):
                    value = rows16(ref, w, r, slice(LANES * b, stop))
                    if width < LANES:
                        value = jnp.concatenate([value, jnp.zeros((16, LANES - width), F32)], axis=1)
                    put(w, (starts[name] + b) * rows_of + r, value)
        columns = []
        for ref in vecs:
            total = jnp.sum(ref[...], axis=1, keepdims=True)
            if ref.shape[0] == d:
                columns.append(total[half * 2 * w : half * (2 * w + 1)])
                columns.append(total[half * (2 * w + 1) : half * (2 * w + 2)])
            else:
                columns.append(total[half * w : half * (w + 1)])
        lane = lax.broadcasted_iota(jnp.int32, (half, LANES), 1)
        value = jnp.zeros((half, LANES), F32)
        for at, column in enumerate(columns):
            value = jnp.where(lane == at, column, value)
        value = jnp.concatenate([value, jnp.zeros((rows_of * 16 - half, LANES), F32)], axis=0)
        for r in range(rows_of):
            put(w, starts["vec"] * rows_of + r, value[16 * r : 16 * r + 16])
        filled = blocks * rows_of
        if streams * per > filled:
            pack[w, filled : streams * per] = jnp.zeros((streams * per - filled, 16, LANES), BF)

    exchange = pltpu.make_async_remote_copy(
        src_ref=pack.at[1 - me],
        dst_ref=got,
        send_sem=wa_sem.at[0],
        recv_sem=wa_sem.at[1],
        device_id={"wa": 1 - me},
        device_id_type=MESH,
    )
    exchange.start()
    exchange.wait()

    chunk = 8

    def add_into(dst, dst_at, src, src_at, count):
        def body(i, _):
            total = dst[pl.ds(dst_at + i * chunk, chunk)].astype(F32) + src[pl.ds(src_at + i * chunk, chunk)].astype(F32)
            dst[pl.ds(dst_at + i * chunk, chunk)] = total.astype(BF)
            return 0

        whole_chunks = count // chunk
        if whole_chunks:
            lax.fori_loop(0, whole_chunks, body, 0)
        for i in range(whole_chunks * chunk, count):
            total = dst[pl.ds(dst_at + i, 1)].astype(F32) + src[pl.ds(src_at + i, 1)].astype(F32)
            dst[pl.ds(dst_at + i, 1)] = total.astype(BF)

    mine = pack.at[me]
    add_into(mine, 0, got, 0, streams * per)

    orders = [[(s + k) % len(bits) for k in range(len(bits))] for s in range(streams)]
    offsets = [s * per for s in range(streams)]
    sizes = [per] * streams
    landing = [s * per for s in range(streams)]
    trail = []
    for k in range(len(bits)):
        flights = []
        for s in range(streams):
            which = orders[s][k]
            partner = partners[which]
            size = sizes[s] // 2
            high = lax.rem(lax.div(seq, bits[which]), 2)
            keep = offsets[s] + high * size
            give = offsets[s] + (1 - high) * size
            copy = pltpu.make_async_remote_copy(
                src_ref=mine.at[pl.ds(give, size)],
                dst_ref=rs_got.at[pl.ds(landing[s], size)],
                send_sem=rs_send.at[k, s],
                recv_sem=rs_recv.at[k, s],
                device_id={"seq": partner},
                device_id_type=MESH,
            )
            copy.start()
            flights.append((copy, keep, size, landing[s]))
            landing[s] += size
            offsets[s], sizes[s] = keep, size
        trail.append([(orders[s][k], offsets[s], sizes[s]) for s in range(streams)])
        for copy, keep, size, land in flights:
            copy.wait()
            add_into(mine, keep, rs_got, land, size)
    for s in range(streams):
        size = sizes[s]

        def keep_own(i, _, s=s):
            out[pl.ds(offsets[s] + i, 1)] = mine[pl.ds(offsets[s] + i, 1)]
            return 0

        lax.fori_loop(0, size, keep_own, 0)
    for k in reversed(range(len(bits))):
        flights = []
        for s in range(streams):
            which, at, size = trail[k][s]
            copy = pltpu.make_async_remote_copy(
                src_ref=out.at[pl.ds(at, size)],
                dst_ref=out.at[pl.ds(at, size)],
                send_sem=ag_send.at[k, s],
                recv_sem=ag_recv.at[k, s],
                device_id={"seq": partners[which]},
                device_id_type=MESH,
            )
            copy.start()
            flights.append(copy)
        for copy in flights:
            copy.wait()


def unpack_kernel(plan, packed, *outs):
    d, inner = plan
    half = inner // 2
    starts, _ = section_blocks(d, inner)
    rows_of = 13
    me = lax.axis_index("wa")

    def block(at):
        return packed[at * rows_of : (at + 1) * rows_of].reshape(rows_of * 16, LANES).astype(F32)

    def matrix(name, used):
        parts = [block(starts[name] + b) for b in range(-(-used // LANES))]
        return jnp.concatenate(parts, axis=1)

    def my_half(line, size):
        return jnp.where(me == 0, line[:, 0:size], line[:, size : 2 * size])

    vec = block(starts["vec"])[0:half]
    turned = vec.T

    def write(ref, pieces):
        ref[...] = jnp.concatenate(pieces, axis=1).reshape(ref.shape)

    for side, taps in enumerate((ENCODER_TAPS, DECODER_TAPS)):
        tag = "ed"[side]
        first_g, first_b, red_w, red_b, mid_g, mid_b, ker, ker_b, last_g, last_b, exp_w, exp_b = outs[12 * side : 12 * side + 12]
        at = 8 * side
        write(first_g, [turned[at : at + 1], turned[at + 1 : at + 2]])
        write(first_b, [turned[at + 2 : at + 3], turned[at + 3 : at + 4]])
        write(mid_g, [turned[at + 4 : at + 5]])
        write(mid_b, [turned[at + 5 : at + 6]])
        write(last_g, [turned[at + 6 : at + 7]])
        write(last_b, [turned[at + 7 : at + 8]])
        value = matrix(tag + "_we", d)
        exp_w[...] = value[0:half, 0:d]
        write(exp_b, [my_half(value[half : half + 1, 0:d], d // 2)])
        value = matrix(tag + "_k", taps * inner)
        for j in range(taps):
            ker[j] = value[0:half, j * inner : (j + 1) * inner]
        centre = (ENCODER_SHIFTS if side == 0 else DECODER_SHIFTS).index(0)
        write(ker_b, [my_half(value[half : half + 1, centre * inner : (centre + 1) * inner], half)])
        value = matrix(tag + "_wr", d + AUG)[0:half]
        red_w[...] = value[:, 0:d]
        write(red_b, [value[:, d:].T[0:1]])


def reduce_gradients(mats, vecs, d, inner, n, half_shapes):
    _, blocks = section_blocks(d, inner)
    streams = 3
    total = blocks * 13
    per = -(-total // (streams * n)) * n
    steps = max(1, n.bit_length() - 1)
    vm = pl.BlockSpec(memory_space=pltpu.VMEM)
    count = streams * per
    sem = pltpu.SemaphoreType.DMA
    packed = pl.pallas_call(
        functools.partial(reduce_kernel, (d, inner, n, streams, per)),
        out_shape=jax.ShapeDtypeStruct((count, 16, LANES), BF),
        in_specs=[vm] * 18,
        out_specs=vm,
        scratch_shapes=[
            pltpu.VMEM((2, count, 16, LANES), BF),
            pltpu.VMEM((count, 16, LANES), BF),
            pltpu.VMEM((count, 16, LANES), BF),
            sem((2,)),
            sem((steps, streams)),
            sem((steps, streams)),
            sem((steps, streams)),
            sem((steps, streams)),
        ],
        compiler_params=params(5),
        name="reduce_gradients",
    )(*mats, *vecs)
    return pl.pallas_call(
        functools.partial(unpack_kernel, (d, inner)),
        out_shape=[jax.ShapeDtypeStruct(s, F32) for s in half_shapes],
        in_specs=[vm],
        out_specs=[vm] * 24,
        compiler_params=params(),
        name="unpack_gradients",
    )(packed)


def local(n, stream, doc_start, doc_end, cotangent, *weights):
    rows, d = stream.shape[1], stream.shape[2]
    inner = weights[6].shape[1] * 2
    steps = rows // TILE
    x, cot = stream[0].T, cotangent[0].T
    starts, ends = doc_start, doc_end
    weights = [w.T if at % 12 == 2 else w for at, w in enumerate(weights)]
    enc, dec = gather_weights(weights, d, inner)
    wrt_e, kt_e, wet_e, we_e, kb_e, wr_e, g1_e, b1_e, g2_e, b2_e, g3_e, b3_e = enc
    wrt_d, kt_d, wet_d, we_d, kb_d, wr_d, g1_d, b1_d, g2_d, b2_d, g3_d, b3_d = dec

    def tile(i):
        return (i + steps - 1) % steps

    def cols(channels):
        return pl.BlockSpec((channels, TILE), lambda i: (0, tile(i)))

    per = TILE // LANES

    def block_before(channels):
        return pl.BlockSpec((channels, LANES), lambda i: (0, (per * tile(i) + per * steps - 1) % (per * steps)))

    def block_after(channels):
        return pl.BlockSpec((channels, LANES), lambda i: (0, (per * tile(i) + per) % (per * steps)))

    def spec(a):
        return whole(a.shape)

    def wide(channels, dtype=BF):
        return jax.ShapeDtypeStruct((channels, rows), dtype)

    def fixed(shape, dtype=F32):
        return jax.ShapeDtypeStruct(shape, dtype)

    d1, i1 = d + AUG, inner + AUG
    norm_wide = [(d1, BF), (d, BF), (d, BF), (8, F32)]
    norm_in = [(i1, BF), (inner, BF), (inner, BF), (8, F32)]

    def outs_of(items):
        return [wide(c, t) for c, t in items], [cols(c) for c, _ in items]

    shapes, specs = outs_of(norm_wide + norm_in)
    edge = fixed((inner, LANES), BF)
    ins = [wrt_e, g1_e, b1_e, g2_e, b2_e]
    h1e, z1e, d1e, r1e, h2e, z2e, d2e, r2e, el, er = pl.pallas_call(
        functools.partial(enc_in_kernel, steps),
        grid=(steps,),
        out_shape=shapes + [edge, edge],
        in_specs=[cols(d)] + [spec(a) for a in ins],
        out_specs=specs + [whole(edge.shape)] * 2,
        scratch_shapes=[
            pltpu.VMEM((d, TILE), F32),
            pltpu.VMEM((inner, TILE), F32),
        ]
        + edge_scratch("both", inner),
        compiler_params=params(1),
        name="encoder_in",
    )(x, *ins)

    shapes, specs = outs_of(norm_in + [(d, BF)] + norm_wide + norm_in)
    ins = [kt_e, wet_e, wrt_d, g3_e, b3_e, g1_d, b1_d, g2_d, b2_d]
    h3e, z3e, d3e, r3e, x1, h1d, z1d, d1d, r1d, h2d, z2d, d2d, r2d, eld = pl.pallas_call(
        functools.partial(enc_out_kernel, steps),
        grid=(steps,),
        out_shape=shapes + [edge],
        in_specs=[cols(1), cols(1), block_before(i1), cols(i1), block_after(i1), spec(el), spec(er), cols(d)]
        + [spec(a) for a in ins],
        out_specs=specs + [whole(edge.shape)],
        scratch_shapes=[
            pltpu.VMEM((ENCODER_TAPS * inner + AUG, TILE), BF),
            pltpu.VMEM((inner, LANES), BF),
            pltpu.VMEM((inner, LANES), BF),
            pltpu.VMEM((inner, TILE), F32),
            pltpu.VMEM((d, TILE), F32),
            pltpu.VMEM((inner, TILE), F32),
        ]
        + edge_scratch("right", inner),
        compiler_params=params(2),
        name="encoder_out",
    )(starts, ends, h2e, h2e, h2e, el, er, x, *ins)

    shapes, specs = outs_of([(i1, BF), (inner, BF)])
    sums = [fixed((i1, d)), fixed((inner, LANES)), fixed((inner, LANES))]
    ins = [kt_d, we_d, g3_d, b3_d]
    h3d, evr_d, erd, dwe_d, dg3_d, db3_d = pl.pallas_call(
        functools.partial(dec_out_kernel, steps),
        grid=(steps,),
        out_shape=shapes + [edge] + sums,
        in_specs=[cols(1), cols(1), block_before(i1), cols(i1), spec(eld), cols(d)] + [spec(a) for a in ins],
        out_specs=specs + [whole(edge.shape)] + [whole(s.shape) for s in sums],
        scratch_shapes=[
            pltpu.VMEM((DECODER_TAPS * inner + AUG, TILE), BF),
            pltpu.VMEM((inner, LANES), BF),
            pltpu.VMEM((inner, TILE), F32),
            pltpu.VMEM((inner, TILE), BF),
            pltpu.VMEM((inner, TILE), BF),
            pltpu.VMEM((8, TILE), F32),
            pltpu.VMEM((inner, TILE), F32),
        ]
        + edge_scratch("left", inner),
        compiler_params=params(3),
        name="decoder_out",
    )(starts, ends, h2d, h2d, eld, cot, *ins)

    shapes, specs = outs_of([(d, BF), (inner, BF)])
    small, large = fixed((inner, LANES)), fixed((d, LANES))
    sums = [fixed((i1, DECODER_TAPS * inner)), fixed((inner, d1)), fixed((i1, d))]
    sums += [small, small, large, large, small, small]
    ins = [kb_d, wr_d, we_e, g2_d, g1_d, g3_e]
    stash = [h2d, z2d, d2d, r2d, h1d, z1d, d1d, r1d, cot, h3e, z3e, d3e, r3e]
    ey, evr_e, el2, er2, dk_d, dwr_d, dwe_e, dg2_d, db2_d, dg1_d, db1_d, dg3_e, db3_e = pl.pallas_call(
        functools.partial(dec_back_kernel, steps),
        grid=(steps,),
        out_shape=shapes + [edge, edge] + sums,
        in_specs=[cols(1), cols(1), cols(inner), block_after(inner), spec(erd)]
        + [spec(a) for a in ins]
        + [cols(a.shape[0]) for a in stash],
        out_specs=specs + [whole(edge.shape)] * 2 + [whole(s.shape) for s in sums],
        scratch_shapes=[
            pltpu.VMEM((DECODER_TAPS * inner, TILE), BF),
            pltpu.VMEM((inner, LANES), BF),
            pltpu.VMEM((inner, TILE), F32),
            pltpu.VMEM((d, TILE), F32),
            pltpu.VMEM((inner, TILE), BF),
        ]
        + edge_scratch("both", inner),
        compiler_params=params(4),
        name="decoder_back",
    )(starts, ends, evr_d, evr_d, erd, *ins, *stash)

    sums = [fixed((i1, ENCODER_TAPS * inner)), fixed((inner, d1)), small, small, large, large]
    ins = [kb_e, wr_e, wet_d, g2_e, g1_e]
    stash = [h2e, z2e, d2e, r2e, h1e, z1e, d1e, r1e, ey, x1, h3d]
    full = wide(d, F32)
    out, grad, dk_e, dwr_e, dg2_e, db2_e, dg1_e, db1_e = pl.pallas_call(
        functools.partial(enc_back_kernel, steps),
        grid=(steps,),
        out_shape=[full, full] + sums,
        in_specs=[cols(1), cols(1), block_before(inner), cols(inner), block_after(inner), spec(el2), spec(er2)]
        + [spec(a) for a in ins]
        + [cols(a.shape[0]) for a in stash],
        out_specs=[cols(d), cols(d)] + [whole(s.shape) for s in sums],
        scratch_shapes=[
            pltpu.VMEM((ENCODER_TAPS * inner, TILE), BF),
            pltpu.VMEM((inner, LANES), BF),
            pltpu.VMEM((inner, LANES), BF),
            pltpu.VMEM((inner, TILE), F32),
            pltpu.VMEM((d, TILE), F32),
            pltpu.VMEM((inner, TILE), BF),
        ],
        compiler_params=params(),
        name="encoder_back",
    )(starts, ends, evr_e, evr_e, evr_e, el2, er2, *ins, *stash)

    mats = [dwe_e, dk_e, dwr_e, dwe_d, dk_d, dwr_d]
    vecs = [dg1_e, db1_e, dg2_e, db2_e, dg3_e, db3_e, dg1_d, db1_d, dg2_d, db2_d, dg3_d, db3_d]
    shares = reduce_gradients(mats, vecs, d, inner, n, [w.shape for w in weights])
    shares = [w.T if at % 12 == 2 else w for at, w in enumerate(shares)]
    return (out.T[None], grad.T[None], *shares)


def solution(mesh):
    rows = P("wa", "seq", None)
    block = (
        P("wa"), P("wa"), P(None, "wa"), P("wa"), P("wa"), P("wa"),
        P(None, "wa", None), P("wa"), P("wa"), P("wa"), P("wa", None), P("wa"),
    )
    return jax.shard_map(
        functools.partial(local, mesh.shape["seq"]),
        mesh=mesh,
        in_specs=(rows, P("wa", "seq"), P("wa", "seq"), rows, *block, *block),
        out_specs=(rows, rows, *block, *block),
        check_vma=False,
    )
```

```python
import functools

import jax
import jax.numpy as jnp
from jax import lax
from jax.experimental import pallas as pl
from jax.experimental.pallas import tpu as pltpu
from jax.sharding import PartitionSpec as P

ENCODER_TAPS = 5
ENCODER_DILATION = 8
DECODER_TAPS = 3
DECODER_DILATION = 16
EPS = 1e-05

MESH = pl.DeviceIdType.MESH
BF = jnp.bfloat16
F32 = jnp.float32
LANES = 128
TILE = 512
HALF = 256
AUG = 16
VMEM_LIMIT = 56 * 1024 * 1024
GELU_1 = 2.0 * 0.7978845608028654
GELU_3 = 8.0 * 0.7978845608028654 * 0.044715

ENCODER_SHIFTS = tuple(ENCODER_DILATION * (j - ENCODER_TAPS // 2) for j in range(ENCODER_TAPS))
DECODER_SHIFTS = tuple(-DECODER_DILATION * (DECODER_TAPS - 1 - j) for j in range(DECODER_TAPS))


def params(collective=None):
    if collective is None:
        return pltpu.CompilerParams(vmem_limit_bytes=VMEM_LIMIT)
    return pltpu.CompilerParams(
        vmem_limit_bytes=VMEM_LIMIT, collective_id=collective, has_side_effects=True
    )


def whole(shape):
    return pl.BlockSpec(shape, lambda *_: (0,) * len(shape))


def nt_dot(left, right):
    return lax.dot_general(left, right, (((1,), (1,)), ((), ())), preferred_element_type=F32)


def nn_dot(left, right):
    return jnp.dot(left, right, preferred_element_type=F32)


def lanes_of(column, width):
    return jnp.concatenate([column] * (width // LANES), axis=1)


def fold(value):
    total = value[:, :LANES]
    for at in range(LANES, value.shape[1], LANES):
        total = total + value[:, at : at + LANES]
    return total


def weights_kernel(dims, *refs):
    d, inner, taps = dims
    n_in = 24
    ins, refs = refs[:n_in], refs[n_in:]
    outs, refs = refs[:30], refs[30:]
    (small_own, small_got, k_own0, k_own1, e_own0, e_own1, r_own0, r_own1, *rest) = refs
    (r_got0, r_got1, k_got0, k_got1, e_got0, e_got1, send, recv) = rest
    me = lax.axis_index("wa")
    other = 1 - me
    barrier = pltpu.get_barrier_semaphore()
    pl.semaphore_signal(barrier, inc=1, device_id={"wa": other}, device_id_type=MESH)
    pl.semaphore_wait(barrier, 1)

    half = inner // 2
    pad = k_own0.shape[1]
    small_own[...] = jnp.zeros_like(small_own)
    small_at = []
    for side in range(2):
        for at in (0, 1, 3, 4, 5, 7, 8, 9, 11):
            small_at.append(12 * side + at)
    for row, at in enumerate(small_at):
        n = ins[at].shape[0]
        small_own[row : row + 1, 0:n] = ins[at][...].astype(F32).reshape(1, n)
    owns, gots = [], []
    for side, (k_own, e_own, r_own) in enumerate(((k_own0, e_own0, r_own0), (k_own1, e_own1, r_own1))):
        base = 12 * side
        k_own[:, half - 8 : pad, :] = jnp.zeros((taps[side], pad - half + 8, inner), BF)
        k_own[:, 0:half, :] = ins[base + 6][...]
        e_own[half - 8 : pad, :] = jnp.zeros((pad - half + 8, d), BF)
        e_own[0:half, :] = ins[base + 10][...]
        r_own[half - 8 : pad, :] = jnp.zeros((pad - half + 8, d), BF)
        r_own[0:half, :] = ins[base + 2][...]
        owns += [r_own, k_own, e_own]
    owns.append(small_own)
    gots = [r_got0, k_got0, e_got0, r_got1, k_got1, e_got1, small_got]
    copies = []
    for at, (own, got) in enumerate(zip(owns, gots)):
        copies.append(
            pltpu.make_async_remote_copy(
                src_ref=own,
                dst_ref=got,
                send_sem=send.at[at],
                recv_sem=recv.at[at],
                device_id={"wa": other},
                device_id_type=MESH,
            )
        )
        copies[-1].start()
    for copy in copies:
        copy.wait()

    first_core = me == 0

    def ordered(own, got):
        own, got = own.astype(F32), got.astype(F32)
        return jnp.where(first_core, own, got), jnp.where(first_core, got, own)

    small0, small1 = ordered(small_own[...], small_got[...])

    def column(row, n):
        line = jnp.concatenate([small0[row : row + 1, 0 : n // 2], small1[row : row + 1, 0 : n // 2]], axis=1)
        return jnp.broadcast_to(line, (LANES, n)).T

    def bias_columns(value):
        where = lax.broadcasted_iota(jnp.int32, (value.shape[0], AUG), 1) == 0
        return jnp.where(where, value[:, :AUG], 0.0).astype(BF)

    for side in range(2):
        o = outs[15 * side : 15 * side + 15]
        wrt, kt, wet, we, kb, wr, *vectors = o
        base = 9 * side
        for at, (row, n) in enumerate(((0, d), (3, inner), (6, inner))):
            gain, half_gain, half_bias = vectors[3 * at : 3 * at + 3]
            gain[...] = column(base + row, n)
            half_gain[...] = gain[...] * 0.5
            half_bias[...] = column(base + row + 1, n) * 0.5
        n = taps[side]
        r0, r1 = ordered(owns[3 * side][0:half, :], gots[3 * side][0:half, :])
        r = jnp.concatenate([r0, r1], axis=0)
        wr[...] = r.T.astype(BF)
        wrt[:, 0:d] = r.astype(BF)
        wrt[:, d : d + AUG] = bias_columns(column(base + 2, inner))
        e0, e1 = ordered(owns[3 * side + 2][0:half, :], gots[3 * side + 2][0:half, :])
        e = jnp.concatenate([e0, e1], axis=0)
        we[...] = e.astype(BF)
        wet[:, 0:inner] = e.T.astype(BF)
        wet[:, inner : inner + AUG] = bias_columns(column(base + 8, d))
        for j in range(n):
            k0, k1 = ordered(owns[3 * side + 1][j, 0:half, :], gots[3 * side + 1][j, 0:half, :])
            k = jnp.concatenate([k0, k1], axis=0)
            kb[:, j * inner : (j + 1) * inner] = k.astype(BF)
            kt[:, j * inner : (j + 1) * inner] = k.T.astype(BF)
        kt[:, n * inner : n * inner + AUG] = bias_columns(column(base + 5, inner))


def gather_weights(args, d, inner):
    taps = (ENCODER_TAPS, DECODER_TAPS)
    half = inner // 2
    pad = -(-half // 16) * 16
    shapes = []
    for n in taps:
        shapes += [
            ((inner, d + AUG), BF),
            ((inner, n * inner + AUG), BF),
            ((d, inner + AUG), BF),
            ((inner, d), BF),
            ((inner, n * inner), BF),
            ((d, inner), BF),
        ]
        for c in (d, inner, inner):
            shapes += [((c, LANES), F32)] * 3
    vm = pl.BlockSpec(memory_space=pltpu.VMEM)
    small = pltpu.VMEM((24, 512), F32)
    kk = [pltpu.VMEM((n, pad, inner), BF) for n in taps]
    ee = [pltpu.VMEM((pad, d), BF)] * 2
    outs = pl.pallas_call(
        functools.partial(weights_kernel, (d, inner, taps)),
        out_shape=[jax.ShapeDtypeStruct(*s) for s in shapes],
        in_specs=[vm] * 24,
        out_specs=[vm] * 30,
        scratch_shapes=[small, small, *kk, *ee, *ee, *ee, *kk, *ee]
        + [pltpu.SemaphoreType.DMA((7,)), pltpu.SemaphoreType.DMA((7,))],
        compiler_params=params(0),
        name="gather_weights",
    )(*args)
    return outs[:15], outs[15:]


def pacing(thunks, slots):
    state = [0, 0]
    thunks = list(thunks)

    def between():
        while state[1] < len(thunks) and state[0] * len(thunks) >= state[1] * slots:
            thunks[state[1]]()
            state[1] += 1
        state[0] += 1

    return between


def add_product(total, left, right):
    def piece(at, stop):
        total[:, at:stop] += nt_dot(left[...], right[at:stop, :])

    columns = right.shape[0]
    return [functools.partial(piece, at, min(at + HALF, columns)) for at in range(0, columns, HALF)]


def norm_forward(src, lanes, channels, gain, bias, h_out, z_out, d_out, r_out, keep=None, fill=()):
    width = lanes.stop - lanes.start
    between = pacing(fill, 3 * (channels // 16))
    total = [jnp.zeros((8, width), F32) for _ in range(4)]
    for c in range(0, channels, 16):
        between()
        x = src[c : c + 16, lanes].astype(F32)
        if keep is not None:
            keep[c : c + 16, lanes] = x
        at = (c // 8) % 4
        total[at] = total[at] + x[0:8]
        total[at + 1] = total[at + 1] + x[8:16]
    mean = jnp.sum((total[0] + total[1]) + (total[2] + total[3]), axis=0, keepdims=True) * (1.0 / channels)
    wide = jnp.broadcast_to(mean, (16, width))
    values = src if keep is None else keep
    total = [jnp.zeros((8, width), F32) for _ in range(4)]
    for c in range(0, channels, 16):
        between()
        centre = values[c : c + 16, lanes] - wide
        square = centre * centre
        at = (c // 8) % 4
        total[at] = total[at] + square[0:8]
        total[at + 1] = total[at + 1] + square[8:16]
    spread = jnp.sum((total[0] + total[1]) + (total[2] + total[3]), axis=0, keepdims=True) * (1.0 / channels)
    r = lax.rsqrt(spread + EPS)
    if r_out is not None:
        r_out[:, lanes] = jnp.broadcast_to(r, (8, width))
    rw = jnp.broadcast_to(r, (16, width))
    mw = jnp.broadcast_to(mean * r, (16, width))
    one, point = BF(1.0), BF(0.5)
    for c in range(0, channels, 16):
        between()
        rows = slice(c, c + 16)
        z = values[rows, lanes] * rw - mw
        half = (z * lanes_of(gain[rows, :], width) + lanes_of(bias[rows, :], width)).astype(BF)
        sq = half * half
        t = jnp.tanh(half * (sq * BF(GELU_3) + BF(GELU_1)))
        up = one + t
        h_out[rows, lanes] = half * up
        d_out[rows, lanes] = up * (point + half * (sq * BF(1.5 * GELU_3) + BF(0.5 * GELU_1)) * (one - t))
        z_out[rows, lanes] = z.astype(BF)


def norm_backward(grad, lanes, channels, gain, z_in, d_in, r_in, gain_sum, bias_sum, keep, emit, fill=()):
    width = lanes.stop - lanes.start
    between = pacing(fill, 2 * (channels // 16))
    one = [jnp.zeros((8, width), F32) for _ in range(2)]
    two = [jnp.zeros((8, width), F32) for _ in range(2)]
    r = r_in[0:1, lanes]
    rw = jnp.broadcast_to(r, (16, width))
    for c in range(0, channels, 16):
        between()
        rows = slice(c, c + 16)
        da = grad[rows, lanes] * d_in[rows, lanes].astype(F32)
        p = da * z_in[rows, lanes].astype(F32)
        bias_sum[rows, :] += fold(da)
        gain_sum[rows, :] += fold(p)
        wide = lanes_of(gain[rows, :], width)
        dz = da * wide
        q = p * wide
        keep[rows, lanes] = (dz * rw).astype(BF)
        for at in range(2):
            one[at] = one[at] + dz[8 * at : 8 * at + 8]
            two[at] = two[at] + q[8 * at : 8 * at + 8]
    scale = r * (1.0 / channels)
    m1 = jnp.broadcast_to(jnp.sum(one[0] + one[1], axis=0, keepdims=True) * scale, (16, width)).astype(BF)
    m2 = jnp.broadcast_to(jnp.sum(two[0] + two[1], axis=0, keepdims=True) * scale, (16, width)).astype(BF)
    for c in range(0, channels, 16):
        between()
        rows = slice(c, c + 16)
        emit(rows, keep[rows, lanes] - (z_in[rows, lanes] * m2 + m1))


def tap_mask(starts, ends, first, shift):
    place = first + shift + lax.broadcasted_iota(jnp.int32, (8, TILE), 1)
    usable = (place >= jnp.broadcast_to(starts[...], (8, TILE))) & (place < jnp.broadcast_to(ends[...], (8, TILE)))
    one = jnp.where(usable, 1.0, 0.0)
    return jnp.concatenate([one, one], axis=0).astype(BF)


def stack_taps(stack, shifts, before, main, after, starts, ends, first, inner):
    for j, shift in enumerate(shifts):
        if not shift:
            stack[j * inner : (j + 1) * inner, :] = main[0:inner, :]
            continue
        mask = tap_mask(starts, ends, first, shift)
        for c in range(0, inner, 16):
            rows = slice(c, c + 16)
            if shift < 0:
                span = jnp.concatenate([before[rows, :], main[rows, :]], axis=1)
                span = pltpu.roll(span, -shift, 1)[:, LANES:]
            else:
                span = jnp.concatenate([main[rows, :], after[rows, :]], axis=1)
                span = pltpu.roll(span, TILE + LANES - shift, 1)[:, :TILE]
            stack[j * inner + c : j * inner + c + 16, :] = span * mask


def ones_rows(width):
    where = lax.broadcasted_iota(jnp.int32, (AUG, width), 0) == 0
    return jnp.where(where, 1.0, 0.0).astype(BF)


def neighbours():
    me = lax.axis_index("seq")
    n = lax.axis_size("seq")
    return lax.rem(me + n - 1, n), lax.rem(me + 1, n)


def greet(others):
    barrier = pltpu.get_barrier_semaphore()
    for device in others:
        pl.semaphore_signal(barrier, inc=1, device_id=device, device_id_type=MESH)
    pl.semaphore_wait(barrier, len(others))


def send_copy(src, dst, send_sem, recv_sem, device):
    return pltpu.make_async_remote_copy(
        src_ref=src, dst_ref=dst, send_sem=send_sem, recv_sem=recv_sem, device_id=device, device_id_type=MESH
    )


def later_tile(step, steps):
    return lax.rem(step + 1, steps)


def first_place(tile, steps):
    return lax.axis_index("seq") * (steps * TILE) + tile * TILE


CHAINS = (slice(0, HALF), slice(HALF, TILE))


def enc_in_kernel(x, wrt, g1, b1, g2, b2, h1, z1, d1, r1, h2, z2, d2, r2, xt, u):
    d, inner = x.shape[0], wrt.shape[0]
    h1[d : d + AUG, :] = ones_rows(TILE)
    h2[inner : inner + AUG, :] = ones_rows(TILE)
    one, two = CHAINS

    def make_u(lanes):
        u[:, lanes] = nn_dot(wrt[...], h1[:, lanes])

    norm_forward(x, one, d, g1, b1, h1, z1, d1, r1, xt)
    norm_forward(x, two, d, g1, b1, h1, z1, d1, r1, xt, [lambda: make_u(one)])
    norm_forward(u, one, inner, g2, b2, h2, z2, d2, r2, None, [lambda: make_u(two)])
    norm_forward(u, two, inner, g2, b2, h2, z2, d2, r2)


def choose_edge(window, block, edge, at_end):
    window[...] = block[0 : window.shape[0], :]

    @pl.when(at_end)
    def _():
        window[...] = edge[0 : window.shape[0], :]


def trade_edges(step, steps, head, tail, got_l, got_r, send, recv, others=()):
    left, right = neighbours()
    to_left = send_copy(head, got_r, send.at[0], recv.at[0], {"seq": left})
    to_right = send_copy(tail, got_l, send.at[1], recv.at[1], {"seq": right})

    @pl.when(step == 0)
    def _():
        greet([{"seq": left}, {"seq": right}, *others])
        to_left.start()
        to_right.start()

    @pl.when(step == steps - 2)
    def _():
        to_left.wait()
        to_right.wait()


def enc_out_kernel(
    steps, starts, ends, before, main, after, head, tail, xt, kt, wet, wrt, g3, b3, g1, b1, g2, b2,
    h3, z3, d3, r3, x1, h1, z1, d1, r1, h2, z2, d2, r2, edge_o,
    stack, win_b, win_a, v, y, u, got_l, got_r, own, got, send, recv,
):
    step = pl.program_id(0)
    d, inner = xt.shape[0], v.shape[0]
    trade_edges(step, steps, head, tail, got_l, got_r, send, recv)
    choose_edge(win_b, before, got_l, step == steps - 1)
    choose_edge(win_a, after, got_r, step == steps - 2)
    stack_taps(stack, ENCODER_SHIFTS, win_b, main, win_a, starts, ends, first_place(later_tile(step, steps), steps), inner)
    stack[len(ENCODER_SHIFTS) * inner :, :] = ones_rows(TILE)
    h3[inner : inner + AUG, :] = ones_rows(TILE)
    h1[d : d + AUG, :] = ones_rows(TILE)
    h2[inner : inner + AUG, :] = ones_rows(TILE)
    one, two = CHAINS

    def make_v(lanes):
        v[:, lanes] = nn_dot(kt[...], stack[:, lanes])

    def make_y(lanes):
        y[:, lanes] = nn_dot(wet[...], h3[:, lanes]) + xt[:, lanes].astype(F32)

    def make_u(lanes):
        u[:, lanes] = nn_dot(wrt[...], h1[:, lanes])

    def norm_last(lanes, fill):
        norm_forward(v, lanes, inner, g3, b3, h3, z3, d3, r3, None, fill)

    def norm_first(lanes, fill):
        for c in range(0, d, 16):
            x1[c : c + 16, lanes] = y[c : c + 16, lanes].astype(BF)
        norm_forward(y, lanes, d, g1, b1, h1, z1, d1, r1, None, fill)

    make_v(one)
    norm_last(one, [lambda: make_v(two)])
    norm_last(two, [lambda: make_y(one)])
    norm_first(one, [lambda: make_y(two)])
    norm_first(two, [lambda: make_u(one)])
    norm_forward(u, one, inner, g2, b2, h2, z2, d2, r2, None, [lambda: make_u(two)])
    norm_forward(u, two, inner, g2, b2, h2, z2, d2, r2)

    def give():
        return send_copy(own, got, send.at[2], recv.at[2], {"seq": neighbours()[1]})

    @pl.when(step == steps - 2)
    def _():
        own[...] = h2[:, TILE - LANES : TILE]
        give().start()

    @pl.when(step == steps - 1)
    def _():
        give().wait()
        edge_o[...] = got[...]


def dec_out_kernel(
    steps, starts, ends, before, main, e_l, cot_t, x1, kt, we, wet, f3, b3, g3,
    out, evr, dwe, dg3, db3,
    stack, win_b, v, h3, z3, d3, r3, g, kept,
):
    step = pl.program_id(0)
    inner = v.shape[0]

    @pl.when(step == 0)
    def _():
        dwe[...] = jnp.zeros_like(dwe)
        dg3[...] = jnp.zeros_like(dg3)
        db3[...] = jnp.zeros_like(db3)

    choose_edge(win_b, before, e_l, step == 0)
    stack_taps(stack, DECODER_SHIFTS, win_b, main, None, starts, ends, first_place(step, steps), inner)
    stack[len(DECODER_SHIFTS) * inner :, :] = ones_rows(TILE)
    h3[inner : inner + AUG, :] = ones_rows(TILE)
    one, two = CHAINS

    def make_v(lanes):
        v[:, lanes] = nn_dot(kt[...], stack[:, lanes])

    def make_g(lanes):
        g[:, lanes] = nn_dot(we[...], cot_t[:, lanes])

    def back(lanes, fill):
        def emit(rows, value):
            evr[rows, lanes] = value

        norm_backward(g, lanes, inner, g3, z3, d3, r3, dg3, db3, kept, emit, fill)

    def make_out(lanes):
        out[:, lanes] = nn_dot(wet[...], h3[:, lanes]) + x1[:, lanes].astype(F32)

    make_g(one)
    make_g(two)
    make_v(one)
    norm_forward(v, one, inner, f3, b3, h3, z3, d3, r3, None, [lambda: make_v(two)])
    norm_forward(v, two, inner, f3, b3, h3, z3, d3, r3)
    products = add_product(dwe, h3, cot_t)
    back(one, [lambda: make_out(one), *products[:2]])
    back(two, [lambda: make_out(two), *products[2:]])


def dec_back_kernel(
    plan, starts, ends, main, after, head, kb, wr, we, g2, g1, g3,
    h2, z2, d2, r2, h1, z1, d1, r1, cot_t, h3, z3, d3, r3, dwe_d,
    ey, evr, packed, dg2, db2, dg1, db1, dg3, db3,
    dk, dwrt, dwe, stack, win_a, g, big, eur, kept, got, send, recv,
):
    steps = plan.steps
    step = pl.program_id(0)
    d, inner = cot_t.shape[0], g.shape[0]

    @pl.when(step == 0)
    def _():
        for ref in (dk, dwrt, dwe, dg2, db2, dg1, db1, dg3, db3):
            ref[...] = jnp.zeros_like(ref)

    left, right = neighbours()
    to_left = send_copy(head, got, send.at[0], recv.at[0], {"seq": left})

    @pl.when(step == 0)
    def _():
        greet([{"seq": left}, {"seq": right}])
        to_left.start()

    @pl.when(step == steps - 1)
    def _():
        to_left.wait()

    choose_edge(win_a, after, got, step == steps - 1)
    back = tuple(-s for s in DECODER_SHIFTS)
    stack_taps(stack, back, None, main, win_a, starts, ends, first_place(step, steps), inner)
    one, two = CHAINS

    def make_g2(lanes):
        g[:, lanes] = nn_dot(kb[...], stack[:, lanes])

    def make_g1(lanes):
        big[:, lanes] = nn_dot(wr[...], eur[:, lanes])

    def make_g3(lanes):
        g[:, lanes] = nn_dot(we[...], ey[:, lanes])

    def back2(lanes, fill):
        def emit(rows, value):
            eur[rows, lanes] = value

        norm_backward(g, lanes, inner, g2, z2, d2, r2, dg2, db2, kept, emit, fill)

    def back1(lanes, fill):
        def emit(rows, value):
            ey[rows, lanes] = value + cot_t[rows, lanes]

        norm_backward(big, lanes, d, g1, z1, d1, r1, dg1, db1, kept, emit, fill)

    def back3(lanes, fill):
        def emit(rows, value):
            evr[rows, lanes] = value

        norm_backward(g, lanes, inner, g3, z3, d3, r3, dg3, db3, kept, emit, fill)

    make_g2(one)
    by_k = add_product(dk, h2, stack)
    back2(one, [lambda: make_g2(two)])
    back2(two, [lambda: make_g1(one)])
    by_r = add_product(dwrt, eur, h1)
    back1(one, [lambda: make_g1(two), *by_k[:3]])
    back1(two, [lambda: make_g3(one), *by_k[3:], *by_r[:2]])
    make_g3(two)
    by_e = add_product(dwe, h3, ey)
    back3(one, [*by_r[2:], *by_e[:1]])
    back3(two, by_e[1:])

    @pl.when(step == steps - 1)
    def _():
        pack_gradients(packed, plan, ((dwe_d, d), (dk, dk.shape[1]), (dwrt, d + AUG), (dwe, d)), ())


def enc_back_kernel(
    plan, starts, ends, before, main, after, head, tail, kb, wr, g2, g1,
    h2, z2, d2, r2, h1, z1, d1, r1, ey, given, *rest,
):
    vecs, rest = rest[:8], rest[8:]
    (
        grad, packed, summed,
        dk, dwrt, dg2, db2, dg1, db1,
        stack, win_b, win_a, g, big, eur, kept, got_l, got_r, send, recv,
    ), traffic = rest[:20], rest[20:]
    steps = plan.steps
    step = pl.program_id(0)
    d, inner = ey.shape[0], g.shape[0]

    @pl.when(step == 0)
    def _():
        for ref in (dk, dwrt, dg2, db2, dg1, db1):
            ref[...] = jnp.zeros_like(ref)

    sum_over = Summing(plan.early, given, summed, traffic)
    trade_edges(step, steps, head, tail, got_l, got_r, send, recv, sum_over.partners())

    stage_count = sum_over.steps + 2
    due = [0, 2] + [6 + 6 * i // max(1, stage_count - 3) for i in range(stage_count - 2)]

    def hook(at):
        for stage, place in enumerate(due):
            where = (place // 2, place % 2) if place < 2 * steps else (steps - 1, 2)
            if where[1] == at:

                @pl.when(step == where[0])
                def _(stage=stage):
                    sum_over.reduce_stage(stage)

    hook(0)
    choose_edge(win_b, before, got_l, step == steps - 1)
    choose_edge(win_a, after, got_r, step == steps - 2)
    back = tuple(-s for s in ENCODER_SHIFTS)
    stack_taps(stack, back, win_b, main, win_a, starts, ends, first_place(later_tile(step, steps), steps), inner)
    one, two = CHAINS

    def make_g2(lanes):
        g[:, lanes] = nn_dot(kb[...], stack[:, lanes])

    def make_g1(lanes):
        big[:, lanes] = nn_dot(wr[...], eur[:, lanes])

    def back2(lanes, fill):
        def emit(rows, value):
            eur[rows, lanes] = value

        norm_backward(g, lanes, inner, g2, z2, d2, r2, dg2, db2, kept, emit, fill)

    def back1(lanes, fill):
        def emit(rows, value):
            grad[rows, lanes] = value + ey[rows, lanes]

        norm_backward(big, lanes, d, g1, z1, d1, r1, dg1, db1, kept, emit, fill)

    make_g2(one)
    by_k = add_product(dk, h2, stack)
    back2(one, [lambda: make_g2(two)])
    back2(two, [lambda: make_g1(one), *by_k[:1]])
    hook(1)
    by_r = add_product(dwrt, eur, h1)
    back1(one, [lambda: make_g1(two), *by_k[1:5]])
    back1(two, [*by_k[5:], *by_r])

    @pl.when(step == steps - 1)
    def _():
        sums = (dg1, db1, dg2, db2, *vecs)
        pack_gradients(packed, plan, ((dk, dk.shape[1]), (dwrt, d + AUG)), sums)

    hook(2)


ROWS_OF = 13


def blocks_of(used):
    return -(-used // LANES)


class Part:
    def __init__(self, sections, vectors, streams, n):
        self.starts, at = {}, 0
        for name, used in sections:
            self.starts[name] = (at, used)
            at += blocks_of(used)
        if vectors:
            self.starts["vec"] = (at, LANES)
            at += 1
        self.filled = at * ROWS_OF
        self.streams = streams
        self.per = -(-self.filled // (streams * n)) * n
        self.pieces = streams * self.per
        self.n = n
        self.bits = []
        while 1 << len(self.bits) < n:
            self.bits.append(1 << len(self.bits))


class Plan:
    def __init__(self, d, inner, steps, n):
        self.d, self.inner, self.steps, self.n = d, inner, steps, n
        early = (("d_we", d), ("d_k", DECODER_TAPS * inner), ("d_wr", d + AUG), ("e_we", d))
        self.early = Part(early, False, 2, n)
        self.late = Part((("e_k", ENCODER_TAPS * inner), ("e_wr", d + AUG)), True, 4, n)


def pack_gradients(packed, plan, mats, vecs):
    d, inner = plan.d, plan.inner
    half = inner // 2
    for w in range(2):
        at = 0
        for ref, used in mats:
            for b in range(blocks_of(used)):
                stop = min(used, LANES * (b + 1))
                lanes = slice(LANES * b, stop)
                for r in range(ROWS_OF):
                    base = half * w + 16 * r
                    if r < ROWS_OF - 1:
                        value = ref[base : base + 16, lanes]
                    else:
                        value = ref[base : base + 8, lanes]
                        low = ref[inner : inner + 8, lanes] if ref.shape[0] > inner else jnp.zeros_like(value)
                        value = jnp.concatenate([value, low], axis=0)
                    if stop - LANES * b < LANES:
                        blank = jnp.zeros((16, LANES * (b + 1) - stop), F32)
                        value = jnp.concatenate([value, blank], axis=1)
                    packed[w, at] = value.astype(BF)
                    at += 1
        if vecs:
            columns = []
            for ref in vecs:
                total = jnp.sum(ref[...], axis=1, keepdims=True)
                if ref.shape[0] == d:
                    columns.append(total[2 * half * w : 2 * half * w + half])
                    columns.append(total[2 * half * w + half : 2 * half * w + 2 * half])
                else:
                    columns.append(total[half * w : half * (w + 1)])
            lane = lax.broadcasted_iota(jnp.int32, (half, LANES), 1)
            value = jnp.zeros((half, LANES), F32)
            for lane_at, column in enumerate(columns):
                value = jnp.where(lane == lane_at, column, value)
            value = jnp.concatenate([value, jnp.zeros((ROWS_OF * 16 - half, LANES), F32)], axis=0)
            for r in range(ROWS_OF):
                packed[w, at] = value[16 * r : 16 * r + 16].astype(BF)
                at += 1
        left = packed.shape[1] - at
        if left:
            packed[w, at : packed.shape[1]] = jnp.zeros((left, 16, LANES), BF)


def in_chunks(count, body):
    size = max(c for c in range(1, 17) if count % c == 0)

    def step(i, _):
        body(i * size, size)
        return 0

    lax.fori_loop(0, count // size, step, 0)


def copy_pieces(dst, src, at, count):
    dst[pl.ds(at, count)] = src[pl.ds(at, count)]


class Summing:
    def __init__(self, part, given, out, traffic):
        self.part, self.given, self.out = part, given, out
        self.got, self.total, self.leave, self.landed, self.core, self.down, *up = traffic
        self.up = up[0] if up else None
        self.me = lax.axis_index("wa")
        self.seq = lax.axis_index("seq")
        self.steps = len(part.bits)
        self.orders = []
        for s in range(part.streams):
            order = list(range(self.steps))
            if s % 2 and self.steps > 1:
                order[0], order[1] = order[1], order[0]
            self.orders.append(order)

    @staticmethod
    def scratch(part):
        sem = pltpu.SemaphoreType.DMA
        steps = max(1, len(part.bits))
        pieces = (part.pieces, 16, LANES)
        return [
            pltpu.VMEM(pieces, BF),
            pltpu.VMEM(pieces, F32),
            pltpu.VMEM(pieces, BF),
            pltpu.VMEM(pieces, BF),
            sem((2,)),
            sem((2, steps, part.streams)),
        ]

    @staticmethod
    def spread_scratch(part):
        return [pltpu.SemaphoreType.DMA((2, max(1, len(part.bits)), part.streams))]

    def high(self, which):
        return lax.rem(lax.div(self.seq, self.part.bits[which]), 2)

    def partner(self, which):
        bit = self.part.bits[which]
        return {"seq": self.seq + bit - 2 * bit * self.high(which)}

    def partners(self):
        return [{"wa": 1 - self.me}] + [self.partner(k) for k in range(self.steps)]

    def range_at(self, s, k):
        start, size, land = s * self.part.per, self.part.per, s * self.part.per
        for i in range(k):
            size //= 2
            start = start + self.high(self.orders[s][i]) * size
            if i < k - 1:
                land += size
        return start, size, land

    def core_copy(self):
        return send_copy(
            self.given.at[1 - self.me], self.got, self.core.at[0], self.core.at[1], {"wa": 1 - self.me}
        )

    def down_copy(self, s, k):
        start, size, _ = self.range_at(s, k)
        _, half, land = self.range_at(s, k + 1)
        which = self.orders[s][k]
        give = start + (1 - self.high(which)) * half
        return send_copy(
            self.leave.at[pl.ds(give, half)],
            self.landed.at[pl.ds(land, half)],
            self.down.at[0, k, s],
            self.down.at[1, k, s],
            self.partner(which),
        )

    def up_copy(self, s, k):
        start, size, _ = self.range_at(s, k + 1)
        ref = self.out.at[pl.ds(start, size)]
        return send_copy(ref, ref, self.up.at[0, k, s], self.up.at[1, k, s], self.partner(self.orders[s][k]))

    def add(self, s, k):
        start, size, land = self.range_at(s, k)
        last = k == self.steps

        def summed(at, count):
            if k == 0:
                own = self.given[self.me, pl.ds(start + at, count)].astype(F32)
                return own + self.got[pl.ds(start + at, count)].astype(F32)
            return self.total[pl.ds(start + at, count)] + self.landed[pl.ds(land + at, count)].astype(F32)

        if last:

            def finish(at, count):
                self.out[pl.ds(start + at, count)] = summed(at, count).astype(BF)

            in_chunks(size, finish)
            return
        half = size // 2
        high = self.high(self.orders[s][k])
        give, keep = (1 - high) * half, high * half

        def to_leave(at, count):
            self.leave[pl.ds(start + give + at, count)] = summed(give + at, count).astype(BF)

        def to_keep(at, count):
            self.total[pl.ds(start + keep + at, count)] = summed(keep + at, count)

        in_chunks(half, to_leave)
        self.down_copy(s, k).start()
        in_chunks(half, to_keep)

    def reduce_stage(self, at):
        if at == 0:
            self.core_copy().start()
            return
        if at == 1:
            self.core_copy().wait()
        for s in range(self.part.streams):
            if at > 1:
                self.down_copy(s, at - 2).wait()
            self.add(s, at - 1)

    def spread_stage(self, at):
        for s in range(self.part.streams):
            if at > 0:
                self.up_copy(s, self.steps - at).wait()
            if at < self.steps:
                self.up_copy(s, self.steps - at - 1).start()

    def take_share(self, source):
        for s in range(self.part.streams):
            start, size, _ = self.range_at(s, self.steps)
            in_chunks(size, lambda at, count, start=start: copy_pieces(self.out, source, start + at, count))


def sum_kernel(plan, late_given, early_share, early_out, late_out, *traffic):
    late = Summing(plan.late, late_given, late_out, traffic[:7])
    early = Summing(plan.early, None, early_out, (None,) * 6 + traffic[7:])
    steps = late.steps
    greet(late.partners())
    late.reduce_stage(0)
    early.take_share(early_share)
    early.spread_stage(0)
    late.reduce_stage(1)
    for at in range(steps):
        early.spread_stage(at + 1)
        late.reduce_stage(at + 2)
    for at in range(steps + 1):
        late.spread_stage(at)


def finish_kernel(plan, grad_low, early, late, grad, *outs):
    d, inner = plan.d, plan.inner
    half = inner // 2
    grad[...] = grad_low[...].astype(F32)

    @pl.when(pl.program_id(0) == 0)
    def _():
        me = lax.axis_index("wa")

        def matrix(name):
            part, ref = (plan.early, early) if name in plan.early.starts else (plan.late, late)
            first, used = part.starts[name]
            parts = []
            for b in range(first, first + blocks_of(used)):
                value = ref[b * ROWS_OF : (b + 1) * ROWS_OF].reshape(ROWS_OF * 16, LANES)
                parts.append(value.astype(F32))
            return jnp.concatenate(parts, axis=1)

        def my_half(line, size):
            return jnp.where(me == 0, line[:, 0:size], line[:, size : 2 * size])

        turned = matrix("vec")[0:half].T

        def write(ref, pieces):
            ref[...] = jnp.concatenate(pieces, axis=1).reshape(ref.shape)

        for side, taps in enumerate((ENCODER_TAPS, DECODER_TAPS)):
            tag = "ed"[side]
            first_g, first_b, red_w, red_b, mid_g, mid_b, ker, ker_b, last_g, last_b, exp_w, exp_b = outs[
                12 * side : 12 * side + 12
            ]
            at = 8 * side
            write(first_g, [turned[at : at + 1], turned[at + 1 : at + 2]])
            write(first_b, [turned[at + 2 : at + 3], turned[at + 3 : at + 4]])
            write(mid_g, [turned[at + 4 : at + 5]])
            write(mid_b, [turned[at + 5 : at + 6]])
            write(last_g, [turned[at + 6 : at + 7]])
            write(last_b, [turned[at + 7 : at + 8]])
            value = matrix(tag + "_we")
            exp_w[...] = value[0:half, 0:d]
            write(exp_b, [my_half(value[half : half + 1, 0:d], d // 2)])
            value = matrix(tag + "_k")
            for j in range(taps):
                ker[j] = value[0:half, j * inner : (j + 1) * inner]
            centre = (ENCODER_SHIFTS if side == 0 else DECODER_SHIFTS).index(0)
            write(ker_b, [my_half(value[half : half + 1, centre * inner : (centre + 1) * inner], half)])
            value = matrix(tag + "_wr")[0:half]
            red_w[...] = value[:, 0:d]
            write(red_b, [value[:, d:].T[0:1]])


def local(n, stream, doc_start, doc_end, cotangent, *weights):
    rows, d = stream.shape[1], stream.shape[2]
    inner = weights[6].shape[1] * 2
    steps = rows // TILE
    x, cot = stream[0].T, cotangent[0].T
    starts, ends = doc_start, doc_end
    weights = [w.T if at % 12 == 2 else w for at, w in enumerate(weights)]
    enc, dec = gather_weights(weights, d, inner)
    wrt_e, kt_e, wet_e, we_e, kb_e, wr_e, g1_e, f1_e, b1_e, g2_e, f2_e, b2_e, g3_e, f3_e, b3_e = enc
    wrt_d, kt_d, wet_d, we_d, kb_d, wr_d, g1_d, f1_d, b1_d, g2_d, f2_d, b2_d, g3_d, f3_d, b3_d = dec

    plan = Plan(d, inner, steps, n)
    blocks = rows // LANES
    per = TILE // LANES

    def spec(a):
        return whole(a.shape)

    def wide(channels, dtype=BF):
        return jax.ShapeDtypeStruct((channels, rows), dtype)

    def fixed(shape, dtype=F32):
        return jax.ShapeDtypeStruct(shape, dtype)

    class Order:
        def __init__(self, first):
            self.tile = lambda i: (i + first) % steps

        def cols(self, channels):
            return pl.BlockSpec((channels, TILE), lambda i: (0, self.tile(i)))

        def before(self, channels):
            return pl.BlockSpec((channels, LANES), lambda i: (0, (per * self.tile(i) + blocks - 1) % blocks))

        def after(self, channels):
            return pl.BlockSpec((channels, LANES), lambda i: (0, (per * self.tile(i) + per) % blocks))

    def head(channels):
        return pl.BlockSpec((channels, LANES), lambda i: (0, 0))

    def tail(channels):
        return pl.BlockSpec((channels, LANES), lambda i: (0, blocks - 1))

    plain, later = Order(0), Order(1)
    d1, i1 = d + AUG, inner + AUG
    norm_wide = [(d1, BF), (d, BF), (d, BF), (8, F32)]
    norm_in = [(i1, BF), (inner, BF), (inner, BF), (8, F32)]
    sem = pltpu.SemaphoreType.DMA
    vmem = pltpu.VMEM

    def outs_of(order, items):
        return [wide(c, t) for c, t in items], [order.cols(c) for c, _ in items]

    shapes, specs = outs_of(plain, norm_wide + norm_in)
    ins = [wrt_e, f1_e, b1_e, f2_e, b2_e]
    h1e, z1e, d1e, r1e, h2e, z2e, d2e, r2e = pl.pallas_call(
        enc_in_kernel,
        grid=(steps,),
        out_shape=shapes,
        in_specs=[plain.cols(d)] + [spec(a) for a in ins],
        out_specs=specs,
        scratch_shapes=[vmem((d, TILE), F32), vmem((inner, TILE), F32)],
        compiler_params=params(),
        name="encoder_in",
    )(x, *ins)

    shapes, specs = outs_of(later, norm_in + [(d, BF)] + norm_wide + norm_in)
    ins = [kt_e, wet_e, wrt_d, f3_e, b3_e, f1_d, b1_d, f2_d, b2_d]
    h3e, z3e, d3e, r3e, x1, h1d, z1d, d1d, r1d, h2d, z2d, d2d, r2d, edge_d = pl.pallas_call(
        functools.partial(enc_out_kernel, steps),
        grid=(steps,),
        out_shape=shapes + [fixed((i1, LANES), BF)],
        in_specs=[later.cols(1), later.cols(1), later.before(i1), later.cols(i1), later.after(i1)]
        + [head(i1), tail(i1), later.cols(d)]
        + [spec(a) for a in ins],
        out_specs=specs + [whole((i1, LANES))],
        scratch_shapes=[
            vmem((ENCODER_TAPS * inner + AUG, TILE), BF),
            vmem((inner, LANES), BF),
            vmem((inner, LANES), BF),
            vmem((inner, TILE), F32),
            vmem((d, TILE), F32),
            vmem((inner, TILE), F32),
        ]
        + [vmem((i1, LANES), BF)] * 4
        + [sem((3,)), sem((3,))],
        compiler_params=params(1),
        name="encoder_out",
    )(starts, ends, h2e, h2e, h2e, h2e, h2e, x, *ins)

    small, large = fixed((inner, LANES)), fixed((d, LANES))
    sums = [fixed((i1, d)), small, small]
    ins = [kt_d, we_d, wet_d, f3_d, b3_d, g3_d]
    out, evr_d, dwe_d, dg3_d, db3_d = pl.pallas_call(
        functools.partial(dec_out_kernel, steps),
        grid=(steps,),
        out_shape=[wide(d, F32), wide(inner)] + sums,
        in_specs=[plain.cols(1), plain.cols(1), plain.before(i1), plain.cols(i1), spec(edge_d)]
        + [plain.cols(d), plain.cols(d)]
        + [spec(a) for a in ins],
        out_specs=[plain.cols(d), plain.cols(inner)] + [whole(s.shape) for s in sums],
        scratch_shapes=[
            vmem((DECODER_TAPS * inner + AUG, TILE), BF),
            vmem((inner, LANES), BF),
            vmem((inner, TILE), F32),
            vmem((i1, TILE), BF),
            vmem((inner, TILE), BF),
            vmem((inner, TILE), BF),
            vmem((8, TILE), F32),
            vmem((inner, TILE), F32),
            vmem((inner, TILE), BF),
        ],
        compiler_params=params(),
        name="decoder_out",
    )(starts, ends, h2d, h2d, edge_d, cot, x1, *ins)

    shapes, specs = outs_of(plain, [(d, BF), (inner, BF)])
    early = fixed((2, plan.early.pieces, 16, LANES), BF)
    sums = [small, small, large, large, small, small]
    ins = [kb_d, wr_d, we_e, g2_d, g1_d, g3_e]
    stash = [h2d, z2d, d2d, r2d, h1d, z1d, d1d, r1d, cot, h3e, z3e, d3e, r3e]
    ey, evr_e, packed, dg2_d, db2_d, dg1_d, db1_d, dg3_e, db3_e = pl.pallas_call(
        functools.partial(dec_back_kernel, plan),
        grid=(steps,),
        out_shape=shapes + [early] + sums,
        in_specs=[plain.cols(1), plain.cols(1), plain.cols(inner), plain.after(inner), head(inner)]
        + [spec(a) for a in ins]
        + [plain.cols(a.shape[0]) for a in stash]
        + [spec(dwe_d)],
        out_specs=specs + [whole(early.shape)] + [whole(s.shape) for s in sums],
        scratch_shapes=[
            vmem((i1, DECODER_TAPS * inner), F32),
            vmem((inner, d1), F32),
            vmem((i1, d), F32),
            vmem((DECODER_TAPS * inner, TILE), BF),
            vmem((inner, LANES), BF),
            vmem((inner, TILE), F32),
            vmem((d, TILE), F32),
            vmem((inner, TILE), BF),
            vmem((d, TILE), BF),
            vmem((inner, LANES), BF),
            sem((1,)),
            sem((1,)),
        ],
        compiler_params=params(2),
        name="decoder_back",
    )(starts, ends, evr_d, evr_d, evr_d, *ins, *stash, dwe_d)

    late = fixed((2, plan.late.pieces, 16, LANES), BF)
    early_sum = fixed((plan.early.pieces, 16, LANES), BF)
    ins = [kb_e, wr_e, g2_e, g1_e]
    stash = [h2e, z2e, d2e, r2e, h1e, z1e, d1e, r1e, ey]
    vecs = [dg3_e, db3_e, dg1_d, db1_d, dg2_d, db2_d, dg3_d, db3_d]
    grad_low, packed_late, summed = pl.pallas_call(
        functools.partial(enc_back_kernel, plan),
        grid=(steps,),
        out_shape=[wide(d), late, early_sum],
        in_specs=[later.cols(1), later.cols(1), later.before(inner), later.cols(inner), later.after(inner)]
        + [head(inner), tail(inner)]
        + [spec(a) for a in ins]
        + [later.cols(a.shape[0]) for a in stash]
        + [whole(early.shape)]
        + [spec(a) for a in vecs],
        out_specs=[later.cols(d), whole(late.shape), whole(early_sum.shape)],
        scratch_shapes=[
            vmem((i1, ENCODER_TAPS * inner), F32),
            vmem((inner, d1), F32),
            vmem((inner, LANES), F32),
            vmem((inner, LANES), F32),
            vmem((d, LANES), F32),
            vmem((d, LANES), F32),
            vmem((ENCODER_TAPS * inner, TILE), BF),
            vmem((inner, LANES), BF),
            vmem((inner, LANES), BF),
            vmem((inner, TILE), F32),
            vmem((d, TILE), F32),
            vmem((inner, TILE), BF),
            vmem((d, TILE), BF),
            vmem((inner, LANES), BF),
            vmem((inner, LANES), BF),
            sem((2,)),
            sem((2,)),
        ]
        + Summing.scratch(plan.early),
        compiler_params=params(3),
        name="encoder_back",
    )(starts, ends, evr_e, evr_e, evr_e, evr_e, evr_e, *ins, *stash, packed, *vecs)

    vm = pl.BlockSpec(memory_space=pltpu.VMEM)
    early_whole, late_whole = pl.pallas_call(
        functools.partial(sum_kernel, plan),
        out_shape=[early_sum, fixed((plan.late.pieces, 16, LANES), BF)],
        in_specs=[vm, vm],
        out_specs=[vm, vm],
        scratch_shapes=Summing.scratch(plan.late)
        + Summing.spread_scratch(plan.late)
        + Summing.spread_scratch(plan.early),
        compiler_params=params(4),
        name="sum_gradients",
    )(packed_late, summed)

    grad, *shares = pl.pallas_call(
        functools.partial(finish_kernel, plan),
        grid=(steps,),
        out_shape=[wide(d, F32)] + [fixed(w.shape) for w in weights],
        in_specs=[plain.cols(d), whole(early_whole.shape), whole(late_whole.shape)],
        out_specs=[plain.cols(d)] + [whole(w.shape) for w in weights],
        compiler_params=params(),
        name="finish",
    )(grad_low, early_whole, late_whole)
    shares = [w.T if at % 12 == 2 else w for at, w in enumerate(shares)]
    return (out.T[None], grad.T[None], *shares)


def solution(mesh):
    rows = P("wa", "seq", None)
    block = (
        P("wa"), P("wa"), P(None, "wa"), P("wa"), P("wa"), P("wa"),
        P(None, "wa", None), P("wa"), P("wa"), P("wa"), P("wa", None), P("wa"),
    )
    return jax.shard_map(
        functools.partial(local, mesh.shape["seq"]),
        mesh=mesh,
        in_specs=(rows, P("wa", "seq"), P("wa", "seq"), rows, *block, *block),
        out_specs=(rows, rows, *block, *block),
        check_vma=False,
    )
```

```python
import functools

import jax
import jax.numpy as jnp
from jax import lax
from jax.experimental import pallas as pl
from jax.experimental.pallas import tpu as pltpu
from jax.sharding import PartitionSpec as P

ENCODER_TAPS = 5
ENCODER_DILATION = 8
DECODER_TAPS = 3
DECODER_DILATION = 16
EPS = 1e-05

MESH = pl.DeviceIdType.MESH
BF = jnp.bfloat16
F32 = jnp.float32
LANES = 128
TILE = 512
HALF = 256
AUG = 16
VMEM_LIMIT = 56 * 1024 * 1024
GELU_1 = 2.0 * 0.7978845608028654
GELU_3 = 8.0 * 0.7978845608028654 * 0.044715

ENCODER_SHIFTS = tuple(ENCODER_DILATION * (j - ENCODER_TAPS // 2) for j in range(ENCODER_TAPS))
DECODER_SHIFTS = tuple(-DECODER_DILATION * (DECODER_TAPS - 1 - j) for j in range(DECODER_TAPS))


def params(collective=None):
    if collective is None:
        return pltpu.CompilerParams(vmem_limit_bytes=VMEM_LIMIT)
    return pltpu.CompilerParams(
        vmem_limit_bytes=VMEM_LIMIT, collective_id=collective, has_side_effects=True
    )


def whole(shape):
    return pl.BlockSpec(shape, lambda *_: (0,) * len(shape))


def nt_dot(left, right):
    return lax.dot_general(left, right, (((1,), (1,)), ((), ())), preferred_element_type=F32)


def nn_dot(left, right):
    return jnp.dot(left, right, preferred_element_type=F32)


def lanes_of(column, width):
    return jnp.concatenate([column] * (width // LANES), axis=1)


def fold(value):
    total = value[:, :LANES]
    for at in range(LANES, value.shape[1], LANES):
        total = total + value[:, at : at + LANES]
    return total


def weights_kernel(dims, *refs):
    d, inner, taps = dims
    n_in = 24
    ins, refs = refs[:n_in], refs[n_in:]
    results, refs = refs[:30], refs[30:]
    outs, refs = refs[:30], refs[30:]
    (small_own, small_got, k_own0, k_own1, e_own0, e_own1, r_own0, r_own1, *rest) = refs
    (r_got0, r_got1, k_got0, k_got1, e_got0, e_got1, k_all, send, recv, store) = rest
    me = lax.axis_index("wa")
    other = 1 - me
    barrier = pltpu.get_barrier_semaphore()
    pl.semaphore_signal(barrier, inc=1, device_id={"wa": other}, device_id_type=MESH)
    pl.semaphore_wait(barrier, 1)

    half = inner // 2
    pad = k_own0.shape[1]
    small_own[...] = jnp.zeros_like(small_own)
    small_at = []
    for side in range(2):
        for at in (0, 1, 3, 4, 5, 7, 8, 9, 11):
            small_at.append(12 * side + at)
    for row, at in enumerate(small_at):
        n = ins[at].shape[0]
        small_own[row : row + 1, 0:n] = ins[at][...].astype(F32).reshape(1, n)
    owns, gots = [], []
    for side, (k_own, e_own, r_own) in enumerate(((k_own0, e_own0, r_own0), (k_own1, e_own1, r_own1))):
        base = 12 * side
        k_own[:, half - 8 : pad, :] = jnp.zeros((taps[side], pad - half + 8, inner), BF)
        k_own[:, 0:half, :] = ins[base + 6][...]
        e_own[half - 8 : pad, :] = jnp.zeros((pad - half + 8, d), BF)
        e_own[0:half, :] = ins[base + 10][...]
        r_own[half - 8 : pad, :] = jnp.zeros((pad - half + 8, d), BF)
        r_own[0:half, :] = ins[base + 2][...]
        owns += [r_own, k_own, e_own]
    owns.append(small_own)
    gots = [r_got0, k_got0, e_got0, r_got1, k_got1, e_got1, small_got]
    copies = []
    pairs = list(zip(owns, gots))
    for at in (6, 0, 2, 1, 3, 5, 4):
        own, got = pairs[at]
        copies.append(
            pltpu.make_async_remote_copy(
                src_ref=own,
                dst_ref=got,
                send_sem=send.at[at],
                recv_sem=recv.at[at],
                device_id={"wa": other},
                device_id_type=MESH,
            )
        )
        copies[-1].start()
    arrival = dict(zip((6, 0, 2, 1, 3, 5, 4), copies))
    stores = []

    def keep(at):
        stores.append(pltpu.make_async_copy(outs[at], results[at], store.at[at]))
        stores[-1].start()

    first_core = me == 0
    square = (HALF, HALF)
    unit = lax.broadcasted_iota(jnp.int32, square, 0) == lax.broadcasted_iota(jnp.int32, square, 1)
    unit = jnp.where(unit, 1.0, 0.0).astype(BF)

    def turn(out, columns, count, width=None):
        for a in range(0, count, HALF):
            b = min(a + HALF, count)
            piece = nt_dot(unit[0 : b - a, 0 : b - a], columns(a, b)).astype(BF)
            if width is None:
                out[a:b, :] = piece
            else:
                out[a:b, 0:width] = piece

    def ordered(own, got):
        own, got = own.astype(F32), got.astype(F32)
        return jnp.where(first_core, own, got), jnp.where(first_core, got, own)

    arrival[6].wait()
    small0, small1 = ordered(small_own[...], small_got[...])

    def column(row, n):
        line = jnp.concatenate([small0[row : row + 1, 0 : n // 2], small1[row : row + 1, 0 : n // 2]], axis=1)
        return jnp.broadcast_to(line, (LANES, n)).T

    def bias_columns(value):
        where = lax.broadcasted_iota(jnp.int32, (value.shape[0], AUG), 1) == 0
        return jnp.where(where, value[:, :AUG], 0.0).astype(BF)

    for side in range(2):
        o = outs[15 * side : 15 * side + 15]
        wrt, kt, wet, we, kb, wr, *vectors = o
        base = 9 * side
        for at, (row, n) in enumerate(((0, d), (3, inner), (6, inner))):
            gain, half_gain, half_bias = vectors[3 * at : 3 * at + 3]
            gain[...] = column(base + row, n)
            half_gain[...] = gain[...] * 0.5
            half_bias[...] = column(base + row + 1, n) * 0.5
        n = taps[side]
        first = 15 * side
        for at in range(6, 15):
            keep(first + at)
        arrival[3 * side].wait()
        r0, r1 = ordered(owns[3 * side][0:half, :], gots[3 * side][0:half, :])
        wrt[:, 0:d] = jnp.concatenate([r0, r1], axis=0).astype(BF)
        wrt[:, d : d + AUG] = bias_columns(column(base + 2, inner))
        keep(first)
        turn(wr, lambda a, b: wrt[:, a:b], d)
        keep(first + 5)
        arrival[3 * side + 2].wait()
        e0, e1 = ordered(owns[3 * side + 2][0:half, :], gots[3 * side + 2][0:half, :])
        we[...] = jnp.concatenate([e0, e1], axis=0).astype(BF)
        keep(first + 3)
        turn(wet, lambda a, b: we[:, a:b], d, inner)
        wet[:, inner : inner + AUG] = bias_columns(column(base + 8, d))
        keep(first + 2)
        arrival[3 * side + 1].wait()
        for j in range(n):
            k0, k1 = ordered(owns[3 * side + 1][j, 0:half, :], gots[3 * side + 1][j, 0:half, :])
            k = jnp.concatenate([k0, k1], axis=0).astype(BF)
            for channels, place in tap_pieces(j, n, inner):
                kb[:, place] = k[:, channels]
                k_all[place, :] = k[channels, :]
        keep(first + 4)
        turn(kt, lambda a, b: k_all[0 : n * inner, a:b], inner, n * inner)
        kt[:, n * inner : n * inner + AUG] = bias_columns(column(base + 5, inner))
        keep(first + 1)
    for copy in stores:
        copy.wait()


def gather_weights(args, d, inner):
    taps = (ENCODER_TAPS, DECODER_TAPS)
    half = inner // 2
    pad = -(-half // 16) * 16
    shapes = []
    for n in taps:
        shapes += [
            ((inner, d + AUG), BF),
            ((inner, n * inner + AUG), BF),
            ((d, inner + AUG), BF),
            ((inner, d), BF),
            ((inner, n * inner), BF),
            ((d, inner), BF),
        ]
        for c in (d, inner, inner):
            shapes += [((c, LANES), F32)] * 3
    vm = pl.BlockSpec(memory_space=pltpu.VMEM)
    small = pltpu.VMEM((24, 512), F32)
    kk = [pltpu.VMEM((n, pad, inner), BF) for n in taps]
    ee = [pltpu.VMEM((pad, d), BF)] * 2
    outs = pl.pallas_call(
        functools.partial(weights_kernel, (d, inner, taps)),
        out_shape=[jax.ShapeDtypeStruct(*s) for s in shapes],
        in_specs=[vm] * 24,
        out_specs=[pl.BlockSpec(memory_space=pl.ANY)] * 30,
        scratch_shapes=[pltpu.VMEM(*shape) for shape in shapes]
        + [small, small, *kk, *ee, *ee, *ee, *kk, *ee]
        + [pltpu.VMEM((taps[0] * inner, inner), BF)]
        + [pltpu.SemaphoreType.DMA((7,)), pltpu.SemaphoreType.DMA((7,)), pltpu.SemaphoreType.DMA((30,))],
        compiler_params=params(0),
        name="gather_weights",
    )(*args)
    return outs[:15], outs[15:]


def pacing(thunks, slots):
    state = [0, 0]
    thunks = list(thunks)

    def between():
        while state[1] < len(thunks) and state[0] * len(thunks) >= state[1] * slots:
            thunks[state[1]]()
            state[1] += 1
        state[0] += 1

    return between


def add_product(total, left, right):
    def piece(at, stop):
        total[:, at:stop] += nt_dot(left[...], right[at:stop, :])

    columns = right.shape[0]
    return [functools.partial(piece, at, min(at + HALF, columns)) for at in range(0, columns, HALF)]


def norm_forward(src, lanes, channels, gain, bias, h_out, z_out, d_out, r_out, keep=None, fill=(), at=None, h_copy=None):
    width = lanes.stop - lanes.start
    between = pacing(fill, 3 * (channels // 16))
    total = [jnp.zeros((8, width), F32) for _ in range(4)]
    for c in range(0, channels, 16):
        between()
        x = src[c : c + 16, at or lanes].astype(F32)
        if keep is not None:
            keep[c : c + 16, at or lanes] = x
        k = (c // 8) % 4
        total[k] = total[k] + x[0:8]
        total[k + 1] = total[k + 1] + x[8:16]
    mean = jnp.sum((total[0] + total[1]) + (total[2] + total[3]), axis=0, keepdims=True) * (1.0 / channels)
    wide = jnp.broadcast_to(mean, (16, width))
    values = src if keep is None else keep
    total = [jnp.zeros((8, width), F32) for _ in range(4)]
    for c in range(0, channels, 16):
        between()
        centre = values[c : c + 16, at or lanes] - wide
        square = centre * centre
        k = (c // 8) % 4
        total[k] = total[k] + square[0:8]
        total[k + 1] = total[k + 1] + square[8:16]
    spread = jnp.sum((total[0] + total[1]) + (total[2] + total[3]), axis=0, keepdims=True) * (1.0 / channels)
    r = lax.rsqrt(spread + EPS)
    if r_out is not None:
        r_out[:, lanes] = jnp.broadcast_to(r, (8, width))
    rw = jnp.broadcast_to(r, (16, width))
    mw = jnp.broadcast_to(mean * r, (16, width))
    one, point = BF(1.0), BF(0.5)
    for c in range(0, channels, 16):
        between()
        rows = slice(c, c + 16)
        z = values[rows, at or lanes] * rw - mw
        half = (z * lanes_of(gain[rows, :], width) + lanes_of(bias[rows, :], width)).astype(BF)
        sq = half * half
        t = jnp.tanh(half * (sq * BF(GELU_3) + BF(GELU_1)))
        up = one + t
        h_out[rows, lanes] = half * up
        if h_copy is not None:
            h_copy[rows, :] = half * up
        d_out[rows, lanes] = up * (point + half * (sq * BF(1.5 * GELU_3) + BF(0.5 * GELU_1)) * (one - t))
        z_out[rows, lanes] = z.astype(BF)


def norm_backward(grad, lanes, channels, gain, z_in, d_in, r_in, gain_sum, bias_sum, keep, emit, fill=(), at=None):
    width = lanes.stop - lanes.start
    between = pacing(fill, 2 * (channels // 16))
    one = [jnp.zeros((8, width), F32) for _ in range(2)]
    two = [jnp.zeros((8, width), F32) for _ in range(2)]
    r = r_in[0:1, lanes]
    rw = jnp.broadcast_to(r, (16, width))
    for c in range(0, channels, 16):
        between()
        rows = slice(c, c + 16)
        da = grad[rows, at or lanes] * d_in[rows, lanes].astype(F32)
        p = da * z_in[rows, lanes].astype(F32)
        bias_sum[rows, :] += fold(da)
        gain_sum[rows, :] += fold(p)
        wide = lanes_of(gain[rows, :], width)
        dz = da * wide
        q = p * wide
        keep[rows, at or lanes] = (dz * rw).astype(BF)
        for k in range(2):
            one[k] = one[k] + dz[8 * k : 8 * k + 8]
            two[k] = two[k] + q[8 * k : 8 * k + 8]
    scale = r * (1.0 / channels)
    m1 = jnp.broadcast_to(jnp.sum(one[0] + one[1], axis=0, keepdims=True) * scale, (16, width)).astype(BF)
    m2 = jnp.broadcast_to(jnp.sum(two[0] + two[1], axis=0, keepdims=True) * scale, (16, width)).astype(BF)
    for c in range(0, channels, 16):
        between()
        rows = slice(c, c + 16)
        emit(rows, keep[rows, at or lanes] - (z_in[rows, lanes] * m2 + m1))


def tap_mask(starts, ends, first, shift):
    place = first + shift + lax.broadcasted_iota(jnp.int32, (8, TILE), 1)
    usable = (place >= jnp.broadcast_to(starts[...], (8, TILE))) & (place < jnp.broadcast_to(ends[...], (8, TILE)))
    one = jnp.where(usable, 1.0, 0.0)
    return jnp.concatenate([one, one], axis=0).astype(BF)


def tap_row(j, c, taps, inner):
    aligned = inner // LANES * LANES
    return j * aligned + c if c < aligned else taps * aligned + j * (inner - aligned) + c - aligned


def tap_pieces(j, taps, inner):
    aligned = inner // LANES * LANES
    for a, b in ((0, aligned), (aligned, inner)):
        at = tap_row(j, a, taps, inner)
        yield slice(a, b), slice(at, at + b - a)


def stack_taps(stack, shifts, before, main, after, starts, ends, first, inner):
    for j, shift in enumerate(shifts):
        if not shift:
            for channels, place in tap_pieces(j, len(shifts), inner):
                stack[place, :] = main[channels, :]
            continue
        mask = tap_mask(starts, ends, first, shift)
        for c in range(0, inner, 16):
            rows = slice(c, c + 16)
            if shift < 0:
                span = jnp.concatenate([before[rows, :], main[rows, :]], axis=1)
                span = pltpu.roll(span, -shift, 1)[:, LANES:]
            else:
                span = jnp.concatenate([main[rows, :], after[rows, :]], axis=1)
                span = pltpu.roll(span, TILE + LANES - shift, 1)[:, :TILE]
            at = tap_row(j, c, len(shifts), inner)
            stack[at : at + 16, :] = span * mask


def ones_rows(width):
    where = lax.broadcasted_iota(jnp.int32, (AUG, width), 0) == 0
    return jnp.where(where, 1.0, 0.0).astype(BF)


def neighbours():
    me = lax.axis_index("seq")
    n = lax.axis_size("seq")
    return lax.rem(me + n - 1, n), lax.rem(me + 1, n)


def greet(others):
    barrier = pltpu.get_barrier_semaphore()
    for device in others:
        pl.semaphore_signal(barrier, inc=1, device_id=device, device_id_type=MESH)
    pl.semaphore_wait(barrier, len(others))


def send_copy(src, dst, send_sem, recv_sem, device):
    return pltpu.make_async_remote_copy(
        src_ref=src, dst_ref=dst, send_sem=send_sem, recv_sem=recv_sem, device_id=device, device_id_type=MESH
    )


def later_tile(step, steps):
    return lax.rem(step + 1, steps)


def first_place(tile, steps):
    return lax.axis_index("seq") * (steps * TILE) + tile * TILE


CHAINS = (slice(0, HALF), slice(HALF, TILE))
EVERY = slice(0, HALF)


def enc_in_kernel(x, wrt, g1, b1, g2, b2, h1, z1, d1, r1, h2, z2, d2, r2, xt, u0, u1, h_wide0, h_wide1):
    d, inner = x.shape[0], wrt.shape[0]
    h1[d : d + AUG, :] = ones_rows(TILE)
    h2[inner : inner + AUG, :] = ones_rows(TILE)
    u, h_wide = (u0, u1), (h_wide0, h_wide1)
    for k in range(2):
        h_wide[k][d : d + AUG, :] = ones_rows(HALF)
        norm_forward(x, CHAINS[k], d, g1, b1, h1, z1, d1, r1, xt, h_copy=h_wide[k])
        u[k][...] = nn_dot(wrt[...], h_wide[k][...])
    for k in range(2):
        norm_forward(u[k], CHAINS[k], inner, g2, b2, h2, z2, d2, r2, at=EVERY)


def choose_edge(window, block, edge, at_end):
    window[...] = block[0 : window.shape[0], :]

    @pl.when(at_end)
    def _():
        window[...] = edge[0 : window.shape[0], :]


def trade_edges(step, steps, head, tail, got_l, got_r, send, recv, others=()):
    left, right = neighbours()
    to_left = send_copy(head, got_r, send.at[0], recv.at[0], {"seq": left})
    to_right = send_copy(tail, got_l, send.at[1], recv.at[1], {"seq": right})

    @pl.when(step == 0)
    def _():
        greet([{"seq": left}, {"seq": right}, *others])
        to_left.start()
        to_right.start()

    @pl.when(step == steps - 2)
    def _():
        to_left.wait()
        to_right.wait()


def enc_out_kernel(
    steps, starts, ends, before, main, after, head, tail, xt, kt, wet, wrt, g3, b3, g1, b1, g2, b2,
    h3, z3, d3, r3, x1, h1, z1, d1, r1, h2, z2, d2, r2, edge_o,
    stack, win_b, win_a, v0, v1, y0, y1, u0, u1, h_in0, h_in1, h_wide0, h_wide1, got_l, got_r, own, got, send, recv,
):
    step = pl.program_id(0)
    d, inner = xt.shape[0], v0.shape[0]
    v, y, u, h_in, h_wide = (v0, v1), (y0, y1), (u0, u1), (h_in0, h_in1), (h_wide0, h_wide1)
    trade_edges(step, steps, head, tail, got_l, got_r, send, recv)
    choose_edge(win_b, before, got_l, step == steps - 1)
    choose_edge(win_a, after, got_r, step == steps - 2)
    stack_taps(stack, ENCODER_SHIFTS, win_b, main, win_a, starts, ends, first_place(later_tile(step, steps), steps), inner)
    stack[len(ENCODER_SHIFTS) * inner :, :] = ones_rows(TILE)
    h3[inner : inner + AUG, :] = ones_rows(TILE)
    h1[d : d + AUG, :] = ones_rows(TILE)
    h2[inner : inner + AUG, :] = ones_rows(TILE)
    one, two = CHAINS

    def make_v(k):
        v[k][...] = nn_dot(kt[...], stack[:, CHAINS[k]])

    def make_y(k):
        y[k][...] = nn_dot(wet[...], h_in[k][...]) + xt[:, CHAINS[k]].astype(F32)

    def make_u(k):
        u[k][...] = nn_dot(wrt[...], h_wide[k][...])

    def norm_last(k):
        norm_forward(v[k], CHAINS[k], inner, g3, b3, h3, z3, d3, r3, at=EVERY, h_copy=h_in[k])

    def norm_first(k):
        for c in range(0, d, 16):
            x1[c : c + 16, CHAINS[k]] = y[k][c : c + 16, :].astype(BF)
        norm_forward(y[k], CHAINS[k], d, g1, b1, h1, z1, d1, r1, at=EVERY, h_copy=h_wide[k])

    def norm_mid(k):
        norm_forward(u[k], CHAINS[k], inner, g2, b2, h2, z2, d2, r2, at=EVERY)

    for k in range(2):
        h_in[k][inner : inner + AUG, :] = ones_rows(HALF)
        h_wide[k][d : d + AUG, :] = ones_rows(HALF)
    make_v(0)
    make_v(1)
    norm_last(0)
    make_y(0)
    norm_last(1)
    make_y(1)
    norm_first(0)
    make_u(0)
    norm_first(1)
    make_u(1)
    norm_mid(0)
    norm_mid(1)

    def give():
        return send_copy(own, got, send.at[2], recv.at[2], {"seq": neighbours()[1]})

    @pl.when(step == steps - 2)
    def _():
        own[...] = h2[:, TILE - LANES : TILE]
        give().start()

    @pl.when(step == steps - 1)
    def _():
        give().wait()
        edge_o[...] = got[...]


def dec_out_kernel(
    plan, starts, ends, before, main, e_l, cot_t, x1, kt, we, wet, f3, b3, g3,
    out, evr, packed, dg3, db3,
    dwe, stack, win_b, v0, v1, h3, z3, d3, r3, g0, g1, kept0, kept1, h_in0, h_in1,
):
    steps = plan.steps
    step = pl.program_id(0)
    inner = v0.shape[0]
    v, g, kept, h_in = (v0, v1), (g0, g1), (kept0, kept1), (h_in0, h_in1)

    @pl.when(step == 0)
    def _():
        dwe[...] = jnp.zeros_like(dwe)
        dg3[...] = jnp.zeros_like(dg3)
        db3[...] = jnp.zeros_like(db3)

    choose_edge(win_b, before, e_l, step == 0)
    stack_taps(stack, DECODER_SHIFTS, win_b, main, None, starts, ends, first_place(step, steps), inner)
    stack[len(DECODER_SHIFTS) * inner :, :] = ones_rows(TILE)
    h3[inner : inner + AUG, :] = ones_rows(TILE)

    def make_out(k):
        out[:, CHAINS[k]] = nn_dot(wet[...], h_in[k][...]) + x1[:, CHAINS[k]].astype(F32)

    def back(k, fill):
        def emit(rows, value):
            evr[rows, CHAINS[k]] = value

        norm_backward(g[k], CHAINS[k], inner, g3, z3, d3, r3, dg3, db3, kept[k], emit, fill, EVERY)

    for k in range(2):
        h_in[k][inner : inner + AUG, :] = ones_rows(HALF)
        g[k][...] = nn_dot(we[...], cot_t[:, CHAINS[k]])
    for k in range(2):
        v[k][...] = nn_dot(kt[...], stack[:, CHAINS[k]])
    for k in range(2):
        norm_forward(v[k], CHAINS[k], inner, f3, b3, h3, z3, d3, r3, at=EVERY, h_copy=h_in[k])
    products = add_product(dwe, h3, cot_t)
    back(0, [lambda: make_out(0), *products[:2]])
    back(1, [lambda: make_out(1), *products[2:]])

    @pl.when(step == steps - 1)
    def _():
        pack_gradients(packed, plan, ((dwe, dwe.shape[1]),), ())


def dec_back_kernel(
    plan, starts, ends, main, after, head, kb, wr, we, g2, g1, g3,
    h2, z2, d2, r2, h1, z1, d1, r1, cot_t, h3, z3, d3, r3, given,
    ey, evr, packed, first, dg2, db2, dg1, db1, dg3, db3,
    dk, dwrt, dwe, stack, win_a, ga0, ga1, gb0, gb1, big0, big1, eur, eur0, eur1, ey0, ey1,
    kept0, kept1, keeps0, keeps1, got, send, recv, *traffic,
):
    steps = plan.steps
    sum_over = Summing(plan.first, given, first, traffic)
    k = sum_over.steps
    due = [0, 2] + [5 + 6 * i // max(1, k - 1) for i in range(k)]
    hook = hooks(steps, [(place, functools.partial(sum_over.reduce_stage, at)) for at, place in enumerate(due)])
    step = pl.program_id(0)
    d, inner = cot_t.shape[0], ga0.shape[0]
    ga, gb, big, eurs, eys = (ga0, ga1), (gb0, gb1), (big0, big1), (eur0, eur1), (ey0, ey1)
    kept, keeps = (kept0, kept1), (keeps0, keeps1)

    @pl.when(step == 0)
    def _():
        for ref in (dk, dwrt, dwe, dg2, db2, dg1, db1, dg3, db3):
            ref[...] = jnp.zeros_like(ref)

    left, right = neighbours()
    to_left = send_copy(head, got, send.at[0], recv.at[0], {"seq": left})

    @pl.when(step == 0)
    def _():
        greet([{"seq": left}, {"seq": right}, *sum_over.partners()])
        to_left.start()

    @pl.when(step == steps - 1)
    def _():
        to_left.wait()

    hook(0)
    choose_edge(win_a, after, got, step == steps - 1)
    back = tuple(-s for s in DECODER_SHIFTS)
    stack_taps(stack, back, None, main, win_a, starts, ends, first_place(step, steps), inner)

    def back2(k, fill):
        def emit(rows, value):
            eur[rows, CHAINS[k]] = value
            eurs[k][rows, :] = value

        norm_backward(ga[k], CHAINS[k], inner, g2, z2, d2, r2, dg2, db2, keeps[k], emit, fill, EVERY)

    def back1(k, fill):
        def emit(rows, value):
            total = value + cot_t[rows, CHAINS[k]]
            ey[rows, CHAINS[k]] = total
            eys[k][rows, :] = total

        norm_backward(big[k], CHAINS[k], d, g1, z1, d1, r1, dg1, db1, kept[k], emit, fill, EVERY)

    def back3(k, fill):
        def emit(rows, value):
            evr[rows, CHAINS[k]] = value

        norm_backward(gb[k], CHAINS[k], inner, g3, z3, d3, r3, dg3, db3, keeps[k], emit, fill, EVERY)

    for k in range(2):
        ga[k][...] = nn_dot(kb[...], stack[:, CHAINS[k]])
    by_k = add_product(dk, h2, stack)
    back2(0, by_k[:2])
    big[0][...] = nn_dot(wr[...], eur0[...])
    back2(1, by_k[2:])
    big[1][...] = nn_dot(wr[...], eur1[...])
    hook(1)
    by_r = add_product(dwrt, eur, h1)
    back1(0, by_r[:2])
    gb[0][...] = nn_dot(we[...], ey0[...])
    back1(1, by_r[2:])
    gb[1][...] = nn_dot(we[...], ey1[...])
    by_e = add_product(dwe, h3, ey)
    back3(0, by_e[:2])
    back3(1, by_e[2:])

    @pl.when(step == steps - 1)
    def _():
        pack_gradients(packed, plan, ((dk, dk.shape[1]), (dwrt, d + AUG), (dwe, d)), ())

    hook(2)


def enc_back_kernel(
    plan, starts, ends, before, main, after, head, tail, kb, wr, g2, g1,
    h2, z2, d2, r2, h1, z1, d1, r1, ey, given, first_share, *rest,
):
    vecs, rest = rest[:8], rest[8:]
    (
        grad, packed, summed, first_whole,
        dk, dwrt, dg2, db2, dg1, db1,
        stack, win_b, win_a, ga0, ga1, big0, big1, eur, eur0, eur1, kept0, kept1, keeps0, keeps1,
        got_l, got_r, send, recv, result, first_up,
    ), traffic = rest[:30], rest[30:]
    steps = plan.steps
    step = pl.program_id(0)
    d, inner = ey.shape[0], ga0.shape[0]
    ga, big, eurs = (ga0, ga1), (big0, big1), (eur0, eur1)
    kept, keeps = (kept0, kept1), (keeps0, keeps1)

    @pl.when(step == 0)
    def _():
        for ref in (dk, dwrt, dg2, db2, dg1, db1):
            ref[...] = jnp.zeros_like(ref)

    sum_over = Summing(plan.early, given, summed, traffic)
    trade_edges(step, steps, head, tail, got_l, got_r, send, recv, sum_over.partners())

    k = sum_over.steps
    due = [0, 2] + [6 + 6 * i // max(1, k - 1) for i in range(k)]
    actions = [(place, functools.partial(sum_over.reduce_stage, at)) for at, place in enumerate(due)]
    first = Summing(plan.first, None, result, (None,) * 6 + (first_up,))

    def begin():
        first.take_share(first_share)
        first.spread_stage(0)

    actions.append((1, begin))
    actions += [(3 + 8 * at // k, functools.partial(first.spread_stage, at + 1)) for at in range(k)]
    hook = hooks(steps, actions)

    hook(0)
    choose_edge(win_b, before, got_l, step == steps - 1)
    choose_edge(win_a, after, got_r, step == steps - 2)
    back = tuple(-s for s in ENCODER_SHIFTS)
    stack_taps(stack, back, win_b, main, win_a, starts, ends, first_place(later_tile(step, steps), steps), inner)

    def back2(k, fill):
        def emit(rows, value):
            eur[rows, CHAINS[k]] = value
            eurs[k][rows, :] = value

        norm_backward(ga[k], CHAINS[k], inner, g2, z2, d2, r2, dg2, db2, keeps[k], emit, fill, EVERY)

    def back1(k, fill):
        def emit(rows, value):
            grad[rows, CHAINS[k]] = value + ey[rows, CHAINS[k]]

        norm_backward(big[k], CHAINS[k], d, g1, z1, d1, r1, dg1, db1, kept[k], emit, fill, EVERY)

    for k in range(2):
        ga[k][...] = nn_dot(kb[...], stack[:, CHAINS[k]])
    by_k = add_product(dk, h2, stack)
    back2(0, by_k[:2])
    big[0][...] = nn_dot(wr[...], eur0[...])
    back2(1, by_k[2:4])
    big[1][...] = nn_dot(wr[...], eur1[...])
    hook(1)
    by_r = add_product(dwrt, eur, h1)
    back1(0, by_k[4:])
    back1(1, by_r)

    @pl.when(step == steps - 1)
    def _():
        in_chunks(plan.first.pieces, lambda at, count: copy_pieces(first_whole, result, at, count))
        sums = (dg1, db1, dg2, db2, *vecs)
        pack_gradients(packed, plan, ((dk, dk.shape[1]), (dwrt, d + AUG)), sums)

    hook(2)


ROWS_OF = 13


def blocks_of(used):
    return -(-used // LANES)


class Part:
    def __init__(self, sections, vectors, streams, n):
        self.starts, at = {}, 0
        for name, used in sections:
            self.starts[name] = (at, used)
            at += blocks_of(used)
        if vectors:
            self.starts["vec"] = (at, LANES)
            at += 1
        self.filled = at * ROWS_OF
        self.streams = streams
        self.per = -(-self.filled // (streams * n)) * n
        self.pieces = streams * self.per
        self.n = n
        self.bits = []
        while 1 << len(self.bits) < n:
            self.bits.append(1 << len(self.bits))


class Plan:
    def __init__(self, d, inner, steps, n):
        self.d, self.inner, self.steps, self.n = d, inner, steps, n
        self.first = Part((("d_we", d),), False, 2, n)
        early = (("d_k", DECODER_TAPS * inner), ("d_wr", d + AUG), ("e_we", d))
        self.early = Part(early, False, 2, n)
        self.late = Part((("e_k", ENCODER_TAPS * inner), ("e_wr", d + AUG)), True, 4, n)


def pack_gradients(packed, plan, mats, vecs):
    d, inner = plan.d, plan.inner
    half = inner // 2
    for w in range(2):
        at = 0
        for ref, used in mats:
            for b in range(blocks_of(used)):
                stop = min(used, LANES * (b + 1))
                lanes = slice(LANES * b, stop)
                for r in range(ROWS_OF):
                    base = half * w + 16 * r
                    if r < ROWS_OF - 1:
                        value = ref[base : base + 16, lanes]
                    else:
                        value = ref[base : base + 8, lanes]
                        low = ref[inner : inner + 8, lanes] if ref.shape[0] > inner else jnp.zeros_like(value)
                        value = jnp.concatenate([value, low], axis=0)
                    if stop - LANES * b < LANES:
                        blank = jnp.zeros((16, LANES * (b + 1) - stop), F32)
                        value = jnp.concatenate([value, blank], axis=1)
                    packed[w, at] = value.astype(BF)
                    at += 1
        if vecs:
            columns = []
            for ref in vecs:
                total = jnp.sum(ref[...], axis=1, keepdims=True)
                if ref.shape[0] == d:
                    columns.append(total[2 * half * w : 2 * half * w + half])
                    columns.append(total[2 * half * w + half : 2 * half * w + 2 * half])
                else:
                    columns.append(total[half * w : half * (w + 1)])
            lane = lax.broadcasted_iota(jnp.int32, (half, LANES), 1)
            value = jnp.zeros((half, LANES), F32)
            for lane_at, column in enumerate(columns):
                value = jnp.where(lane == lane_at, column, value)
            value = jnp.concatenate([value, jnp.zeros((ROWS_OF * 16 - half, LANES), F32)], axis=0)
            for r in range(ROWS_OF):
                packed[w, at] = value[16 * r : 16 * r + 16].astype(BF)
                at += 1
        left = packed.shape[1] - at
        if left:
            packed[w, at : packed.shape[1]] = jnp.zeros((left, 16, LANES), BF)


def in_chunks(count, body):
    size = max(c for c in range(1, 17) if count % c == 0)

    def step(i, _):
        body(i * size, size)
        return 0

    lax.fori_loop(0, count // size, step, 0)


def copy_pieces(dst, src, at, count):
    dst[pl.ds(at, count)] = src[pl.ds(at, count)]


def hooks(steps, actions):
    step = pl.program_id(0)

    def hook(at):
        for place, action in actions:
            where = (place // 2, place % 2) if place < 2 * steps else (steps - 1, 2)
            if where[1] == at:

                @pl.when(step == where[0])
                def _(action=action):
                    action()

    return hook


class Summing:
    def __init__(self, part, given, out, traffic):
        self.part, self.given, self.out = part, given, out
        self.got, self.total, self.leave, self.landed, self.core, self.down, *up = traffic
        self.up = up[0] if up else None
        self.me = lax.axis_index("wa")
        self.seq = lax.axis_index("seq")
        self.steps = len(part.bits)
        self.orders = []
        for s in range(part.streams):
            order = list(range(self.steps))
            if s % 2 and self.steps > 1:
                order[0], order[1] = order[1], order[0]
            self.orders.append(order)

    @staticmethod
    def scratch(part):
        sem = pltpu.SemaphoreType.DMA
        steps = max(1, len(part.bits))
        pieces = (part.pieces, 16, LANES)
        return [
            pltpu.VMEM(pieces, BF),
            pltpu.VMEM(pieces, F32),
            pltpu.VMEM(pieces, BF),
            pltpu.VMEM(pieces, BF),
            sem((2,)),
            sem((2, steps, part.streams)),
        ]

    @staticmethod
    def spread_scratch(part):
        return [pltpu.SemaphoreType.DMA((2, max(1, len(part.bits)), part.streams))]

    def high(self, which):
        return lax.rem(lax.div(self.seq, self.part.bits[which]), 2)

    def partner(self, which):
        bit = self.part.bits[which]
        return {"seq": self.seq + bit - 2 * bit * self.high(which)}

    def partners(self):
        return [{"wa": 1 - self.me}] + [self.partner(k) for k in range(self.steps)]

    def range_at(self, s, k):
        start, size, land = s * self.part.per, self.part.per, s * self.part.per
        for i in range(k):
            size //= 2
            start = start + self.high(self.orders[s][i]) * size
            if i < k - 1:
                land += size
        return start, size, land

    def core_copy(self):
        return send_copy(
            self.given.at[1 - self.me], self.got, self.core.at[0], self.core.at[1], {"wa": 1 - self.me}
        )

    def down_copy(self, s, k):
        start, size, _ = self.range_at(s, k)
        _, half, land = self.range_at(s, k + 1)
        which = self.orders[s][k]
        give = start + (1 - self.high(which)) * half
        return send_copy(
            self.leave.at[pl.ds(give, half)],
            self.landed.at[pl.ds(land, half)],
            self.down.at[0, k, s],
            self.down.at[1, k, s],
            self.partner(which),
        )

    def up_copy(self, s, k):
        start, size, _ = self.range_at(s, k + 1)
        ref = self.out.at[pl.ds(start, size)]
        return send_copy(ref, ref, self.up.at[0, k, s], self.up.at[1, k, s], self.partner(self.orders[s][k]))

    def add(self, s, k):
        start, size, land = self.range_at(s, k)
        last = k == self.steps

        def summed(at, count):
            if k == 0:
                own = self.given[self.me, pl.ds(start + at, count)].astype(F32)
                return own + self.got[pl.ds(start + at, count)].astype(F32)
            return self.total[pl.ds(start + at, count)] + self.landed[pl.ds(land + at, count)].astype(F32)

        if last:

            def finish(at, count):
                self.out[pl.ds(start + at, count)] = summed(at, count).astype(BF)

            in_chunks(size, finish)
            return
        half = size // 2
        high = self.high(self.orders[s][k])
        give, keep = (1 - high) * half, high * half

        def to_leave(at, count):
            self.leave[pl.ds(start + give + at, count)] = summed(give + at, count).astype(BF)

        def to_keep(at, count):
            self.total[pl.ds(start + keep + at, count)] = summed(keep + at, count)

        in_chunks(half, to_leave)
        self.down_copy(s, k).start()
        in_chunks(half, to_keep)

    def reduce_stage(self, at):
        if at == 0:
            self.core_copy().start()
            return
        if at == 1:
            self.core_copy().wait()
        for s in range(self.part.streams):
            if at > 1:
                self.down_copy(s, at - 2).wait()
            self.add(s, at - 1)

    def spread_stage(self, at):
        for s in range(self.part.streams):
            if at > 0:
                self.up_copy(s, self.steps - at).wait()
            if at < self.steps:
                self.up_copy(s, self.steps - at - 1).start()

    def take_share(self, source):
        for s in range(self.part.streams):
            start, size, _ = self.range_at(s, self.steps)
            in_chunks(size, lambda at, count, start=start: copy_pieces(self.out, source, start + at, count))


def sum_kernel(plan, late_given, early_share, early_out, late_out, *traffic):
    late = Summing(plan.late, late_given, late_out, traffic[:7])
    early = Summing(plan.early, None, early_out, (None,) * 6 + traffic[7:])
    steps = late.steps
    greet(late.partners())
    late.reduce_stage(0)
    early.take_share(early_share)
    early.spread_stage(0)
    late.reduce_stage(1)
    for at in range(steps):
        early.spread_stage(at + 1)
        late.reduce_stage(at + 2)
    for at in range(steps + 1):
        late.spread_stage(at)


def finish_kernel(plan, grad_low, first, early, late, grad, *outs):
    d, inner = plan.d, plan.inner
    half = inner // 2
    grad[...] = grad_low[...].astype(F32)

    @pl.when(pl.program_id(0) == 0)
    def _():
        me = lax.axis_index("wa")

        def matrix(name):
            for part, ref in ((plan.first, first), (plan.early, early), (plan.late, late)):
                if name in part.starts:
                    break
            begin, used = part.starts[name]
            parts = []
            for b in range(begin, begin + blocks_of(used)):
                value = ref[b * ROWS_OF : (b + 1) * ROWS_OF].reshape(ROWS_OF * 16, LANES)
                parts.append(value.astype(F32))
            return jnp.concatenate(parts, axis=1)

        def my_half(line, size):
            return jnp.where(me == 0, line[:, 0:size], line[:, size : 2 * size])

        turned = matrix("vec")[0:half].T

        def write(ref, pieces):
            ref[...] = jnp.concatenate(pieces, axis=1).reshape(ref.shape)

        for side, taps in enumerate((ENCODER_TAPS, DECODER_TAPS)):
            tag = "ed"[side]
            first_g, first_b, red_w, red_b, mid_g, mid_b, ker, ker_b, last_g, last_b, exp_w, exp_b = outs[
                12 * side : 12 * side + 12
            ]
            at = 8 * side
            write(first_g, [turned[at : at + 1], turned[at + 1 : at + 2]])
            write(first_b, [turned[at + 2 : at + 3], turned[at + 3 : at + 4]])
            write(mid_g, [turned[at + 4 : at + 5]])
            write(mid_b, [turned[at + 5 : at + 6]])
            write(last_g, [turned[at + 6 : at + 7]])
            write(last_b, [turned[at + 7 : at + 8]])
            value = matrix(tag + "_we")
            exp_w[...] = value[0:half, 0:d]
            write(exp_b, [my_half(value[half : half + 1, 0:d], d // 2)])
            value = matrix(tag + "_k")
            for j in range(taps):
                ker[j] = jnp.concatenate([value[0:half, place] for _, place in tap_pieces(j, taps, inner)], axis=1)
            centre = (ENCODER_SHIFTS if side == 0 else DECODER_SHIFTS).index(0)
            sums = [value[half : half + 1, place] for _, place in tap_pieces(centre, taps, inner)]
            write(ker_b, [my_half(jnp.concatenate(sums, axis=1), half)])
            value = matrix(tag + "_wr")[0:half]
            red_w[...] = value[:, 0:d]
            write(red_b, [value[:, d:].T[0:1]])


def local(n, stream, doc_start, doc_end, cotangent, *weights):
    rows, d = stream.shape[1], stream.shape[2]
    inner = weights[6].shape[1] * 2
    steps = rows // TILE
    x, cot = stream[0].T, cotangent[0].T
    starts, ends = doc_start, doc_end
    weights = [w.T if at % 12 == 2 else w for at, w in enumerate(weights)]
    enc, dec = gather_weights(weights, d, inner)
    wrt_e, kt_e, wet_e, we_e, kb_e, wr_e, g1_e, f1_e, b1_e, g2_e, f2_e, b2_e, g3_e, f3_e, b3_e = enc
    wrt_d, kt_d, wet_d, we_d, kb_d, wr_d, g1_d, f1_d, b1_d, g2_d, f2_d, b2_d, g3_d, f3_d, b3_d = dec

    plan = Plan(d, inner, steps, n)
    blocks = rows // LANES
    per = TILE // LANES

    def spec(a):
        return whole(a.shape)

    def wide(channels, dtype=BF):
        return jax.ShapeDtypeStruct((channels, rows), dtype)

    def fixed(shape, dtype=F32):
        return jax.ShapeDtypeStruct(shape, dtype)

    class Order:
        def __init__(self, first):
            self.tile = lambda i: (i + first) % steps

        def cols(self, channels):
            return pl.BlockSpec((channels, TILE), lambda i: (0, self.tile(i)))

        def before(self, channels):
            return pl.BlockSpec((channels, LANES), lambda i: (0, (per * self.tile(i) + blocks - 1) % blocks))

        def after(self, channels):
            return pl.BlockSpec((channels, LANES), lambda i: (0, (per * self.tile(i) + per) % blocks))

    def head(channels):
        return pl.BlockSpec((channels, LANES), lambda i: (0, 0))

    def tail(channels):
        return pl.BlockSpec((channels, LANES), lambda i: (0, blocks - 1))

    plain, later = Order(0), Order(1)
    d1, i1 = d + AUG, inner + AUG
    norm_wide = [(d1, BF), (d, BF), (d, BF), (8, F32)]
    norm_in = [(i1, BF), (inner, BF), (inner, BF), (8, F32)]
    sem = pltpu.SemaphoreType.DMA
    vmem = pltpu.VMEM

    def outs_of(order, items):
        return [wide(c, t) for c, t in items], [order.cols(c) for c, _ in items]

    shapes, specs = outs_of(plain, norm_wide + norm_in)
    ins = [wrt_e, f1_e, b1_e, f2_e, b2_e]
    h1e, z1e, d1e, r1e, h2e, z2e, d2e, r2e = pl.pallas_call(
        enc_in_kernel,
        grid=(steps,),
        out_shape=shapes,
        in_specs=[plain.cols(d)] + [spec(a) for a in ins],
        out_specs=specs,
        scratch_shapes=[vmem((d, TILE), F32)] + [vmem((inner, HALF), F32)] * 2 + [vmem((d1, HALF), BF)] * 2,
        compiler_params=params(),
        name="encoder_in",
    )(x, *ins)

    shapes, specs = outs_of(later, norm_in + [(d, BF)] + norm_wide + norm_in)
    ins = [kt_e, wet_e, wrt_d, f3_e, b3_e, f1_d, b1_d, f2_d, b2_d]
    h3e, z3e, d3e, r3e, x1, h1d, z1d, d1d, r1d, h2d, z2d, d2d, r2d, edge_d = pl.pallas_call(
        functools.partial(enc_out_kernel, steps),
        grid=(steps,),
        out_shape=shapes + [fixed((i1, LANES), BF)],
        in_specs=[later.cols(1), later.cols(1), later.before(i1), later.cols(i1), later.after(i1)]
        + [head(i1), tail(i1), later.cols(d)]
        + [spec(a) for a in ins],
        out_specs=specs + [whole((i1, LANES))],
        scratch_shapes=[
            vmem((ENCODER_TAPS * inner + AUG, TILE), BF),
            vmem((inner, LANES), BF),
            vmem((inner, LANES), BF),
        ]
        + [vmem((inner, HALF), F32)] * 2
        + [vmem((d, HALF), F32)] * 2
        + [vmem((inner, HALF), F32)] * 2
        + [vmem((i1, HALF), BF)] * 2
        + [vmem((d1, HALF), BF)] * 2
        + [vmem((i1, LANES), BF)] * 4
        + [sem((3,)), sem((3,))],
        compiler_params=params(1),
        name="encoder_out",
    )(starts, ends, h2e, h2e, h2e, h2e, h2e, x, *ins)

    small, large = fixed((inner, LANES)), fixed((d, LANES))
    sums = [fixed((2, plan.first.pieces, 16, LANES), BF), small, small]
    ins = [kt_d, we_d, wet_d, f3_d, b3_d, g3_d]
    out, evr_d, packed_first, dg3_d, db3_d = pl.pallas_call(
        functools.partial(dec_out_kernel, plan),
        grid=(steps,),
        out_shape=[wide(d, F32), wide(inner)] + sums,
        in_specs=[plain.cols(1), plain.cols(1), plain.before(i1), plain.cols(i1), spec(edge_d)]
        + [plain.cols(d), plain.cols(d)]
        + [spec(a) for a in ins],
        out_specs=[plain.cols(d), plain.cols(inner)] + [whole(s.shape) for s in sums],
        scratch_shapes=[
            vmem((i1, d), F32),
            vmem((DECODER_TAPS * inner + AUG, TILE), BF),
            vmem((inner, LANES), BF),
            vmem((inner, HALF), F32),
            vmem((inner, HALF), F32),
            vmem((i1, TILE), BF),
            vmem((inner, TILE), BF),
            vmem((inner, TILE), BF),
            vmem((8, TILE), F32),
        ]
        + [vmem((inner, HALF), F32)] * 2
        + [vmem((inner, HALF), BF)] * 2
        + [vmem((i1, HALF), BF)] * 2,
        compiler_params=params(),
        name="decoder_out",
    )(starts, ends, h2d, h2d, edge_d, cot, x1, *ins)

    shapes, specs = outs_of(plain, [(d, BF), (inner, BF)])
    early = fixed((2, plan.early.pieces, 16, LANES), BF)
    first = fixed((plan.first.pieces, 16, LANES), BF)
    sums = [small, small, large, large, small, small]
    ins = [kb_d, wr_d, we_e, g2_d, g1_d, g3_e]
    stash = [h2d, z2d, d2d, r2d, h1d, z1d, d1d, r1d, cot, h3e, z3e, d3e, r3e]
    ey, evr_e, packed, first_share, dg2_d, db2_d, dg1_d, db1_d, dg3_e, db3_e = pl.pallas_call(
        functools.partial(dec_back_kernel, plan),
        grid=(steps,),
        out_shape=shapes + [early, first] + sums,
        in_specs=[plain.cols(1), plain.cols(1), plain.cols(inner), plain.after(inner), head(inner)]
        + [spec(a) for a in ins]
        + [plain.cols(a.shape[0]) for a in stash]
        + [spec(packed_first)],
        out_specs=specs + [whole(early.shape), whole(first.shape)] + [whole(s.shape) for s in sums],
        scratch_shapes=[
            vmem((i1, DECODER_TAPS * inner), F32),
            vmem((inner, d1), F32),
            vmem((i1, d), F32),
            vmem((DECODER_TAPS * inner, TILE), BF),
            vmem((inner, LANES), BF),
        ]
        + [vmem((inner, HALF), F32)] * 4
        + [vmem((d, HALF), F32)] * 2
        + [vmem((inner, TILE), BF)]
        + [vmem((inner, HALF), BF)] * 2
        + [vmem((d, HALF), BF)] * 4
        + [vmem((inner, HALF), BF)] * 2
        + [vmem((inner, LANES), BF), sem((1,)), sem((1,))]
        + Summing.scratch(plan.first),
        compiler_params=params(2),
        name="decoder_back",
    )(starts, ends, evr_d, evr_d, evr_d, *ins, *stash, packed_first)

    late = fixed((2, plan.late.pieces, 16, LANES), BF)
    early_sum = fixed((plan.early.pieces, 16, LANES), BF)
    ins = [kb_e, wr_e, g2_e, g1_e]
    stash = [h2e, z2e, d2e, r2e, h1e, z1e, d1e, r1e, ey]
    vecs = [dg3_e, db3_e, dg1_d, db1_d, dg2_d, db2_d, dg3_d, db3_d]
    grad_low, packed_late, summed, first_whole = pl.pallas_call(
        functools.partial(enc_back_kernel, plan),
        grid=(steps,),
        out_shape=[wide(d), late, early_sum, first],
        in_specs=[later.cols(1), later.cols(1), later.before(inner), later.cols(inner), later.after(inner)]
        + [head(inner), tail(inner)]
        + [spec(a) for a in ins]
        + [later.cols(a.shape[0]) for a in stash]
        + [whole(early.shape), whole(first.shape)]
        + [spec(a) for a in vecs],
        out_specs=[later.cols(d), whole(late.shape), whole(early_sum.shape), whole(first.shape)],
        scratch_shapes=[
            vmem((i1, ENCODER_TAPS * inner), F32),
            vmem((inner, d1), F32),
            vmem((inner, LANES), F32),
            vmem((inner, LANES), F32),
            vmem((d, LANES), F32),
            vmem((d, LANES), F32),
            vmem((ENCODER_TAPS * inner, TILE), BF),
            vmem((inner, LANES), BF),
            vmem((inner, LANES), BF),
        ]
        + [vmem((inner, HALF), F32)] * 2
        + [vmem((d, HALF), F32)] * 2
        + [vmem((inner, TILE), BF)]
        + [vmem((inner, HALF), BF)] * 2
        + [vmem((d, HALF), BF)] * 2
        + [vmem((inner, HALF), BF)] * 2
        + [vmem((inner, LANES), BF)] * 2
        + [sem((2,)), sem((2,)), vmem(first.shape, BF)]
        + Summing.spread_scratch(plan.first)
        + Summing.scratch(plan.early),
        compiler_params=params(3),
        name="encoder_back",
    )(starts, ends, evr_e, evr_e, evr_e, evr_e, evr_e, *ins, *stash, packed, first_share, *vecs)

    vm = pl.BlockSpec(memory_space=pltpu.VMEM)
    early_whole, late_whole = pl.pallas_call(
        functools.partial(sum_kernel, plan),
        out_shape=[early_sum, fixed((plan.late.pieces, 16, LANES), BF)],
        in_specs=[vm, vm],
        out_specs=[vm, vm],
        scratch_shapes=Summing.scratch(plan.late)
        + Summing.spread_scratch(plan.late)
        + Summing.spread_scratch(plan.early),
        compiler_params=params(4),
        name="sum_gradients",
    )(packed_late, summed)

    grad, *shares = pl.pallas_call(
        functools.partial(finish_kernel, plan),
        grid=(steps,),
        out_shape=[wide(d, F32)] + [fixed(w.shape) for w in weights],
        in_specs=[plain.cols(d), whole(first_whole.shape), whole(early_whole.shape), whole(late_whole.shape)],
        out_specs=[plain.cols(d)] + [whole(w.shape) for w in weights],
        compiler_params=params(),
        name="finish",
    )(grad_low, first_whole, early_whole, late_whole)
    shares = [w.T if at % 12 == 2 else w for at, w in enumerate(shares)]
    return (out.T[None], grad.T[None], *shares)


def solution(mesh):
    rows = P("wa", "seq", None)
    block = (
        P("wa"), P("wa"), P(None, "wa"), P("wa"), P("wa"), P("wa"),
        P(None, "wa", None), P("wa"), P("wa"), P("wa"), P("wa", None), P("wa"),
    )
    return jax.shard_map(
        functools.partial(local, mesh.shape["seq"]),
        mesh=mesh,
        in_specs=(rows, P("wa", "seq"), P("wa", "seq"), rows, *block, *block),
        out_specs=(rows, rows, *block, *block),
        check_vma=False,
    )
```

```python
import functools

import jax
import jax.numpy as jnp
from jax import lax
from jax.experimental import pallas as pl
from jax.experimental.pallas import tpu as pltpu
from jax.sharding import PartitionSpec as P

ENCODER_TAPS = 5
ENCODER_DILATION = 8
DECODER_TAPS = 3
DECODER_DILATION = 16
EPS = 1e-05

MESH = pl.DeviceIdType.MESH
BF = jnp.bfloat16
F32 = jnp.float32
LANES = 128
TILE = 512
HALF = 256
AUG = 16
VMEM_LIMIT = 56 * 1024 * 1024
GELU_1 = 2.0 * 0.7978845608028654
GELU_3 = 8.0 * 0.7978845608028654 * 0.044715

ENCODER_SHIFTS = tuple(ENCODER_DILATION * (j - ENCODER_TAPS // 2) for j in range(ENCODER_TAPS))
DECODER_SHIFTS = tuple(-DECODER_DILATION * (DECODER_TAPS - 1 - j) for j in range(DECODER_TAPS))


def params(collective=None):
    if collective is None:
        return pltpu.CompilerParams(vmem_limit_bytes=VMEM_LIMIT)
    return pltpu.CompilerParams(
        vmem_limit_bytes=VMEM_LIMIT, collective_id=collective, has_side_effects=True
    )


def whole(shape):
    return pl.BlockSpec(shape, lambda *_: (0,) * len(shape))


def nt_dot(left, right):
    return lax.dot_general(left, right, (((1,), (1,)), ((), ())), preferred_element_type=F32)


def nn_dot(left, right):
    return jnp.dot(left, right, preferred_element_type=F32)


def product(out, left, right):
    rows = out.shape[0]
    middle = (rows // 2 + 15) // 16 * 16
    for a, b in ((0, middle), (middle, rows)):
        out[a:b, :] = nn_dot(left[a:b, :], right)


def lanes_of(column, width):
    return jnp.concatenate([column] * (width // LANES), axis=1)


def fold(value):
    total = value[:, :LANES]
    for at in range(LANES, value.shape[1], LANES):
        total = total + value[:, at : at + LANES]
    return total


def weights_kernel(dims, *refs):
    d, inner, taps = dims
    n_in = 24
    ins, refs = refs[:n_in], refs[n_in:]
    results, refs = refs[:30], refs[30:]
    outs, refs = refs[:30], refs[30:]
    (small_own, small_got, k_own0, k_own1, e_own0, e_own1, r_own0, r_own1, *rest) = refs
    (r_got0, r_got1, k_got0, k_got1, e_got0, e_got1, k_all, send, recv, store) = rest
    me = lax.axis_index("wa")
    other = 1 - me
    barrier = pltpu.get_barrier_semaphore()
    pl.semaphore_signal(barrier, inc=1, device_id={"wa": other}, device_id_type=MESH)
    pl.semaphore_wait(barrier, 1)

    half = inner // 2
    pad = k_own0.shape[1]
    small_own[...] = jnp.zeros_like(small_own)
    small_at = []
    for side in range(2):
        for at in (0, 1, 3, 4, 5, 7, 8, 9, 11):
            small_at.append(12 * side + at)
    for row, at in enumerate(small_at):
        n = ins[at].shape[0]
        small_own[row : row + 1, 0:n] = ins[at][...].astype(F32).reshape(1, n)
    owns, gots = [], []
    for side, (k_own, e_own, r_own) in enumerate(((k_own0, e_own0, r_own0), (k_own1, e_own1, r_own1))):
        base = 12 * side
        k_own[:, half - 8 : pad, :] = jnp.zeros((taps[side], pad - half + 8, inner), BF)
        k_own[:, 0:half, :] = ins[base + 6][...]
        e_own[half - 8 : pad, :] = jnp.zeros((pad - half + 8, d), BF)
        e_own[0:half, :] = ins[base + 10][...]
        r_own[half - 8 : pad, :] = jnp.zeros((pad - half + 8, d), BF)
        r_own[0:half, :] = ins[base + 2][...]
        owns += [r_own, k_own, e_own]
    owns.append(small_own)
    gots = [r_got0, k_got0, e_got0, r_got1, k_got1, e_got1, small_got]
    copies = []
    pairs = list(zip(owns, gots))
    for at in (6, 0, 2, 1, 3, 5, 4):
        own, got = pairs[at]
        copies.append(
            pltpu.make_async_remote_copy(
                src_ref=own,
                dst_ref=got,
                send_sem=send.at[at],
                recv_sem=recv.at[at],
                device_id={"wa": other},
                device_id_type=MESH,
            )
        )
        copies[-1].start()
    arrival = dict(zip((6, 0, 2, 1, 3, 5, 4), copies))
    stores = []

    def keep(at):
        stores.append(pltpu.make_async_copy(outs[at], results[at], store.at[at]))
        stores[-1].start()

    first_core = me == 0
    square = (HALF, HALF)
    unit = lax.broadcasted_iota(jnp.int32, square, 0) == lax.broadcasted_iota(jnp.int32, square, 1)
    unit = jnp.where(unit, 1.0, 0.0).astype(BF)

    def turn(out, columns, count, width=None):
        for a in range(0, count, HALF):
            b = min(a + HALF, count)
            piece = nt_dot(unit[0 : b - a, 0 : b - a], columns(a, b)).astype(BF)
            if width is None:
                out[a:b, :] = piece
            else:
                out[a:b, 0:width] = piece

    def ordered(own, got):
        own, got = own.astype(F32), got.astype(F32)
        return jnp.where(first_core, own, got), jnp.where(first_core, got, own)

    arrival[6].wait()
    small0, small1 = ordered(small_own[...], small_got[...])

    def column(row, n):
        line = jnp.concatenate([small0[row : row + 1, 0 : n // 2], small1[row : row + 1, 0 : n // 2]], axis=1)
        return jnp.broadcast_to(line, (LANES, n)).T

    def bias_columns(value):
        where = lax.broadcasted_iota(jnp.int32, (value.shape[0], AUG), 1) == 0
        return jnp.where(where, value[:, :AUG], 0.0).astype(BF)

    for side in range(2):
        o = outs[15 * side : 15 * side + 15]
        wrt, kt, wet, we, kb, wr, *vectors = o
        base = 9 * side
        for at, (row, n) in enumerate(((0, d), (3, inner), (6, inner))):
            gain, half_gain, half_bias = vectors[3 * at : 3 * at + 3]
            gain[...] = column(base + row, n)
            half_gain[...] = gain[...] * 0.5
            half_bias[...] = column(base + row + 1, n) * 0.5
        n = taps[side]
        first = 15 * side
        for at in range(6, 15):
            keep(first + at)
        arrival[3 * side].wait()
        r0, r1 = ordered(owns[3 * side][0:half, :], gots[3 * side][0:half, :])
        wrt[:, 0:d] = jnp.concatenate([r0, r1], axis=0).astype(BF)
        wrt[:, d : d + AUG] = bias_columns(column(base + 2, inner))
        keep(first)
        turn(wr, lambda a, b: wrt[:, a:b], d)
        keep(first + 5)
        arrival[3 * side + 2].wait()
        e0, e1 = ordered(owns[3 * side + 2][0:half, :], gots[3 * side + 2][0:half, :])
        we[...] = jnp.concatenate([e0, e1], axis=0).astype(BF)
        keep(first + 3)
        turn(wet, lambda a, b: we[:, a:b], d, inner)
        wet[:, inner : inner + AUG] = bias_columns(column(base + 8, d))
        keep(first + 2)
        arrival[3 * side + 1].wait()
        for j in range(n):
            k0, k1 = ordered(owns[3 * side + 1][j, 0:half, :], gots[3 * side + 1][j, 0:half, :])
            k = jnp.concatenate([k0, k1], axis=0).astype(BF)
            for channels, place in tap_pieces(j, n, inner):
                kb[:, place] = k[:, channels]
                k_all[place, :] = k[channels, :]
        keep(first + 4)
        turn(kt, lambda a, b: k_all[0 : n * inner, a:b], inner, n * inner)
        kt[:, n * inner : n * inner + AUG] = bias_columns(column(base + 5, inner))
        keep(first + 1)
    for copy in stores:
        copy.wait()


def gather_weights(args, d, inner):
    taps = (ENCODER_TAPS, DECODER_TAPS)
    half = inner // 2
    pad = -(-half // 16) * 16
    shapes = []
    for n in taps:
        shapes += [
            ((inner, d + AUG), BF),
            ((inner, n * inner + AUG), BF),
            ((d, inner + AUG), BF),
            ((inner, d), BF),
            ((inner, n * inner), BF),
            ((d, inner), BF),
        ]
        for c in (d, inner, inner):
            shapes += [((c, LANES), F32)] * 3
    vm = pl.BlockSpec(memory_space=pltpu.VMEM)
    small = pltpu.VMEM((24, 512), F32)
    kk = [pltpu.VMEM((n, pad, inner), BF) for n in taps]
    ee = [pltpu.VMEM((pad, d), BF)] * 2
    outs = pl.pallas_call(
        functools.partial(weights_kernel, (d, inner, taps)),
        out_shape=[jax.ShapeDtypeStruct(*s) for s in shapes],
        in_specs=[vm] * 24,
        out_specs=[pl.BlockSpec(memory_space=pl.ANY)] * 30,
        scratch_shapes=[pltpu.VMEM(*shape) for shape in shapes]
        + [small, small, *kk, *ee, *ee, *ee, *kk, *ee]
        + [pltpu.VMEM((taps[0] * inner, inner), BF)]
        + [pltpu.SemaphoreType.DMA((7,)), pltpu.SemaphoreType.DMA((7,)), pltpu.SemaphoreType.DMA((30,))],
        compiler_params=params(0),
        name="gather_weights",
    )(*args)
    return outs[:15], outs[15:]


def pacing(thunks, slots):
    state = [0, 0]
    thunks = list(thunks)

    def between():
        while state[1] < len(thunks) and state[0] * len(thunks) >= state[1] * slots:
            thunks[state[1]]()
            state[1] += 1
        state[0] += 1

    return between


def add_product(total, left, right):
    def piece(at, stop):
        total[:, at:stop] += nt_dot(left[...], right[at:stop, :])

    columns = right.shape[0]
    return [functools.partial(piece, at, min(at + HALF, columns)) for at in range(0, columns, HALF)]


def norm_forward(src, lanes, channels, gain, bias, h_out, z_out, d_out, r_out, keep=None, fill=(), at=None, h_copy=None):
    width = lanes.stop - lanes.start
    between = pacing(fill, 3 * (channels // 16))
    total = [jnp.zeros((8, width), F32) for _ in range(4)]
    for c in range(0, channels, 16):
        between()
        x = src[c : c + 16, at or lanes].astype(F32)
        if keep is not None:
            keep[c : c + 16, at or lanes] = x
        k = (c // 8) % 4
        total[k] = total[k] + x[0:8]
        total[k + 1] = total[k + 1] + x[8:16]
    mean = jnp.sum((total[0] + total[1]) + (total[2] + total[3]), axis=0, keepdims=True) * (1.0 / channels)
    wide = jnp.broadcast_to(mean, (16, width))
    values = src if keep is None else keep
    total = [jnp.zeros((8, width), F32) for _ in range(4)]
    for c in range(0, channels, 16):
        between()
        centre = values[c : c + 16, at or lanes] - wide
        square = centre * centre
        k = (c // 8) % 4
        total[k] = total[k] + square[0:8]
        total[k + 1] = total[k + 1] + square[8:16]
    spread = jnp.sum((total[0] + total[1]) + (total[2] + total[3]), axis=0, keepdims=True) * (1.0 / channels)
    r = lax.rsqrt(spread + EPS)
    if r_out is not None:
        r_out[:, lanes] = jnp.broadcast_to(r, (8, width))
    rw = jnp.broadcast_to(r, (16, width))
    mw = jnp.broadcast_to(mean * r, (16, width))
    one, point = BF(1.0), BF(0.5)
    for c in range(0, channels, 16):
        between()
        rows = slice(c, c + 16)
        z = values[rows, at or lanes] * rw - mw
        half = (z * lanes_of(gain[rows, :], width) + lanes_of(bias[rows, :], width)).astype(BF)
        sq = half * half
        t = jnp.tanh(half * (sq * BF(GELU_3) + BF(GELU_1)))
        up = one + t
        h_out[rows, lanes] = half * up
        if h_copy is not None:
            h_copy[rows, :] = half * up
        d_out[rows, lanes] = up * (point + half * (sq * BF(1.5 * GELU_3) + BF(0.5 * GELU_1)) * (one - t))
        z_out[rows, lanes] = z.astype(BF)


def norm_backward(grad, lanes, channels, gain, z_in, d_in, r_in, gain_sum, bias_sum, keep, emit, fill=(), at=None):
    width = lanes.stop - lanes.start
    between = pacing(fill, 2 * (channels // 16))
    one = [jnp.zeros((8, width), F32) for _ in range(2)]
    two = [jnp.zeros((8, width), F32) for _ in range(2)]
    r = r_in[0:1, lanes]
    rw = jnp.broadcast_to(r, (16, width))
    for c in range(0, channels, 16):
        between()
        rows = slice(c, c + 16)
        da = grad[rows, at or lanes] * d_in[rows, lanes].astype(F32)
        p = da * z_in[rows, lanes].astype(F32)
        bias_sum[rows, :] += fold(da)
        gain_sum[rows, :] += fold(p)
        wide = lanes_of(gain[rows, :], width)
        dz = da * wide
        q = p * wide
        keep[rows, at or lanes] = (dz * rw).astype(BF)
        for k in range(2):
            one[k] = one[k] + dz[8 * k : 8 * k + 8]
            two[k] = two[k] + q[8 * k : 8 * k + 8]
    scale = r * (1.0 / channels)
    m1 = jnp.broadcast_to(jnp.sum(one[0] + one[1], axis=0, keepdims=True) * scale, (16, width)).astype(BF)
    m2 = jnp.broadcast_to(jnp.sum(two[0] + two[1], axis=0, keepdims=True) * scale, (16, width)).astype(BF)
    for c in range(0, channels, 16):
        between()
        rows = slice(c, c + 16)
        emit(rows, keep[rows, at or lanes] - (z_in[rows, lanes] * m2 + m1))


def tap_mask(starts, ends, first, shift):
    place = first + shift + lax.broadcasted_iota(jnp.int32, (8, TILE), 1)
    usable = (place >= jnp.broadcast_to(starts[...], (8, TILE))) & (place < jnp.broadcast_to(ends[...], (8, TILE)))
    one = jnp.where(usable, 1.0, 0.0)
    return jnp.concatenate([one, one], axis=0).astype(BF)


def tap_row(j, c, taps, inner):
    aligned = inner // LANES * LANES
    return j * aligned + c if c < aligned else taps * aligned + j * (inner - aligned) + c - aligned


def tap_pieces(j, taps, inner):
    aligned = inner // LANES * LANES
    for a, b in ((0, aligned), (aligned, inner)):
        at = tap_row(j, a, taps, inner)
        yield slice(a, b), slice(at, at + b - a)


def stack_taps(stack, shifts, before, main, after, starts, ends, first, inner):
    for j, shift in enumerate(shifts):
        if not shift:
            for channels, place in tap_pieces(j, len(shifts), inner):
                stack[place, :] = main[channels, :]
            continue
        mask = tap_mask(starts, ends, first, shift)
        for c in range(0, inner, 16):
            rows = slice(c, c + 16)
            if shift < 0:
                span = jnp.concatenate([before[rows, :], main[rows, :]], axis=1)
                span = pltpu.roll(span, -shift, 1)[:, LANES:]
            else:
                span = jnp.concatenate([main[rows, :], after[rows, :]], axis=1)
                span = pltpu.roll(span, TILE + LANES - shift, 1)[:, :TILE]
            at = tap_row(j, c, len(shifts), inner)
            stack[at : at + 16, :] = span * mask


def ones_rows(width):
    where = lax.broadcasted_iota(jnp.int32, (AUG, width), 0) == 0
    return jnp.where(where, 1.0, 0.0).astype(BF)


def neighbours():
    me = lax.axis_index("seq")
    n = lax.axis_size("seq")
    return lax.rem(me + n - 1, n), lax.rem(me + 1, n)


def greet(others):
    barrier = pltpu.get_barrier_semaphore()
    for device in others:
        pl.semaphore_signal(barrier, inc=1, device_id=device, device_id_type=MESH)
    pl.semaphore_wait(barrier, len(others))


def send_copy(src, dst, send_sem, recv_sem, device):
    return pltpu.make_async_remote_copy(
        src_ref=src, dst_ref=dst, send_sem=send_sem, recv_sem=recv_sem, device_id=device, device_id_type=MESH
    )


def later_tile(step, steps):
    return lax.rem(step + 1, steps)


def first_place(tile, steps):
    return lax.axis_index("seq") * (steps * TILE) + tile * TILE


CHAINS = (slice(0, HALF), slice(HALF, TILE))
EVERY = slice(0, HALF)


def enc_in_kernel(x, wrt, g1, b1, g2, b2, h1, z1, d1, r1, h2, z2, d2, r2, xt, u0, u1, h_wide0, h_wide1):
    d, inner = x.shape[0], wrt.shape[0]
    h1[d : d + AUG, :] = ones_rows(TILE)
    h2[inner : inner + AUG, :] = ones_rows(TILE)
    u, h_wide = (u0, u1), (h_wide0, h_wide1)
    for k in range(2):
        h_wide[k][d : d + AUG, :] = ones_rows(HALF)
        norm_forward(x, CHAINS[k], d, g1, b1, h1, z1, d1, r1, xt, h_copy=h_wide[k])
        u[k][...] = nn_dot(wrt[...], h_wide[k][...])
    for k in range(2):
        norm_forward(u[k], CHAINS[k], inner, g2, b2, h2, z2, d2, r2, at=EVERY)


def choose_edge(window, block, edge, at_end):
    window[...] = block[0 : window.shape[0], :]

    @pl.when(at_end)
    def _():
        window[...] = edge[0 : window.shape[0], :]


def trade_edges(step, steps, head, tail, got_l, got_r, send, recv, others=()):
    left, right = neighbours()
    to_left = send_copy(head, got_r, send.at[0], recv.at[0], {"seq": left})
    to_right = send_copy(tail, got_l, send.at[1], recv.at[1], {"seq": right})

    @pl.when(step == 0)
    def _():
        greet([{"seq": left}, {"seq": right}, *others])
        to_left.start()
        to_right.start()

    @pl.when(step == steps - 2)
    def _():
        to_left.wait()
        to_right.wait()


def enc_out_kernel(
    steps, starts, ends, before, main, after, head, tail, xt, kt, wet, wrt, g3, b3, g1, b1, g2, b2,
    h3, z3, d3, r3, x1, h1, z1, d1, r1, h2, z2, d2, r2, edge_o,
    stack, win_b, win_a, v0, v1, y0, y1, u0, u1, h_in0, h_in1, h_wide0, h_wide1, got_l, got_r, own, got, send, recv,
):
    step = pl.program_id(0)
    d, inner = xt.shape[0], v0.shape[0]
    v, y, u, h_in, h_wide = (v0, v1), (y0, y1), (u0, u1), (h_in0, h_in1), (h_wide0, h_wide1)
    trade_edges(step, steps, head, tail, got_l, got_r, send, recv)
    choose_edge(win_b, before, got_l, step == steps - 1)
    choose_edge(win_a, after, got_r, step == steps - 2)
    stack_taps(stack, ENCODER_SHIFTS, win_b, main, win_a, starts, ends, first_place(later_tile(step, steps), steps), inner)
    stack[len(ENCODER_SHIFTS) * inner :, :] = ones_rows(TILE)
    h3[inner : inner + AUG, :] = ones_rows(TILE)
    h1[d : d + AUG, :] = ones_rows(TILE)
    h2[inner : inner + AUG, :] = ones_rows(TILE)
    one, two = CHAINS

    def make_v(k):
        product(v[k], kt, stack[:, CHAINS[k]])

    def make_y(k):
        y[k][...] = nn_dot(wet[...], h_in[k][...]) + xt[:, CHAINS[k]].astype(F32)

    def make_u(k):
        u[k][...] = nn_dot(wrt[...], h_wide[k][...])

    def norm_last(k):
        norm_forward(v[k], CHAINS[k], inner, g3, b3, h3, z3, d3, r3, at=EVERY, h_copy=h_in[k])

    def norm_first(k):
        for c in range(0, d, 16):
            x1[c : c + 16, CHAINS[k]] = y[k][c : c + 16, :].astype(BF)
        norm_forward(y[k], CHAINS[k], d, g1, b1, h1, z1, d1, r1, at=EVERY, h_copy=h_wide[k])

    def norm_mid(k):
        norm_forward(u[k], CHAINS[k], inner, g2, b2, h2, z2, d2, r2, at=EVERY)

    for k in range(2):
        h_in[k][inner : inner + AUG, :] = ones_rows(HALF)
        h_wide[k][d : d + AUG, :] = ones_rows(HALF)
    make_v(0)
    make_v(1)
    norm_last(0)
    make_y(0)
    norm_last(1)
    make_y(1)
    norm_first(0)
    make_u(0)
    norm_first(1)
    make_u(1)
    norm_mid(0)
    norm_mid(1)

    def give():
        return send_copy(own, got, send.at[2], recv.at[2], {"seq": neighbours()[1]})

    @pl.when(step == steps - 2)
    def _():
        own[...] = h2[:, TILE - LANES : TILE]
        give().start()

    @pl.when(step == steps - 1)
    def _():
        give().wait()
        edge_o[...] = got[...]


def dec_out_kernel(
    plan, starts, ends, before, main, e_l, cot_t, x1, kt, we, wet, f3, b3, g3,
    out, evr, packed, dg3, db3,
    dwe, stack, win_b, v0, v1, h3, z3, d3, r3, g0, g1, kept0, kept1, h_in0, h_in1,
):
    steps = plan.steps
    step = pl.program_id(0)
    inner = v0.shape[0]
    v, g, kept, h_in = (v0, v1), (g0, g1), (kept0, kept1), (h_in0, h_in1)

    @pl.when(step == 0)
    def _():
        dwe[...] = jnp.zeros_like(dwe)
        dg3[...] = jnp.zeros_like(dg3)
        db3[...] = jnp.zeros_like(db3)

    choose_edge(win_b, before, e_l, step == 0)
    stack_taps(stack, DECODER_SHIFTS, win_b, main, None, starts, ends, first_place(step, steps), inner)
    stack[len(DECODER_SHIFTS) * inner :, :] = ones_rows(TILE)
    h3[inner : inner + AUG, :] = ones_rows(TILE)

    def make_out(k):
        out[:, CHAINS[k]] = nn_dot(wet[...], h_in[k][...]) + x1[:, CHAINS[k]].astype(F32)

    def back(k, fill):
        def emit(rows, value):
            evr[rows, CHAINS[k]] = value

        norm_backward(g[k], CHAINS[k], inner, g3, z3, d3, r3, dg3, db3, kept[k], emit, fill, EVERY)

    for k in range(2):
        h_in[k][inner : inner + AUG, :] = ones_rows(HALF)
        g[k][...] = nn_dot(we[...], cot_t[:, CHAINS[k]])
    for k in range(2):
        product(v[k], kt, stack[:, CHAINS[k]])
    for k in range(2):
        norm_forward(v[k], CHAINS[k], inner, f3, b3, h3, z3, d3, r3, at=EVERY, h_copy=h_in[k])
    products = add_product(dwe, h3, cot_t)
    back(0, [lambda: make_out(0), *products[:2]])
    back(1, [lambda: make_out(1), *products[2:]])

    @pl.when(step == steps - 1)
    def _():
        pack_gradients(packed, plan, ((dwe, dwe.shape[1]),), ())


def dec_back_kernel(
    plan, starts, ends, main, after, head, kb, wr, we, g2, g1, g3,
    h2, z2, d2, r2, h1, z1, d1, r1, cot_t, h3, z3, d3, r3, given,
    ey, evr, packed, first, dg2, db2, dg1, db1, dg3, db3,
    dk, dwrt, dwe, stack, win_a, ga0, ga1, gb0, gb1, big0, big1, eur, eur0, eur1, ey0, ey1,
    kept0, kept1, keeps0, keeps1, got, send, recv, *traffic,
):
    steps = plan.steps
    sum_over = Summing(plan.first, given, first, traffic)
    k = sum_over.steps
    due = [0, 1] + [2 + (i * (steps - 3)) // max(1, k - 1) for i in range(k)]
    hook = hooks(steps, [(place, functools.partial(sum_over.reduce_stage, at)) for at, place in enumerate(due)])
    step = pl.program_id(0)
    d, inner = cot_t.shape[0], ga0.shape[0]
    ga, gb, big, eurs, eys = (ga0, ga1), (gb0, gb1), (big0, big1), (eur0, eur1), (ey0, ey1)
    kept, keeps = (kept0, kept1), (keeps0, keeps1)

    @pl.when(step == 0)
    def _():
        for ref in (dk, dwrt, dwe, dg2, db2, dg1, db1, dg3, db3):
            ref[...] = jnp.zeros_like(ref)

    left, right = neighbours()
    to_left = send_copy(head, got, send.at[0], recv.at[0], {"seq": left})

    @pl.when(step == 0)
    def _():
        greet([{"seq": left}, {"seq": right}, *sum_over.partners()])
        to_left.start()

    @pl.when(step == steps - 1)
    def _():
        to_left.wait()

    hook(False)
    choose_edge(win_a, after, got, step == steps - 1)
    back = tuple(-s for s in DECODER_SHIFTS)
    stack_taps(stack, back, None, main, win_a, starts, ends, first_place(step, steps), inner)

    def back2(k, fill):
        def emit(rows, value):
            eur[rows, CHAINS[k]] = value
            eurs[k][rows, :] = value

        norm_backward(ga[k], CHAINS[k], inner, g2, z2, d2, r2, dg2, db2, keeps[k], emit, fill, EVERY)

    def back1(k, fill):
        def emit(rows, value):
            total = value + cot_t[rows, CHAINS[k]]
            ey[rows, CHAINS[k]] = total
            eys[k][rows, :] = total

        norm_backward(big[k], CHAINS[k], d, g1, z1, d1, r1, dg1, db1, kept[k], emit, fill, EVERY)

    def back3(k, fill):
        def emit(rows, value):
            evr[rows, CHAINS[k]] = value

        norm_backward(gb[k], CHAINS[k], inner, g3, z3, d3, r3, dg3, db3, keeps[k], emit, fill, EVERY)

    for k in range(2):
        product(ga[k], kb, stack[:, CHAINS[k]])
    by_k = add_product(dk, h2, stack)
    back2(0, by_k[:2])
    big[0][...] = nn_dot(wr[...], eur0[...])
    back2(1, by_k[2:])
    big[1][...] = nn_dot(wr[...], eur1[...])
    by_r = add_product(dwrt, eur, h1)
    back1(0, by_r[:2])
    gb[0][...] = nn_dot(we[...], ey0[...])
    back1(1, by_r[2:])
    gb[1][...] = nn_dot(we[...], ey1[...])
    by_e = add_product(dwe, h3, ey)
    back3(0, by_e[:2])
    back3(1, by_e[2:])

    @pl.when(step == steps - 1)
    def _():
        pack_gradients(packed, plan, ((dk, dk.shape[1]), (dwrt, d + AUG), (dwe, d)), ())

    hook(True)


def enc_back_kernel(
    plan, starts, ends, before, main, after, head, tail, kb, wr, g2, g1,
    h2, z2, d2, r2, h1, z1, d1, r1, ey, given, first_share, *rest,
):
    vecs, rest = rest[:8], rest[8:]
    (
        grad, packed, summed, first_whole,
        dk, dwrt, dg2, db2, dg1, db1,
        stack, win_b, win_a, ga0, ga1, big0, big1, eur, eur0, eur1, kept0, kept1, keeps0, keeps1,
        got_l, got_r, send, recv, result, first_up,
    ), traffic = rest[:30], rest[30:]
    steps = plan.steps
    step = pl.program_id(0)
    d, inner = ey.shape[0], ga0.shape[0]
    ga, big, eurs = (ga0, ga1), (big0, big1), (eur0, eur1)
    kept, keeps = (kept0, kept1), (keeps0, keeps1)

    @pl.when(step == 0)
    def _():
        for ref in (dk, dwrt, dg2, db2, dg1, db1):
            ref[...] = jnp.zeros_like(ref)

    sum_over = Summing(plan.early, given, summed, traffic)
    trade_edges(step, steps, head, tail, got_l, got_r, send, recv, sum_over.partners())

    k = sum_over.steps
    due = [0, 1] + [3 + (i * (steps - 3)) // max(1, k - 1) for i in range(k)]
    actions = [(place, functools.partial(sum_over.reduce_stage, at)) for at, place in enumerate(due)]
    first = Summing(plan.first, None, result, (None,) * 6 + (first_up,))

    def begin():
        first.take_share(first_share)
        first.spread_stage(0)

    actions.append((0, begin))
    actions += [(1 + (steps - 2) * (at + 1) // k, functools.partial(first.spread_stage, at + 1)) for at in range(k)]
    hook = hooks(steps, actions)

    hook(False)
    choose_edge(win_b, before, got_l, step == steps - 1)
    choose_edge(win_a, after, got_r, step == steps - 2)
    back = tuple(-s for s in ENCODER_SHIFTS)
    stack_taps(stack, back, win_b, main, win_a, starts, ends, first_place(later_tile(step, steps), steps), inner)

    def back2(k, fill):
        def emit(rows, value):
            eur[rows, CHAINS[k]] = value
            eurs[k][rows, :] = value

        norm_backward(ga[k], CHAINS[k], inner, g2, z2, d2, r2, dg2, db2, keeps[k], emit, fill, EVERY)

    def back1(k, fill):
        def emit(rows, value):
            grad[rows, CHAINS[k]] = value + ey[rows, CHAINS[k]]

        norm_backward(big[k], CHAINS[k], d, g1, z1, d1, r1, dg1, db1, kept[k], emit, fill, EVERY)

    for k in range(2):
        product(ga[k], kb, stack[:, CHAINS[k]])
    by_k = add_product(dk, h2, stack)
    back2(0, by_k[:2])
    big[0][...] = nn_dot(wr[...], eur0[...])
    back2(1, by_k[2:4])
    big[1][...] = nn_dot(wr[...], eur1[...])
    by_r = add_product(dwrt, eur, h1)
    back1(0, by_k[4:])
    back1(1, by_r)

    @pl.when(step == steps - 1)
    def _():
        in_chunks(plan.first.pieces, lambda at, count: copy_pieces(first_whole, result, at, count))
        sums = (dg1, db1, dg2, db2, *vecs)
        pack_gradients(packed, plan, ((dk, dk.shape[1]), (dwrt, d + AUG)), sums)

    hook(True)


LARGE = (2, 6, 10, 14, 18, 22)
ROWS_OF = 13


def blocks_of(used):
    return -(-used // LANES)


class Part:
    def __init__(self, sections, vectors, streams, n):
        self.starts, at = {}, 0
        for name, used in sections:
            self.starts[name] = (at, used)
            at += blocks_of(used)
        if vectors:
            self.starts["vec"] = (at, LANES)
            at += 1
        self.filled = at * ROWS_OF
        self.streams = streams
        self.per = -(-self.filled // (streams * n)) * n
        self.pieces = streams * self.per
        self.n = n
        self.rounds, base = [], 1
        while base < n:
            radix = 4 if n // base == 4 else 2
            self.rounds.append((base, radix))
            base *= radix


class Plan:
    def __init__(self, d, inner, steps, n):
        self.d, self.inner, self.steps, self.n = d, inner, steps, n
        self.first = Part((("d_we", d),), False, 2, n)
        early = (("d_k", DECODER_TAPS * inner), ("d_wr", d + AUG), ("e_we", d))
        self.early = Part(early, False, 2, n)
        self.late = Part((("e_k", ENCODER_TAPS * inner), ("e_wr", d + AUG)), True, 4, n)


def pack_gradients(packed, plan, mats, vecs):
    d, inner = plan.d, plan.inner
    half = inner // 2
    for w in range(2):
        at = 0
        for ref, used in mats:
            for b in range(blocks_of(used)):
                stop = min(used, LANES * (b + 1))
                lanes = slice(LANES * b, stop)
                for r in range(ROWS_OF):
                    base = half * w + 16 * r
                    if r < ROWS_OF - 1:
                        value = ref[base : base + 16, lanes]
                    else:
                        value = ref[base : base + 8, lanes]
                        low = ref[inner : inner + 8, lanes] if ref.shape[0] > inner else jnp.zeros_like(value)
                        value = jnp.concatenate([value, low], axis=0)
                    if stop - LANES * b < LANES:
                        blank = jnp.zeros((16, LANES * (b + 1) - stop), F32)
                        value = jnp.concatenate([value, blank], axis=1)
                    packed[w, at] = value.astype(BF)
                    at += 1
        if vecs:
            columns = []
            for ref in vecs:
                total = jnp.sum(ref[...], axis=1, keepdims=True)
                if ref.shape[0] == d:
                    columns.append(total[2 * half * w : 2 * half * w + half])
                    columns.append(total[2 * half * w + half : 2 * half * w + 2 * half])
                else:
                    columns.append(total[half * w : half * (w + 1)])
            lane = lax.broadcasted_iota(jnp.int32, (half, LANES), 1)
            value = jnp.zeros((half, LANES), F32)
            for lane_at, column in enumerate(columns):
                value = jnp.where(lane == lane_at, column, value)
            value = jnp.concatenate([value, jnp.zeros((ROWS_OF * 16 - half, LANES), F32)], axis=0)
            for r in range(ROWS_OF):
                packed[w, at] = value[16 * r : 16 * r + 16].astype(BF)
                at += 1
        left = packed.shape[1] - at
        if left:
            packed[w, at : packed.shape[1]] = jnp.zeros((left, 16, LANES), BF)


def in_chunks(count, body):
    size = max(c for c in range(1, 17) if count % c == 0)

    def step(i, _):
        body(i * size, size)
        return 0

    lax.fori_loop(0, count // size, step, 0)


def copy_pieces(dst, src, at, count):
    dst[pl.ds(at, count)] = src[pl.ds(at, count)]


def hooks(steps, actions):
    step = pl.program_id(0)

    def hook(end):
        for place, action in actions:
            if (place >= steps) == end:

                @pl.when(step == min(place, steps - 1))
                def _(action=action):
                    action()

    return hook


class Summing:
    def __init__(self, part, given, out, traffic):
        self.part, self.given, self.out = part, given, out
        self.got, self.total, self.leave, self.landed, self.core, self.down, *up = traffic
        self.up = up[0] if up else None
        self.me = lax.axis_index("wa")
        self.seq = lax.axis_index("seq")
        self.steps = len(part.rounds)
        self.orders = []
        for s in range(part.streams):
            order = list(range(self.steps))
            if s % 2 and self.steps > 2:
                order[0], order[1] = order[1], order[0]
            if s % 4 > 1 and self.steps > 2:
                order.insert(1, order.pop())
            self.orders.append(order)

    @staticmethod
    def scratch(part):
        sem = pltpu.SemaphoreType.DMA
        steps = max(1, len(part.rounds))
        pieces = (part.pieces, 16, LANES)
        return [
            pltpu.VMEM(pieces, BF),
            pltpu.VMEM(pieces, F32),
            pltpu.VMEM(pieces, BF),
            pltpu.VMEM(pieces, BF),
            sem((2,)),
            sem((2, steps, part.streams, 3)),
        ]

    @staticmethod
    def spread_scratch(part):
        return [pltpu.SemaphoreType.DMA((2, max(1, len(part.rounds)), part.streams, 3))]

    def digit(self, which, by=0):
        base, radix = self.part.rounds[which]
        return lax.rem(lax.div(self.seq, base) + by, radix)

    def others(self, which):
        return range(1, self.part.rounds[which][1])

    def peer(self, which, by):
        base = self.part.rounds[which][0]
        return {"seq": self.seq + (self.digit(which, by) - self.digit(which)) * base}

    def partners(self):
        peers = [self.peer(which, by) for which in range(self.steps) for by in self.others(which)]
        return [{"wa": 1 - self.me}, *peers]

    def range_at(self, s, k):
        start, size, land = s * self.part.per, self.part.per, s * self.part.per
        for i in range(k):
            radix = self.part.rounds[self.orders[s][i]][1]
            size //= radix
            start = start + self.digit(self.orders[s][i]) * size
            if i < k - 1:
                land += (radix - 1) * size
        return start, size, land

    def core_copy(self):
        return send_copy(
            self.given.at[1 - self.me], self.got, self.core.at[0], self.core.at[1], {"wa": 1 - self.me}
        )

    def down_copy(self, s, k, by):
        start, _, _ = self.range_at(s, k)
        _, size, land = self.range_at(s, k + 1)
        which = self.orders[s][k]
        return send_copy(
            self.leave.at[pl.ds(start + self.digit(which, by) * size, size)],
            self.landed.at[pl.ds(land + (by - 1) * size, size)],
            self.down.at[0, k, s, by - 1],
            self.down.at[1, k, s, by - 1],
            self.peer(which, by),
        )

    def up_copy(self, s, k, by):
        start, size, _ = self.range_at(s, k + 1)
        ref = self.out.at[pl.ds(start, size)]
        which = self.orders[s][k]
        return send_copy(ref, ref, self.up.at[0, k, s, by - 1], self.up.at[1, k, s, by - 1], self.peer(which, by))

    def add(self, s, k):
        start, size, land = self.range_at(s, k)

        def summed(at, count):
            if k == 0:
                own = self.given[self.me, pl.ds(start + at, count)].astype(F32)
                return own + self.got[pl.ds(start + at, count)].astype(F32)
            total = self.total[pl.ds(start + at, count)]
            for by in self.others(self.orders[s][k - 1]):
                total = total + self.landed[pl.ds(land + (by - 1) * size + at, count)].astype(F32)
            return total

        if k == self.steps:

            def finish(at, count):
                self.out[pl.ds(start + at, count)] = summed(at, count).astype(BF)

            in_chunks(size, finish)
            return
        which = self.orders[s][k]
        part = size // self.part.rounds[which][1]
        for by in self.others(which):
            give = self.digit(which, by) * part

            def to_leave(at, count, give=give):
                self.leave[pl.ds(start + give + at, count)] = summed(give + at, count).astype(BF)

            in_chunks(part, to_leave)
            self.down_copy(s, k, by).start()
        own = self.digit(which) * part

        def to_keep(at, count):
            self.total[pl.ds(start + own + at, count)] = summed(own + at, count)

        in_chunks(part, to_keep)

    def reduce_stage(self, at):
        if at == 0:
            self.core_copy().start()
            return
        if at == 1:
            self.core_copy().wait()
        for s in range(self.part.streams):
            if at > 1:
                for by in self.others(self.orders[s][at - 2]):
                    self.down_copy(s, at - 2, by).wait()
            self.add(s, at - 1)

    def spread_stage(self, at):
        for s in range(self.part.streams):
            if at > 0:
                for by in self.others(self.orders[s][self.steps - at]):
                    self.up_copy(s, self.steps - at, by).wait()
            if at < self.steps:
                for by in self.others(self.orders[s][self.steps - at - 1]):
                    self.up_copy(s, self.steps - at - 1, by).start()

    def take_share(self, source):
        for s in range(self.part.streams):
            start, size, _ = self.range_at(s, self.steps)
            in_chunks(size, lambda at, count, start=start: copy_pieces(self.out, source, start + at, count))


def sum_kernel(plan, late_given, early_share, early_out, late_out, *traffic):
    late = Summing(plan.late, late_given, late_out, traffic[:7])
    early = Summing(plan.early, None, early_out, (None,) * 6 + traffic[7:])
    steps = late.steps
    greet(late.partners())
    late.reduce_stage(0)
    early.take_share(early_share)
    early.spread_stage(0)
    late.reduce_stage(1)
    for at in range(steps):
        early.spread_stage(at + 1)
        late.reduce_stage(at + 2)
    for at in range(steps + 1):
        late.spread_stage(at)


def finish_kernel(plan, grad_low, first, early, late, grad, *rest):
    results, large, stored = list(rest[:24]), rest[24:30], rest[30]
    outs, copies = list(results), []
    for at, place in enumerate(LARGE):
        outs[place] = large[at]
        copies.append(pltpu.make_async_copy(large[at], results[place], stored.at[at]))
    d, inner = plan.d, plan.inner
    half = inner // 2
    grad[...] = grad_low[...].astype(F32)

    @pl.when(pl.program_id(0) == 0)
    def _():
        me = lax.axis_index("wa")

        def matrix(name):
            for part, ref in ((plan.first, first), (plan.early, early), (plan.late, late)):
                if name in part.starts:
                    break
            begin, used = part.starts[name]
            parts = []
            for b in range(begin, begin + blocks_of(used)):
                value = ref[b * ROWS_OF : (b + 1) * ROWS_OF].reshape(ROWS_OF * 16, LANES)
                parts.append(value.astype(F32))
            return jnp.concatenate(parts, axis=1)

        def my_half(line, size):
            return jnp.where(me == 0, line[:, 0:size], line[:, size : 2 * size])

        turned = matrix("vec")[0:half].T

        def write(ref, pieces):
            ref[...] = jnp.concatenate(pieces, axis=1).reshape(ref.shape)

        for side, taps in enumerate((ENCODER_TAPS, DECODER_TAPS)):
            tag = "ed"[side]
            first_g, first_b, red_w, red_b, mid_g, mid_b, ker, ker_b, last_g, last_b, exp_w, exp_b = outs[
                12 * side : 12 * side + 12
            ]
            at = 8 * side
            write(first_g, [turned[at : at + 1], turned[at + 1 : at + 2]])
            write(first_b, [turned[at + 2 : at + 3], turned[at + 3 : at + 4]])
            write(mid_g, [turned[at + 4 : at + 5]])
            write(mid_b, [turned[at + 5 : at + 6]])
            write(last_g, [turned[at + 6 : at + 7]])
            write(last_b, [turned[at + 7 : at + 8]])
            value = matrix(tag + "_we")
            exp_w[...] = value[0:half, 0:d]
            write(exp_b, [my_half(value[half : half + 1, 0:d], d // 2)])
            value = matrix(tag + "_k")
            for j in range(taps):
                ker[j] = jnp.concatenate([value[0:half, place] for _, place in tap_pieces(j, taps, inner)], axis=1)
            centre = (ENCODER_SHIFTS if side == 0 else DECODER_SHIFTS).index(0)
            sums = [value[half : half + 1, place] for _, place in tap_pieces(centre, taps, inner)]
            write(ker_b, [my_half(jnp.concatenate(sums, axis=1), half)])
            value = matrix(tag + "_wr")[0:half]
            red_w[...] = value[:, 0:d]
            write(red_b, [value[:, d:].T[0:1]])
            for copy in copies[3 * side : 3 * side + 3]:
                copy.start()

    @pl.when(pl.program_id(0) == plan.steps - 1)
    def _():
        for copy in copies:
            copy.wait()


def local(n, stream, doc_start, doc_end, cotangent, *weights):
    rows, d = stream.shape[1], stream.shape[2]
    inner = weights[6].shape[1] * 2
    steps = rows // TILE
    x, cot = stream[0].T, cotangent[0].T
    starts, ends = doc_start, doc_end
    weights = [w.T if at % 12 == 2 else w for at, w in enumerate(weights)]
    enc, dec = gather_weights(weights, d, inner)
    wrt_e, kt_e, wet_e, we_e, kb_e, wr_e, g1_e, f1_e, b1_e, g2_e, f2_e, b2_e, g3_e, f3_e, b3_e = enc
    wrt_d, kt_d, wet_d, we_d, kb_d, wr_d, g1_d, f1_d, b1_d, g2_d, f2_d, b2_d, g3_d, f3_d, b3_d = dec

    plan = Plan(d, inner, steps, n)
    blocks = rows // LANES
    per = TILE // LANES

    def spec(a):
        return whole(a.shape)

    def wide(channels, dtype=BF):
        return jax.ShapeDtypeStruct((channels, rows), dtype)

    def fixed(shape, dtype=F32):
        return jax.ShapeDtypeStruct(shape, dtype)

    class Order:
        def __init__(self, first):
            self.tile = lambda i: (i + first) % steps

        def cols(self, channels):
            return pl.BlockSpec((channels, TILE), lambda i: (0, self.tile(i)))

        def before(self, channels):
            return pl.BlockSpec((channels, LANES), lambda i: (0, (per * self.tile(i) + blocks - 1) % blocks))

        def after(self, channels):
            return pl.BlockSpec((channels, LANES), lambda i: (0, (per * self.tile(i) + per) % blocks))

    def head(channels):
        return pl.BlockSpec((channels, LANES), lambda i: (0, 0))

    def tail(channels):
        return pl.BlockSpec((channels, LANES), lambda i: (0, blocks - 1))

    plain, later = Order(0), Order(1)
    d1, i1 = d + AUG, inner + AUG
    norm_wide = [(d1, BF), (d, BF), (d, BF), (8, F32)]
    norm_in = [(i1, BF), (inner, BF), (inner, BF), (8, F32)]
    sem = pltpu.SemaphoreType.DMA
    vmem = pltpu.VMEM

    def outs_of(order, items):
        return [wide(c, t) for c, t in items], [order.cols(c) for c, _ in items]

    shapes, specs = outs_of(plain, norm_wide + norm_in)
    ins = [wrt_e, f1_e, b1_e, f2_e, b2_e]
    h1e, z1e, d1e, r1e, h2e, z2e, d2e, r2e = pl.pallas_call(
        enc_in_kernel,
        grid=(steps,),
        out_shape=shapes,
        in_specs=[plain.cols(d)] + [spec(a) for a in ins],
        out_specs=specs,
        scratch_shapes=[vmem((d, TILE), F32)] + [vmem((inner, HALF), F32)] * 2 + [vmem((d1, HALF), BF)] * 2,
        compiler_params=params(),
        name="encoder_in",
    )(x, *ins)

    shapes, specs = outs_of(later, norm_in + [(d, BF)] + norm_wide + norm_in)
    ins = [kt_e, wet_e, wrt_d, f3_e, b3_e, f1_d, b1_d, f2_d, b2_d]
    h3e, z3e, d3e, r3e, x1, h1d, z1d, d1d, r1d, h2d, z2d, d2d, r2d, edge_d = pl.pallas_call(
        functools.partial(enc_out_kernel, steps),
        grid=(steps,),
        out_shape=shapes + [fixed((i1, LANES), BF)],
        in_specs=[later.cols(1), later.cols(1), later.before(i1), later.cols(i1), later.after(i1)]
        + [head(i1), tail(i1), later.cols(d)]
        + [spec(a) for a in ins],
        out_specs=specs + [whole((i1, LANES))],
        scratch_shapes=[
            vmem((ENCODER_TAPS * inner + AUG, TILE), BF),
            vmem((inner, LANES), BF),
            vmem((inner, LANES), BF),
        ]
        + [vmem((inner, HALF), F32)] * 2
        + [vmem((d, HALF), F32)] * 2
        + [vmem((inner, HALF), F32)] * 2
        + [vmem((i1, HALF), BF)] * 2
        + [vmem((d1, HALF), BF)] * 2
        + [vmem((i1, LANES), BF)] * 4
        + [sem((3,)), sem((3,))],
        compiler_params=params(1),
        name="encoder_out",
    )(starts, ends, h2e, h2e, h2e, h2e, h2e, x, *ins)

    small, large = fixed((inner, LANES)), fixed((d, LANES))
    sums = [fixed((2, plan.first.pieces, 16, LANES), BF), small, small]
    ins = [kt_d, we_d, wet_d, f3_d, b3_d, g3_d]
    out, evr_d, packed_first, dg3_d, db3_d = pl.pallas_call(
        functools.partial(dec_out_kernel, plan),
        grid=(steps,),
        out_shape=[wide(d, F32), wide(inner)] + sums,
        in_specs=[plain.cols(1), plain.cols(1), plain.before(i1), plain.cols(i1), spec(edge_d)]
        + [plain.cols(d), plain.cols(d)]
        + [spec(a) for a in ins],
        out_specs=[plain.cols(d), plain.cols(inner)] + [whole(s.shape) for s in sums],
        scratch_shapes=[
            vmem((i1, d), F32),
            vmem((DECODER_TAPS * inner + AUG, TILE), BF),
            vmem((inner, LANES), BF),
            vmem((inner, HALF), F32),
            vmem((inner, HALF), F32),
            vmem((i1, TILE), BF),
            vmem((inner, TILE), BF),
            vmem((inner, TILE), BF),
            vmem((8, TILE), F32),
        ]
        + [vmem((inner, HALF), F32)] * 2
        + [vmem((inner, HALF), BF)] * 2
        + [vmem((i1, HALF), BF)] * 2,
        compiler_params=params(),
        name="decoder_out",
    )(starts, ends, h2d, h2d, edge_d, cot, x1, *ins)

    shapes, specs = outs_of(plain, [(d, BF), (inner, BF)])
    early = fixed((2, plan.early.pieces, 16, LANES), BF)
    first = fixed((plan.first.pieces, 16, LANES), BF)
    sums = [small, small, large, large, small, small]
    ins = [kb_d, wr_d, we_e, g2_d, g1_d, g3_e]
    stash = [h2d, z2d, d2d, r2d, h1d, z1d, d1d, r1d, cot, h3e, z3e, d3e, r3e]
    ey, evr_e, packed, first_share, dg2_d, db2_d, dg1_d, db1_d, dg3_e, db3_e = pl.pallas_call(
        functools.partial(dec_back_kernel, plan),
        grid=(steps,),
        out_shape=shapes + [early, first] + sums,
        in_specs=[plain.cols(1), plain.cols(1), plain.cols(inner), plain.after(inner), head(inner)]
        + [spec(a) for a in ins]
        + [plain.cols(a.shape[0]) for a in stash]
        + [spec(packed_first)],
        out_specs=specs + [whole(early.shape), whole(first.shape)] + [whole(s.shape) for s in sums],
        scratch_shapes=[
            vmem((i1, DECODER_TAPS * inner), F32),
            vmem((inner, d1), F32),
            vmem((i1, d), F32),
            vmem((DECODER_TAPS * inner, TILE), BF),
            vmem((inner, LANES), BF),
        ]
        + [vmem((inner, HALF), F32)] * 4
        + [vmem((d, HALF), F32)] * 2
        + [vmem((inner, TILE), BF)]
        + [vmem((inner, HALF), BF)] * 2
        + [vmem((d, HALF), BF)] * 4
        + [vmem((inner, HALF), BF)] * 2
        + [vmem((inner, LANES), BF), sem((1,)), sem((1,))]
        + Summing.scratch(plan.first),
        compiler_params=params(2),
        name="decoder_back",
    )(starts, ends, evr_d, evr_d, evr_d, *ins, *stash, packed_first)

    late = fixed((2, plan.late.pieces, 16, LANES), BF)
    early_sum = fixed((plan.early.pieces, 16, LANES), BF)
    ins = [kb_e, wr_e, g2_e, g1_e]
    stash = [h2e, z2e, d2e, r2e, h1e, z1e, d1e, r1e, ey]
    vecs = [dg3_e, db3_e, dg1_d, db1_d, dg2_d, db2_d, dg3_d, db3_d]
    grad_low, packed_late, summed, first_whole = pl.pallas_call(
        functools.partial(enc_back_kernel, plan),
        grid=(steps,),
        out_shape=[wide(d), late, early_sum, first],
        in_specs=[later.cols(1), later.cols(1), later.before(inner), later.cols(inner), later.after(inner)]
        + [head(inner), tail(inner)]
        + [spec(a) for a in ins]
        + [later.cols(a.shape[0]) for a in stash]
        + [whole(early.shape), whole(first.shape)]
        + [spec(a) for a in vecs],
        out_specs=[later.cols(d), whole(late.shape), whole(early_sum.shape), whole(first.shape)],
        scratch_shapes=[
            vmem((i1, ENCODER_TAPS * inner), F32),
            vmem((inner, d1), F32),
            vmem((inner, LANES), F32),
            vmem((inner, LANES), F32),
            vmem((d, LANES), F32),
            vmem((d, LANES), F32),
            vmem((ENCODER_TAPS * inner, TILE), BF),
            vmem((inner, LANES), BF),
            vmem((inner, LANES), BF),
        ]
        + [vmem((inner, HALF), F32)] * 2
        + [vmem((d, HALF), F32)] * 2
        + [vmem((inner, TILE), BF)]
        + [vmem((inner, HALF), BF)] * 2
        + [vmem((d, HALF), BF)] * 2
        + [vmem((inner, HALF), BF)] * 2
        + [vmem((inner, LANES), BF)] * 2
        + [sem((2,)), sem((2,)), vmem(first.shape, BF)]
        + Summing.spread_scratch(plan.first)
        + Summing.scratch(plan.early),
        compiler_params=params(3),
        name="encoder_back",
    )(starts, ends, evr_e, evr_e, evr_e, evr_e, evr_e, *ins, *stash, packed, first_share, *vecs)

    vm = pl.BlockSpec(memory_space=pltpu.VMEM)
    early_whole, late_whole = pl.pallas_call(
        functools.partial(sum_kernel, plan),
        out_shape=[early_sum, fixed((plan.late.pieces, 16, LANES), BF)],
        in_specs=[vm, vm],
        out_specs=[vm, vm],
        scratch_shapes=Summing.scratch(plan.late)
        + Summing.spread_scratch(plan.late)
        + Summing.spread_scratch(plan.early),
        compiler_params=params(4),
        name="sum_gradients",
    )(packed_late, summed)

    grad, *shares = pl.pallas_call(
        functools.partial(finish_kernel, plan),
        grid=(steps,),
        out_shape=[wide(d, F32)] + [fixed(w.shape) for w in weights],
        in_specs=[plain.cols(d), whole(first_whole.shape), whole(early_whole.shape), whole(late_whole.shape)],
        out_specs=[plain.cols(d)]
        + [pl.BlockSpec(memory_space=pl.ANY) if at in LARGE else whole(w.shape) for at, w in enumerate(weights)],
        scratch_shapes=[vmem(weights[at].shape, F32) for at in LARGE] + [sem((len(LARGE),))],
        compiler_params=params(),
        name="finish",
    )(grad_low, first_whole, early_whole, late_whole)
    shares = [w.T if at % 12 == 2 else w for at, w in enumerate(shares)]
    return (out.T[None], grad.T[None], *shares)


def solution(mesh):
    rows = P("wa", "seq", None)
    block = (
        P("wa"), P("wa"), P(None, "wa"), P("wa"), P("wa"), P("wa"),
        P(None, "wa", None), P("wa"), P("wa"), P("wa"), P("wa", None), P("wa"),
    )
    return jax.shard_map(
        functools.partial(local, mesh.shape["seq"]),
        mesh=mesh,
        in_specs=(rows, P("wa", "seq"), P("wa", "seq"), rows, *block, *block),
        out_specs=(rows, rows, *block, *block),
        check_vma=False,
    )
```

```python
import functools

import jax
import jax.numpy as jnp
from jax import lax
from jax.experimental import pallas as pl
from jax.experimental.pallas import tpu as pltpu
from jax.sharding import PartitionSpec as P

ENCODER_TAPS = 5
ENCODER_DILATION = 8
DECODER_TAPS = 3
DECODER_DILATION = 16
EPS = 1e-05

MESH = pl.DeviceIdType.MESH
BF = jnp.bfloat16
F32 = jnp.float32
LANES = 128
TILE = 512
HALF = 256
AUG = 16
VMEM_LIMIT = 56 * 1024 * 1024
GELU_1 = 2.0 * 0.7978845608028654
GELU_3 = 8.0 * 0.7978845608028654 * 0.044715

ENCODER_SHIFTS = tuple(ENCODER_DILATION * (j - ENCODER_TAPS // 2) for j in range(ENCODER_TAPS))
DECODER_SHIFTS = tuple(-DECODER_DILATION * (DECODER_TAPS - 1 - j) for j in range(DECODER_TAPS))


def params(collective=None):
    if collective is None:
        return pltpu.CompilerParams(vmem_limit_bytes=VMEM_LIMIT)
    return pltpu.CompilerParams(
        vmem_limit_bytes=VMEM_LIMIT, collective_id=collective, has_side_effects=True
    )


def whole(shape):
    return pl.BlockSpec(shape, lambda *_: (0,) * len(shape))


def nt_dot(left, right):
    return lax.dot_general(left, right, (((1,), (1,)), ((), ())), preferred_element_type=F32)


def nn_dot(left, right):
    return jnp.dot(left, right, preferred_element_type=F32)


def product(out, left, right, extra=None):
    rows = out.shape[0]
    middle = (rows // 2 + 15) // 16 * 16
    for a, b in ((0, middle), (middle, rows)):
        value = nn_dot(left[a:b, :], right)
        out[a:b, :] = value if extra is None else value + extra[a:b, :].astype(F32)


def lanes_of(column, width):
    return jnp.concatenate([column] * (width // LANES), axis=1)


def fold(value):
    total = value[:, :LANES]
    for at in range(LANES, value.shape[1], LANES):
        total = total + value[:, at : at + LANES]
    return total


def weights_kernel(dims, *refs):
    d, inner, taps = dims
    n_in = 24
    ins, refs = refs[:n_in], refs[n_in:]
    results, refs = refs[:30], refs[30:]
    outs, refs = refs[:30], refs[30:]
    (small_own, small_got, k_own0, k_own1, e_own0, e_own1, r_own0, r_own1, *rest) = refs
    (r_got0, r_got1, k_got0, k_got1, e_got0, e_got1, k_all, send, recv, store) = rest
    me = lax.axis_index("wa")
    other = 1 - me
    barrier = pltpu.get_barrier_semaphore()
    pl.semaphore_signal(barrier, inc=1, device_id={"wa": other}, device_id_type=MESH)
    pl.semaphore_wait(barrier, 1)

    half = inner // 2
    pad = k_own0.shape[1]
    small_own[...] = jnp.zeros_like(small_own)
    small_at = []
    for side in range(2):
        for at in (0, 1, 3, 4, 5, 7, 8, 9, 11):
            small_at.append(12 * side + at)
    for row, at in enumerate(small_at):
        n = ins[at].shape[0]
        small_own[row : row + 1, 0:n] = ins[at][...].astype(F32).reshape(1, n)
    owns, gots = [], []
    for side, (k_own, e_own, r_own) in enumerate(((k_own0, e_own0, r_own0), (k_own1, e_own1, r_own1))):
        base = 12 * side
        k_own[:, half - 8 : pad, :] = jnp.zeros((taps[side], pad - half + 8, inner), BF)
        k_own[:, 0:half, :] = ins[base + 6][...]
        e_own[half - 8 : pad, :] = jnp.zeros((pad - half + 8, d), BF)
        e_own[0:half, :] = ins[base + 10][...]
        r_own[half - 8 : pad, :] = jnp.zeros((pad - half + 8, d), BF)
        r_own[0:half, :] = ins[base + 2][...]
        owns += [r_own, k_own, e_own]
    owns.append(small_own)
    gots = [r_got0, k_got0, e_got0, r_got1, k_got1, e_got1, small_got]
    copies = []
    pairs = list(zip(owns, gots))
    for at in (6, 0, 2, 1, 3, 5, 4):
        own, got = pairs[at]
        copies.append(
            pltpu.make_async_remote_copy(
                src_ref=own,
                dst_ref=got,
                send_sem=send.at[at],
                recv_sem=recv.at[at],
                device_id={"wa": other},
                device_id_type=MESH,
            )
        )
        copies[-1].start()
    arrival = dict(zip((6, 0, 2, 1, 3, 5, 4), copies))
    stores = []

    def keep(at):
        stores.append(pltpu.make_async_copy(outs[at], results[at], store.at[at]))
        stores[-1].start()

    first_core = me == 0
    square = (HALF, HALF)
    unit = lax.broadcasted_iota(jnp.int32, square, 0) == lax.broadcasted_iota(jnp.int32, square, 1)
    unit = jnp.where(unit, 1.0, 0.0).astype(BF)

    def turn(out, columns, count, width=None):
        for a in range(0, count, HALF):
            b = min(a + HALF, count)
            piece = nt_dot(unit[0 : b - a, 0 : b - a], columns(a, b)).astype(BF)
            if width is None:
                out[a:b, :] = piece
            else:
                out[a:b, 0:width] = piece

    def ordered(own, got):
        own, got = own.astype(F32), got.astype(F32)
        return jnp.where(first_core, own, got), jnp.where(first_core, got, own)

    arrival[6].wait()
    small0, small1 = ordered(small_own[...], small_got[...])

    def column(row, n):
        line = jnp.concatenate([small0[row : row + 1, 0 : n // 2], small1[row : row + 1, 0 : n // 2]], axis=1)
        return jnp.broadcast_to(line, (LANES, n)).T

    def bias_columns(value):
        where = lax.broadcasted_iota(jnp.int32, (value.shape[0], AUG), 1) == 0
        return jnp.where(where, value[:, :AUG], 0.0).astype(BF)

    for side in range(2):
        o = outs[15 * side : 15 * side + 15]
        wrt, kt, wet, we, kb, wr, *vectors = o
        base = 9 * side
        for at, (row, n) in enumerate(((0, d), (3, inner), (6, inner))):
            gain, half_gain, half_bias = vectors[3 * at : 3 * at + 3]
            gain[...] = column(base + row, n)
            half_gain[...] = gain[...] * 0.5
            half_bias[...] = column(base + row + 1, n) * 0.5
        n = taps[side]
        first = 15 * side
        for at in range(6, 15):
            keep(first + at)
        arrival[3 * side].wait()
        r0, r1 = ordered(owns[3 * side][0:half, :], gots[3 * side][0:half, :])
        wrt[:, 0:d] = jnp.concatenate([r0, r1], axis=0).astype(BF)
        wrt[:, d : d + AUG] = bias_columns(column(base + 2, inner))
        keep(first)
        turn(wr, lambda a, b: wrt[:, a:b], d)
        keep(first + 5)
        arrival[3 * side + 2].wait()
        e0, e1 = ordered(owns[3 * side + 2][0:half, :], gots[3 * side + 2][0:half, :])
        we[...] = jnp.concatenate([e0, e1], axis=0).astype(BF)
        keep(first + 3)
        turn(wet, lambda a, b: we[:, a:b], d, inner)
        wet[:, inner : inner + AUG] = bias_columns(column(base + 8, d))
        keep(first + 2)
        arrival[3 * side + 1].wait()
        for j in range(n):
            k0, k1 = ordered(owns[3 * side + 1][j, 0:half, :], gots[3 * side + 1][j, 0:half, :])
            k = jnp.concatenate([k0, k1], axis=0).astype(BF)
            for channels, place in tap_pieces(j, n, inner):
                kb[:, place] = k[:, channels]
                k_all[place, :] = k[channels, :]
        keep(first + 4)
        turn(kt, lambda a, b: k_all[0 : n * inner, a:b], inner, n * inner)
        kt[:, n * inner : n * inner + AUG] = bias_columns(column(base + 5, inner))
        keep(first + 1)
    for copy in stores:
        copy.wait()


def gather_weights(args, d, inner):
    taps = (ENCODER_TAPS, DECODER_TAPS)
    half = inner // 2
    pad = -(-half // 16) * 16
    shapes = []
    for n in taps:
        shapes += [
            ((inner, d + AUG), BF),
            ((inner, n * inner + AUG), BF),
            ((d, inner + AUG), BF),
            ((inner, d), BF),
            ((inner, n * inner), BF),
            ((d, inner), BF),
        ]
        for c in (d, inner, inner):
            shapes += [((c, LANES), F32)] * 3
    vm = pl.BlockSpec(memory_space=pltpu.VMEM)
    small = pltpu.VMEM((24, 512), F32)
    kk = [pltpu.VMEM((n, pad, inner), BF) for n in taps]
    ee = [pltpu.VMEM((pad, d), BF)] * 2
    outs = pl.pallas_call(
        functools.partial(weights_kernel, (d, inner, taps)),
        out_shape=[jax.ShapeDtypeStruct(*s) for s in shapes],
        in_specs=[vm] * 24,
        out_specs=[pl.BlockSpec(memory_space=pl.ANY)] * 30,
        scratch_shapes=[pltpu.VMEM(*shape) for shape in shapes]
        + [small, small, *kk, *ee, *ee, *ee, *kk, *ee]
        + [pltpu.VMEM((taps[0] * inner, inner), BF)]
        + [pltpu.SemaphoreType.DMA((7,)), pltpu.SemaphoreType.DMA((7,)), pltpu.SemaphoreType.DMA((30,))],
        compiler_params=params(0),
        name="gather_weights",
    )(*args)
    return outs[:15], outs[15:]


def pacing(thunks, slots):
    state = [0, 0]
    thunks = list(thunks)

    def between():
        while state[1] < len(thunks) and state[0] * len(thunks) >= state[1] * slots:
            thunks[state[1]]()
            state[1] += 1
        state[0] += 1

    return between


def add_product(total, left, right):
    def piece(at, stop):
        total[:, at:stop] += nt_dot(left[...], right[at:stop, :])

    columns = right.shape[0]
    return [functools.partial(piece, at, min(at + HALF, columns)) for at in range(0, columns, HALF)]


def norm_forward(src, lanes, channels, gain, bias, h_out, z_out, d_out, r_out, keep=None, fill=(), at=None, h_copy=None):
    width = lanes.stop - lanes.start
    between = pacing(fill, 3 * (channels // 16))
    total = [jnp.zeros((8, width), F32) for _ in range(4)]
    for c in range(0, channels, 16):
        between()
        x = src[c : c + 16, at or lanes].astype(F32)
        if keep is not None:
            keep[c : c + 16, at or lanes] = x
        k = (c // 8) % 4
        total[k] = total[k] + x[0:8]
        total[k + 1] = total[k + 1] + x[8:16]
    mean = jnp.sum((total[0] + total[1]) + (total[2] + total[3]), axis=0, keepdims=True) * (1.0 / channels)
    wide = jnp.broadcast_to(mean, (16, width))
    values = src if keep is None else keep
    total = [jnp.zeros((8, width), F32) for _ in range(4)]
    for c in range(0, channels, 16):
        between()
        centre = values[c : c + 16, at or lanes] - wide
        square = centre * centre
        k = (c // 8) % 4
        total[k] = total[k] + square[0:8]
        total[k + 1] = total[k + 1] + square[8:16]
    spread = jnp.sum((total[0] + total[1]) + (total[2] + total[3]), axis=0, keepdims=True) * (1.0 / channels)
    r = lax.rsqrt(spread + EPS)
    if r_out is not None:
        r_out[:, lanes] = jnp.broadcast_to(r, (8, width))
    rw = jnp.broadcast_to(r, (16, width))
    mw = jnp.broadcast_to(mean * r, (16, width))
    one, point = BF(1.0), BF(0.5)
    for c in range(0, channels, 16):
        between()
        rows = slice(c, c + 16)
        z = values[rows, at or lanes] * rw - mw
        half = (z * lanes_of(gain[rows, :], width) + lanes_of(bias[rows, :], width)).astype(BF)
        sq = half * half
        t = jnp.tanh(half * (sq * BF(GELU_3) + BF(GELU_1)))
        up = one + t
        h_out[rows, lanes] = half * up
        if h_copy is not None:
            h_copy[rows, :] = half * up
        d_out[rows, lanes] = up * (point + half * (sq * BF(1.5 * GELU_3) + BF(0.5 * GELU_1)) * (one - t))
        z_out[rows, lanes] = z.astype(BF)


def norm_backward(grad, lanes, channels, gain, z_in, d_in, r_in, gain_sum, bias_sum, keep, emit, fill=(), at=None):
    width = lanes.stop - lanes.start
    between = pacing(fill, 2 * (channels // 16))
    one = [jnp.zeros((8, width), F32) for _ in range(2)]
    two = [jnp.zeros((8, width), F32) for _ in range(2)]
    r = r_in[0:1, lanes]
    rw = jnp.broadcast_to(r, (16, width))
    for c in range(0, channels, 16):
        between()
        rows = slice(c, c + 16)
        da = grad[rows, at or lanes] * d_in[rows, lanes].astype(F32)
        p = da * z_in[rows, lanes].astype(F32)
        bias_sum[rows, :] += fold(da)
        gain_sum[rows, :] += fold(p)
        wide = lanes_of(gain[rows, :], width)
        dz = da * wide
        q = p * wide
        keep[rows, at or lanes] = (dz * rw).astype(BF)
        for k in range(2):
            one[k] = one[k] + dz[8 * k : 8 * k + 8]
            two[k] = two[k] + q[8 * k : 8 * k + 8]
    scale = r * (1.0 / channels)
    m1 = jnp.broadcast_to(jnp.sum(one[0] + one[1], axis=0, keepdims=True) * scale, (16, width)).astype(BF)
    m2 = jnp.broadcast_to(jnp.sum(two[0] + two[1], axis=0, keepdims=True) * scale, (16, width)).astype(BF)
    for c in range(0, channels, 16):
        between()
        rows = slice(c, c + 16)
        emit(rows, keep[rows, at or lanes] - (z_in[rows, lanes] * m2 + m1))


def tap_mask(starts, ends, first, shift):
    place = first + shift + lax.broadcasted_iota(jnp.int32, (8, TILE), 1)
    usable = (place >= jnp.broadcast_to(starts[...], (8, TILE))) & (place < jnp.broadcast_to(ends[...], (8, TILE)))
    one = jnp.where(usable, 1.0, 0.0)
    return jnp.concatenate([one, one], axis=0).astype(BF)


def tap_row(j, c, taps, inner):
    aligned = inner // LANES * LANES
    return j * aligned + c if c < aligned else taps * aligned + j * (inner - aligned) + c - aligned


def tap_pieces(j, taps, inner):
    aligned = inner // LANES * LANES
    for a, b in ((0, aligned), (aligned, inner)):
        at = tap_row(j, a, taps, inner)
        yield slice(a, b), slice(at, at + b - a)


def stack_taps(stack, shifts, before, main, after, starts, ends, first, inner):
    for j, shift in enumerate(shifts):
        if not shift:
            for channels, place in tap_pieces(j, len(shifts), inner):
                stack[place, :] = main[channels, :]
            continue
        mask = tap_mask(starts, ends, first, shift)
        for c in range(0, inner, 16):
            rows = slice(c, c + 16)
            if shift < 0:
                span = jnp.concatenate([before[rows, :], main[rows, :]], axis=1)
                span = pltpu.roll(span, -shift, 1)[:, LANES:]
            else:
                span = jnp.concatenate([main[rows, :], after[rows, :]], axis=1)
                span = pltpu.roll(span, TILE + LANES - shift, 1)[:, :TILE]
            at = tap_row(j, c, len(shifts), inner)
            stack[at : at + 16, :] = span * mask


def ones_rows(width):
    where = lax.broadcasted_iota(jnp.int32, (AUG, width), 0) == 0
    return jnp.where(where, 1.0, 0.0).astype(BF)


def neighbours():
    me = lax.axis_index("seq")
    n = lax.axis_size("seq")
    return lax.rem(me + n - 1, n), lax.rem(me + 1, n)


def greet(others):
    barrier = pltpu.get_barrier_semaphore()
    for device in others:
        pl.semaphore_signal(barrier, inc=1, device_id=device, device_id_type=MESH)
    pl.semaphore_wait(barrier, len(others))


def send_copy(src, dst, send_sem, recv_sem, device):
    return pltpu.make_async_remote_copy(
        src_ref=src, dst_ref=dst, send_sem=send_sem, recv_sem=recv_sem, device_id=device, device_id_type=MESH
    )


def later_tile(step, steps):
    return lax.rem(step + 1, steps)


def first_place(tile, steps):
    return lax.axis_index("seq") * (steps * TILE) + tile * TILE


CHAINS = (slice(0, HALF), slice(HALF, TILE))
EVERY = slice(0, HALF)


def enc_in_kernel(x, wrt, g1, b1, g2, b2, h1, z1, d1, r1, h2, z2, d2, r2, xt, u0, u1, h_wide0, h_wide1):
    d, inner = x.shape[0], wrt.shape[0]
    h1[d : d + AUG, :] = ones_rows(TILE)
    h2[inner : inner + AUG, :] = ones_rows(TILE)
    u, h_wide = (u0, u1), (h_wide0, h_wide1)
    for k in range(2):
        h_wide[k][d : d + AUG, :] = ones_rows(HALF)
        norm_forward(x, CHAINS[k], d, g1, b1, h1, z1, d1, r1, xt, h_copy=h_wide[k])
        product(u[k], wrt, h_wide[k][...])
    for k in range(2):
        norm_forward(u[k], CHAINS[k], inner, g2, b2, h2, z2, d2, r2, at=EVERY)


def choose_edge(window, block, edge, at_end):
    window[...] = block[0 : window.shape[0], :]

    @pl.when(at_end)
    def _():
        window[...] = edge[0 : window.shape[0], :]


def trade_edges(step, steps, head, tail, got_l, got_r, send, recv, others=()):
    left, right = neighbours()
    to_left = send_copy(head, got_r, send.at[0], recv.at[0], {"seq": left})
    to_right = send_copy(tail, got_l, send.at[1], recv.at[1], {"seq": right})

    @pl.when(step == 0)
    def _():
        greet([{"seq": left}, {"seq": right}, *others])
        to_left.start()
        to_right.start()

    @pl.when(step == steps - 2)
    def _():
        to_left.wait()
        to_right.wait()


def enc_out_kernel(
    steps, starts, ends, before, main, after, head, tail, xt, kt, wet, wrt, g3, b3, g1, b1, g2, b2,
    h3, z3, d3, r3, x1, h1, z1, d1, r1, h2, z2, d2, r2, edge_o,
    stack, win_b, win_a, v0, v1, y0, y1, u0, u1, h_in0, h_in1, h_wide0, h_wide1, got_l, got_r, own, got, send, recv,
):
    step = pl.program_id(0)
    d, inner = xt.shape[0], v0.shape[0]
    v, y, u, h_in, h_wide = (v0, v1), (y0, y1), (u0, u1), (h_in0, h_in1), (h_wide0, h_wide1)
    trade_edges(step, steps, head, tail, got_l, got_r, send, recv)
    choose_edge(win_b, before, got_l, step == steps - 1)
    choose_edge(win_a, after, got_r, step == steps - 2)
    stack_taps(stack, ENCODER_SHIFTS, win_b, main, win_a, starts, ends, first_place(later_tile(step, steps), steps), inner)
    stack[len(ENCODER_SHIFTS) * inner :, :] = ones_rows(TILE)
    h3[inner : inner + AUG, :] = ones_rows(TILE)
    h1[d : d + AUG, :] = ones_rows(TILE)
    h2[inner : inner + AUG, :] = ones_rows(TILE)
    one, two = CHAINS

    def make_v(k):
        product(v[k], kt, stack[:, CHAINS[k]])

    def make_y(k):
        product(y[k], wet, h_in[k][...], xt[:, CHAINS[k]])

    def make_u(k):
        product(u[k], wrt, h_wide[k][...])

    def norm_last(k):
        norm_forward(v[k], CHAINS[k], inner, g3, b3, h3, z3, d3, r3, at=EVERY, h_copy=h_in[k])

    def norm_first(k):
        for c in range(0, d, 16):
            x1[c : c + 16, CHAINS[k]] = y[k][c : c + 16, :].astype(BF)
        norm_forward(y[k], CHAINS[k], d, g1, b1, h1, z1, d1, r1, at=EVERY, h_copy=h_wide[k])

    def norm_mid(k):
        norm_forward(u[k], CHAINS[k], inner, g2, b2, h2, z2, d2, r2, at=EVERY)

    for k in range(2):
        h_in[k][inner : inner + AUG, :] = ones_rows(HALF)
        h_wide[k][d : d + AUG, :] = ones_rows(HALF)
    make_v(0)
    make_v(1)
    norm_last(0)
    make_y(0)
    norm_last(1)
    make_y(1)
    norm_first(0)
    make_u(0)
    norm_first(1)
    make_u(1)
    norm_mid(0)
    norm_mid(1)

    def give():
        return send_copy(own, got, send.at[2], recv.at[2], {"seq": neighbours()[1]})

    @pl.when(step == steps - 2)
    def _():
        own[...] = h2[:, TILE - LANES : TILE]
        give().start()

    @pl.when(step == steps - 1)
    def _():
        give().wait()
        edge_o[...] = got[...]


def dec_out_kernel(
    plan, starts, ends, before, main, e_l, cot_t, x1, kt, we, wet, f3, b3, g3,
    out, evr, packed, dg3, db3,
    dwe, stack, win_b, v0, v1, h3, z3, d3, r3, g0, g1, kept0, kept1, h_in0, h_in1,
):
    steps = plan.steps
    step = pl.program_id(0)
    inner = v0.shape[0]
    v, g, kept, h_in = (v0, v1), (g0, g1), (kept0, kept1), (h_in0, h_in1)

    @pl.when(step == 0)
    def _():
        dwe[...] = jnp.zeros_like(dwe)
        dg3[...] = jnp.zeros_like(dg3)
        db3[...] = jnp.zeros_like(db3)

    choose_edge(win_b, before, e_l, step == 0)
    stack_taps(stack, DECODER_SHIFTS, win_b, main, None, starts, ends, first_place(step, steps), inner)
    stack[len(DECODER_SHIFTS) * inner :, :] = ones_rows(TILE)
    h3[inner : inner + AUG, :] = ones_rows(TILE)

    def make_out(k):
        out[:, CHAINS[k]] = nn_dot(wet[...], h_in[k][...]) + x1[:, CHAINS[k]].astype(F32)

    def back(k, fill):
        def emit(rows, value):
            evr[rows, CHAINS[k]] = value

        norm_backward(g[k], CHAINS[k], inner, g3, z3, d3, r3, dg3, db3, kept[k], emit, fill, EVERY)

    for k in range(2):
        h_in[k][inner : inner + AUG, :] = ones_rows(HALF)
        g[k][...] = nn_dot(we[...], cot_t[:, CHAINS[k]])
    for k in range(2):
        product(v[k], kt, stack[:, CHAINS[k]])
    for k in range(2):
        norm_forward(v[k], CHAINS[k], inner, f3, b3, h3, z3, d3, r3, at=EVERY, h_copy=h_in[k])
    products = add_product(dwe, h3, cot_t)
    back(0, [lambda: make_out(0), *products[:2]])
    back(1, [lambda: make_out(1), *products[2:]])

    @pl.when(step == steps - 1)
    def _():
        pack_gradients(packed, plan, ((dwe, dwe.shape[1]),), ())


def dec_back_kernel(
    plan, starts, ends, main, after, head, kb, wr, we, g2, g1, g3,
    h2, z2, d2, r2, h1, z1, d1, r1, cot_t, h3, z3, d3, r3, given,
    ey, evr, packed, first, dg2, db2, dg1, db1, dg3, db3,
    dk, dwrt, dwe, stack, win_a, ga0, ga1, gb0, gb1, big0, big1, eur, eur0, eur1, ey0, ey1,
    kept0, kept1, keeps0, keeps1, got, send, recv, *traffic,
):
    steps = plan.steps
    sum_over = Summing(plan.first, given, first, traffic)
    k = sum_over.steps
    due = [0, 1] + [2 + (i * (steps - 3)) // max(1, k - 1) for i in range(k)]
    hook = hooks(steps, [(place, functools.partial(sum_over.reduce_stage, at)) for at, place in enumerate(due)])
    step = pl.program_id(0)
    d, inner = cot_t.shape[0], ga0.shape[0]
    ga, gb, big, eurs, eys = (ga0, ga1), (gb0, gb1), (big0, big1), (eur0, eur1), (ey0, ey1)
    kept, keeps = (kept0, kept1), (keeps0, keeps1)

    @pl.when(step == 0)
    def _():
        for ref in (dk, dwrt, dwe, dg2, db2, dg1, db1, dg3, db3):
            ref[...] = jnp.zeros_like(ref)

    left, right = neighbours()
    to_left = send_copy(head, got, send.at[0], recv.at[0], {"seq": left})

    @pl.when(step == 0)
    def _():
        greet([{"seq": left}, {"seq": right}, *sum_over.partners()])
        to_left.start()

    @pl.when(step == steps - 1)
    def _():
        to_left.wait()

    hook(False)
    choose_edge(win_a, after, got, step == steps - 1)
    back = tuple(-s for s in DECODER_SHIFTS)
    stack_taps(stack, back, None, main, win_a, starts, ends, first_place(step, steps), inner)

    def back2(k, fill):
        def emit(rows, value):
            eur[rows, CHAINS[k]] = value
            eurs[k][rows, :] = value

        norm_backward(ga[k], CHAINS[k], inner, g2, z2, d2, r2, dg2, db2, keeps[k], emit, fill, EVERY)

    def back1(k, fill):
        def emit(rows, value):
            total = value + cot_t[rows, CHAINS[k]]
            ey[rows, CHAINS[k]] = total
            eys[k][rows, :] = total

        norm_backward(big[k], CHAINS[k], d, g1, z1, d1, r1, dg1, db1, kept[k], emit, fill, EVERY)

    def back3(k, fill):
        def emit(rows, value):
            evr[rows, CHAINS[k]] = value

        norm_backward(gb[k], CHAINS[k], inner, g3, z3, d3, r3, dg3, db3, keeps[k], emit, fill, EVERY)

    for k in range(2):
        product(ga[k], kb, stack[:, CHAINS[k]])
    by_k = add_product(dk, h2, stack)
    back2(0, by_k[:2])
    big[0][...] = nn_dot(wr[...], eur0[...])
    back2(1, by_k[2:])
    big[1][...] = nn_dot(wr[...], eur1[...])
    by_r = add_product(dwrt, eur, h1)
    back1(0, by_r[:2])
    gb[0][...] = nn_dot(we[...], ey0[...])
    back1(1, by_r[2:])
    gb[1][...] = nn_dot(we[...], ey1[...])
    by_e = add_product(dwe, h3, ey)
    back3(0, by_e[:2])
    back3(1, by_e[2:])

    @pl.when(step == steps - 1)
    def _():
        pack_gradients(packed, plan, ((dk, dk.shape[1]), (dwrt, d + AUG), (dwe, d)), ())

    hook(True)


def enc_back_kernel(
    plan, starts, ends, before, main, after, head, tail, kb, wr, g2, g1,
    h2, z2, d2, r2, h1, z1, d1, r1, ey, given, first_share, *rest,
):
    vecs, rest = rest[:8], rest[8:]
    (
        grad, packed, summed, first_whole,
        dk, dwrt, dg2, db2, dg1, db1,
        stack, win_b, win_a, ga0, ga1, big0, big1, eur, eur0, eur1, kept0, kept1, keeps0, keeps1,
        got_l, got_r, send, recv, result, first_up, first_sem, vec_sem,
    ), rest = rest[:32], rest[32:]
    held, traffic = rest[:8], rest[8:]
    loads = [pltpu.make_async_copy(vecs[at], held[at], vec_sem.at[at]) for at in range(8)]
    steps = plan.steps
    step = pl.program_id(0)
    d, inner = ey.shape[0], ga0.shape[0]
    ga, big, eurs = (ga0, ga1), (big0, big1), (eur0, eur1)
    kept, keeps = (kept0, kept1), (keeps0, keeps1)

    @pl.when(step == 0)
    def _():
        for load in loads:
            load.start()
        for ref in (dk, dwrt, dg2, db2, dg1, db1):
            ref[...] = jnp.zeros_like(ref)

    sum_over = Summing(plan.early, given, summed, traffic)
    trade_edges(step, steps, head, tail, got_l, got_r, send, recv, sum_over.partners())

    k = sum_over.steps
    due = [0, 1] + [3 + (i * (steps - 3)) // max(1, k - 1) for i in range(k)]
    actions = [(place, functools.partial(sum_over.reduce_stage, at)) for at, place in enumerate(due)]
    first = Summing(plan.first, None, result, (None,) * 8 + (first_up, first_sem))

    def begin():
        first.take_share(first_share)
        first.spread_stage(0)

    actions.append((0, begin))
    actions += [(1 + (steps - 2) * (at + 1) // k, functools.partial(first.spread_stage, at + 1)) for at in range(k)]
    hook = hooks(steps, actions)

    hook(False)
    choose_edge(win_b, before, got_l, step == steps - 1)
    choose_edge(win_a, after, got_r, step == steps - 2)
    back = tuple(-s for s in ENCODER_SHIFTS)
    stack_taps(stack, back, win_b, main, win_a, starts, ends, first_place(later_tile(step, steps), steps), inner)

    def back2(k, fill):
        def emit(rows, value):
            eur[rows, CHAINS[k]] = value
            eurs[k][rows, :] = value

        norm_backward(ga[k], CHAINS[k], inner, g2, z2, d2, r2, dg2, db2, keeps[k], emit, fill, EVERY)

    def back1(k, fill):
        def emit(rows, value):
            grad[rows, CHAINS[k]] = value + ey[rows, CHAINS[k]]

        norm_backward(big[k], CHAINS[k], d, g1, z1, d1, r1, dg1, db1, kept[k], emit, fill, EVERY)

    for k in range(2):
        product(ga[k], kb, stack[:, CHAINS[k]])
    by_k = add_product(dk, h2, stack)
    back2(0, by_k[:2])
    big[0][...] = nn_dot(wr[...], eur0[...])
    back2(1, by_k[2:4])
    big[1][...] = nn_dot(wr[...], eur1[...])
    by_r = add_product(dwrt, eur, h1)
    back1(0, by_k[4:])
    back1(1, by_r)

    @pl.when(step == steps - 1)
    def _():
        in_chunks(plan.first.pieces, lambda at, count: copy_pieces(first_whole, result, at, count))
        for load in loads:
            load.wait()
        sums = (dg1, db1, dg2, db2, *held)
        pack_gradients(packed, plan, ((dk, dk.shape[1]), (dwrt, d + AUG)), sums)

    hook(True)


LARGE = (2, 6, 10, 14, 18, 22)
ROWS_OF = 13


def blocks_of(used):
    return -(-used // LANES)


class Part:
    def __init__(self, sections, vectors, streams, n):
        self.starts, at = {}, 0
        for name, used in sections:
            self.starts[name] = (at, used)
            at += blocks_of(used)
        if vectors:
            self.starts["vec"] = (at, LANES)
            at += 1
        self.filled = at * ROWS_OF
        self.streams = streams
        self.per = -(-self.filled // (streams * n)) * n
        self.pieces = streams * self.per
        self.n = n
        self.rounds, base = [], 1
        while base < n:
            radix = 4 if n // base == 4 else 2
            self.rounds.append((base, radix))
            base *= radix


class Plan:
    def __init__(self, d, inner, steps, n):
        self.d, self.inner, self.steps, self.n = d, inner, steps, n
        self.first = Part((("d_we", d),), False, 2, n)
        early = (("d_k", DECODER_TAPS * inner), ("d_wr", d + AUG), ("e_we", d))
        self.early = Part(early, False, 2, n)
        self.late = Part((("e_k", ENCODER_TAPS * inner), ("e_wr", d + AUG)), True, 4, n)


def pack_gradients(packed, plan, mats, vecs):
    d, inner = plan.d, plan.inner
    half = inner // 2
    for w in range(2):
        at = 0
        for ref, used in mats:
            for b in range(blocks_of(used)):
                stop = min(used, LANES * (b + 1))
                lanes = slice(LANES * b, stop)
                for r in range(ROWS_OF):
                    base = half * w + 16 * r
                    if r < ROWS_OF - 1:
                        value = ref[base : base + 16, lanes]
                    else:
                        value = ref[base : base + 8, lanes]
                        low = ref[inner : inner + 8, lanes] if ref.shape[0] > inner else jnp.zeros_like(value)
                        value = jnp.concatenate([value, low], axis=0)
                    if stop - LANES * b < LANES:
                        blank = jnp.zeros((16, LANES * (b + 1) - stop), F32)
                        value = jnp.concatenate([value, blank], axis=1)
                    packed[w, at] = value.astype(BF)
                    at += 1
        if vecs:
            columns = []
            for ref in vecs:
                total = jnp.sum(ref[...], axis=1, keepdims=True)
                if ref.shape[0] == d:
                    columns.append(total[2 * half * w : 2 * half * w + half])
                    columns.append(total[2 * half * w + half : 2 * half * w + 2 * half])
                else:
                    columns.append(total[half * w : half * (w + 1)])
            lane = lax.broadcasted_iota(jnp.int32, (half, LANES), 1)
            value = jnp.zeros((half, LANES), F32)
            for lane_at, column in enumerate(columns):
                value = jnp.where(lane == lane_at, column, value)
            value = jnp.concatenate([value, jnp.zeros((ROWS_OF * 16 - half, LANES), F32)], axis=0)
            for r in range(ROWS_OF):
                packed[w, at] = value[16 * r : 16 * r + 16].astype(BF)
                at += 1
        left = packed.shape[1] - at
        if left:
            packed[w, at : packed.shape[1]] = jnp.zeros((left, 16, LANES), BF)


def in_chunks(count, body):
    size = max(c for c in range(1, 17) if count % c == 0)

    def step(i, _):
        body(i * size, size)
        return 0

    lax.fori_loop(0, count // size, step, 0)


def copy_pieces(dst, src, at, count):
    dst[pl.ds(at, count)] = src[pl.ds(at, count)]


def hooks(steps, actions):
    step = pl.program_id(0)

    def hook(end):
        for place, action in actions:
            if (place >= steps) == end:

                @pl.when(step == min(place, steps - 1))
                def _(action=action):
                    action()

    return hook


class Summing:
    def __init__(self, part, given, out, traffic):
        self.part, self.given, self.out = part, given, out
        self.got, self.total, self.leave, self.landed, self.core, self.down, self.own, self.own_sem, *up = traffic
        self.up, self.share_sem = up if up else (None, None)
        self.me = lax.axis_index("wa")
        self.seq = lax.axis_index("seq")
        self.steps = len(part.rounds)
        self.orders = []
        for s in range(part.streams):
            order = list(range(self.steps))
            if s % 2 and self.steps > 2:
                order[0], order[1] = order[1], order[0]
            if s % 4 > 1 and self.steps > 2:
                order.insert(1, order.pop())
            self.orders.append(order)

    @staticmethod
    def scratch(part):
        sem = pltpu.SemaphoreType.DMA
        steps = max(1, len(part.rounds))
        pieces = (part.pieces, 16, LANES)
        return [
            pltpu.VMEM(pieces, BF),
            pltpu.VMEM(pieces, F32),
            pltpu.VMEM(pieces, BF),
            pltpu.VMEM(pieces, BF),
            sem((2,)),
            sem((2, steps, part.streams, 3)),
            pltpu.VMEM(pieces, BF),
            sem((1,)),
        ]

    @staticmethod
    def spread_scratch(part):
        return [
            pltpu.SemaphoreType.DMA((2, max(1, len(part.rounds)), part.streams, 3)),
            pltpu.SemaphoreType.DMA((part.streams,)),
        ]

    def digit(self, which, by=0):
        base, radix = self.part.rounds[which]
        return lax.rem(lax.div(self.seq, base) + by, radix)

    def others(self, which):
        return range(1, self.part.rounds[which][1])

    def peer(self, which, by):
        base = self.part.rounds[which][0]
        return {"seq": self.seq + (self.digit(which, by) - self.digit(which)) * base}

    def partners(self):
        peers = [self.peer(which, by) for which in range(self.steps) for by in self.others(which)]
        return [{"wa": 1 - self.me}, *peers]

    def range_at(self, s, k):
        start, size, land = s * self.part.per, self.part.per, s * self.part.per
        for i in range(k):
            radix = self.part.rounds[self.orders[s][i]][1]
            size //= radix
            start = start + self.digit(self.orders[s][i]) * size
            if i < k - 1:
                land += (radix - 1) * size
        return start, size, land

    def core_copy(self):
        return send_copy(
            self.given.at[1 - self.me], self.got, self.core.at[0], self.core.at[1], {"wa": 1 - self.me}
        )

    def own_copy(self):
        return pltpu.make_async_copy(self.given.at[self.me], self.own, self.own_sem.at[0])

    def down_copy(self, s, k, by):
        start, _, _ = self.range_at(s, k)
        _, size, land = self.range_at(s, k + 1)
        which = self.orders[s][k]
        return send_copy(
            self.leave.at[pl.ds(start + self.digit(which, by) * size, size)],
            self.landed.at[pl.ds(land + (by - 1) * size, size)],
            self.down.at[0, k, s, by - 1],
            self.down.at[1, k, s, by - 1],
            self.peer(which, by),
        )

    def up_copy(self, s, k, by):
        start, size, _ = self.range_at(s, k + 1)
        ref = self.out.at[pl.ds(start, size)]
        which = self.orders[s][k]
        return send_copy(ref, ref, self.up.at[0, k, s, by - 1], self.up.at[1, k, s, by - 1], self.peer(which, by))

    def add(self, s, k):
        start, size, land = self.range_at(s, k)

        def summed(at, count):
            if k == 0:
                own = self.own[pl.ds(start + at, count)].astype(F32)
                return own + self.got[pl.ds(start + at, count)].astype(F32)
            total = self.total[pl.ds(start + at, count)]
            for by in self.others(self.orders[s][k - 1]):
                total = total + self.landed[pl.ds(land + (by - 1) * size + at, count)].astype(F32)
            return total

        if k == self.steps:

            def finish(at, count):
                self.out[pl.ds(start + at, count)] = summed(at, count).astype(BF)

            in_chunks(size, finish)
            return
        which = self.orders[s][k]
        part = size // self.part.rounds[which][1]
        for by in self.others(which):
            give = self.digit(which, by) * part

            def to_leave(at, count, give=give):
                self.leave[pl.ds(start + give + at, count)] = summed(give + at, count).astype(BF)

            in_chunks(part, to_leave)
            self.down_copy(s, k, by).start()
        own = self.digit(which) * part

        def to_keep(at, count):
            self.total[pl.ds(start + own + at, count)] = summed(own + at, count)

        in_chunks(part, to_keep)

    def reduce_stage(self, at):
        if at == 0:
            self.core_copy().start()
            self.own_copy().start()
            return
        if at == 1:
            self.core_copy().wait()
            self.own_copy().wait()
        for s in range(self.part.streams):
            if at > 1:
                for by in self.others(self.orders[s][at - 2]):
                    self.down_copy(s, at - 2, by).wait()
            self.add(s, at - 1)

    def spread_stage(self, at):
        for s in range(self.part.streams):
            if at > 0:
                for by in self.others(self.orders[s][self.steps - at]):
                    self.up_copy(s, self.steps - at, by).wait()
            if at < self.steps:
                for by in self.others(self.orders[s][self.steps - at - 1]):
                    self.up_copy(s, self.steps - at - 1, by).start()

    def take_share(self, source):
        copies = []
        for s in range(self.part.streams):
            start, size, _ = self.range_at(s, self.steps)
            where = pl.ds(start, size)
            copies.append(pltpu.make_async_copy(source.at[where], self.out.at[where], self.share_sem.at[s]))
            copies[-1].start()
        for copy in copies:
            copy.wait()


def sum_kernel(plan, late_given, early_share, early_out, late_out, *traffic):
    late = Summing(plan.late, late_given, late_out, traffic[:10])
    early = Summing(plan.early, None, early_out, (None,) * 8 + traffic[10:])
    steps = late.steps
    greet(late.partners())
    late.reduce_stage(0)
    early.take_share(early_share)
    early.spread_stage(0)
    late.reduce_stage(1)
    for at in range(steps):
        early.spread_stage(at + 1)
        late.reduce_stage(at + 2)
    for at in range(steps + 1):
        late.spread_stage(at)


def finish_kernel(plan, grad_low, first, early, late, grad, *rest):
    results, large, stored = list(rest[:24]), rest[24:30], rest[30]
    outs, copies = list(results), []
    for at, place in enumerate(LARGE):
        outs[place] = large[at]
        copies.append(pltpu.make_async_copy(large[at], results[place], stored.at[at]))
    d, inner = plan.d, plan.inner
    half = inner // 2
    grad[...] = grad_low[...].astype(F32)

    @pl.when(pl.program_id(0) == 0)
    def _():
        me = lax.axis_index("wa")

        def matrix(name):
            for part, ref in ((plan.first, first), (plan.early, early), (plan.late, late)):
                if name in part.starts:
                    break
            begin, used = part.starts[name]
            parts = []
            for b in range(begin, begin + blocks_of(used)):
                value = ref[b * ROWS_OF : (b + 1) * ROWS_OF].reshape(ROWS_OF * 16, LANES)
                parts.append(value.astype(F32))
            return jnp.concatenate(parts, axis=1)

        def my_half(line, size):
            return jnp.where(me == 0, line[:, 0:size], line[:, size : 2 * size])

        turned = matrix("vec")[0:half].T

        def write(ref, pieces):
            ref[...] = jnp.concatenate(pieces, axis=1).reshape(ref.shape)

        for side, taps in enumerate((ENCODER_TAPS, DECODER_TAPS)):
            tag = "ed"[side]
            first_g, first_b, red_w, red_b, mid_g, mid_b, ker, ker_b, last_g, last_b, exp_w, exp_b = outs[
                12 * side : 12 * side + 12
            ]
            at = 8 * side
            write(first_g, [turned[at : at + 1], turned[at + 1 : at + 2]])
            write(first_b, [turned[at + 2 : at + 3], turned[at + 3 : at + 4]])
            write(mid_g, [turned[at + 4 : at + 5]])
            write(mid_b, [turned[at + 5 : at + 6]])
            write(last_g, [turned[at + 6 : at + 7]])
            write(last_b, [turned[at + 7 : at + 8]])
            value = matrix(tag + "_we")
            exp_w[...] = value[0:half, 0:d]
            write(exp_b, [my_half(value[half : half + 1, 0:d], d // 2)])
            value = matrix(tag + "_k")
            for j in range(taps):
                ker[j] = jnp.concatenate([value[0:half, place] for _, place in tap_pieces(j, taps, inner)], axis=1)
            centre = (ENCODER_SHIFTS if side == 0 else DECODER_SHIFTS).index(0)
            sums = [value[half : half + 1, place] for _, place in tap_pieces(centre, taps, inner)]
            write(ker_b, [my_half(jnp.concatenate(sums, axis=1), half)])
            value = matrix(tag + "_wr")[0:half]
            red_w[...] = value[:, 0:d]
            write(red_b, [value[:, d:].T[0:1]])
            for copy in copies[3 * side : 3 * side + 3]:
                copy.start()

    @pl.when(pl.program_id(0) == plan.steps - 1)
    def _():
        for copy in copies:
            copy.wait()


def local(n, stream, doc_start, doc_end, cotangent, *weights):
    rows, d = stream.shape[1], stream.shape[2]
    inner = weights[6].shape[1] * 2
    steps = rows // TILE
    x, cot = stream[0].T, cotangent[0].T
    starts, ends = doc_start, doc_end
    weights = [w.T if at % 12 == 2 else w for at, w in enumerate(weights)]
    enc, dec = gather_weights(weights, d, inner)
    wrt_e, kt_e, wet_e, we_e, kb_e, wr_e, g1_e, f1_e, b1_e, g2_e, f2_e, b2_e, g3_e, f3_e, b3_e = enc
    wrt_d, kt_d, wet_d, we_d, kb_d, wr_d, g1_d, f1_d, b1_d, g2_d, f2_d, b2_d, g3_d, f3_d, b3_d = dec

    plan = Plan(d, inner, steps, n)
    blocks = rows // LANES
    per = TILE // LANES

    def spec(a):
        return whole(a.shape)

    def wide(channels, dtype=BF):
        return jax.ShapeDtypeStruct((channels, rows), dtype)

    def fixed(shape, dtype=F32):
        return jax.ShapeDtypeStruct(shape, dtype)

    class Order:
        def __init__(self, first):
            self.tile = lambda i: (i + first) % steps

        def cols(self, channels):
            return pl.BlockSpec((channels, TILE), lambda i: (0, self.tile(i)))

        def before(self, channels):
            return pl.BlockSpec((channels, LANES), lambda i: (0, (per * self.tile(i) + blocks - 1) % blocks))

        def after(self, channels):
            return pl.BlockSpec((channels, LANES), lambda i: (0, (per * self.tile(i) + per) % blocks))

    def head(channels):
        return pl.BlockSpec((channels, LANES), lambda i: (0, 0))

    def tail(channels):
        return pl.BlockSpec((channels, LANES), lambda i: (0, blocks - 1))

    plain, later = Order(0), Order(1)
    d1, i1 = d + AUG, inner + AUG
    norm_wide = [(d1, BF), (d, BF), (d, BF), (8, F32)]
    norm_in = [(i1, BF), (inner, BF), (inner, BF), (8, F32)]
    sem = pltpu.SemaphoreType.DMA
    vmem = pltpu.VMEM
    anywhere = pl.BlockSpec(memory_space=pl.ANY)

    def outs_of(order, items):
        return [wide(c, t) for c, t in items], [order.cols(c) for c, _ in items]

    shapes, specs = outs_of(plain, norm_wide + norm_in)
    ins = [wrt_e, f1_e, b1_e, f2_e, b2_e]
    h1e, z1e, d1e, r1e, h2e, z2e, d2e, r2e = pl.pallas_call(
        enc_in_kernel,
        grid=(steps,),
        out_shape=shapes,
        in_specs=[plain.cols(d)] + [spec(a) for a in ins],
        out_specs=specs,
        scratch_shapes=[vmem((d, TILE), F32)] + [vmem((inner, HALF), F32)] * 2 + [vmem((d1, HALF), BF)] * 2,
        compiler_params=params(),
        name="encoder_in",
    )(x, *ins)

    shapes, specs = outs_of(later, norm_in + [(d, BF)] + norm_wide + norm_in)
    ins = [kt_e, wet_e, wrt_d, f3_e, b3_e, f1_d, b1_d, f2_d, b2_d]
    h3e, z3e, d3e, r3e, x1, h1d, z1d, d1d, r1d, h2d, z2d, d2d, r2d, edge_d = pl.pallas_call(
        functools.partial(enc_out_kernel, steps),
        grid=(steps,),
        out_shape=shapes + [fixed((i1, LANES), BF)],
        in_specs=[later.cols(1), later.cols(1), later.before(i1), later.cols(i1), later.after(i1)]
        + [head(i1), tail(i1), later.cols(d)]
        + [spec(a) for a in ins],
        out_specs=specs + [whole((i1, LANES))],
        scratch_shapes=[
            vmem((ENCODER_TAPS * inner + AUG, TILE), BF),
            vmem((inner, LANES), BF),
            vmem((inner, LANES), BF),
        ]
        + [vmem((inner, HALF), F32)] * 2
        + [vmem((d, HALF), F32)] * 2
        + [vmem((inner, HALF), F32)] * 2
        + [vmem((i1, HALF), BF)] * 2
        + [vmem((d1, HALF), BF)] * 2
        + [vmem((i1, LANES), BF)] * 4
        + [sem((3,)), sem((3,))],
        compiler_params=params(1),
        name="encoder_out",
    )(starts, ends, h2e, h2e, h2e, h2e, h2e, x, *ins)

    small, large = fixed((inner, LANES)), fixed((d, LANES))
    sums = [fixed((2, plan.first.pieces, 16, LANES), BF), small, small]
    ins = [kt_d, we_d, wet_d, f3_d, b3_d, g3_d]
    out, evr_d, packed_first, dg3_d, db3_d = pl.pallas_call(
        functools.partial(dec_out_kernel, plan),
        grid=(steps,),
        out_shape=[wide(d, F32), wide(inner)] + sums,
        in_specs=[plain.cols(1), plain.cols(1), plain.before(i1), plain.cols(i1), spec(edge_d)]
        + [plain.cols(d), plain.cols(d)]
        + [spec(a) for a in ins],
        out_specs=[plain.cols(d), plain.cols(inner)] + [whole(s.shape) for s in sums],
        scratch_shapes=[
            vmem((i1, d), F32),
            vmem((DECODER_TAPS * inner + AUG, TILE), BF),
            vmem((inner, LANES), BF),
            vmem((inner, HALF), F32),
            vmem((inner, HALF), F32),
            vmem((i1, TILE), BF),
            vmem((inner, TILE), BF),
            vmem((inner, TILE), BF),
            vmem((8, TILE), F32),
        ]
        + [vmem((inner, HALF), F32)] * 2
        + [vmem((inner, HALF), BF)] * 2
        + [vmem((i1, HALF), BF)] * 2,
        compiler_params=params(),
        name="decoder_out",
    )(starts, ends, h2d, h2d, edge_d, cot, x1, *ins)

    shapes, specs = outs_of(plain, [(d, BF), (inner, BF)])
    early = fixed((2, plan.early.pieces, 16, LANES), BF)
    first = fixed((plan.first.pieces, 16, LANES), BF)
    sums = [small, small, large, large, small, small]
    ins = [kb_d, wr_d, we_e, g2_d, g1_d, g3_e]
    stash = [h2d, z2d, d2d, r2d, h1d, z1d, d1d, r1d, cot, h3e, z3e, d3e, r3e]
    ey, evr_e, packed, first_share, dg2_d, db2_d, dg1_d, db1_d, dg3_e, db3_e = pl.pallas_call(
        functools.partial(dec_back_kernel, plan),
        grid=(steps,),
        out_shape=shapes + [early, first] + sums,
        in_specs=[plain.cols(1), plain.cols(1), plain.cols(inner), plain.after(inner), head(inner)]
        + [spec(a) for a in ins]
        + [plain.cols(a.shape[0]) for a in stash]
        + [anywhere],
        out_specs=specs + [whole(early.shape), whole(first.shape)] + [whole(s.shape) for s in sums],
        scratch_shapes=[
            vmem((i1, DECODER_TAPS * inner), F32),
            vmem((inner, d1), F32),
            vmem((i1, d), F32),
            vmem((DECODER_TAPS * inner, TILE), BF),
            vmem((inner, LANES), BF),
        ]
        + [vmem((inner, HALF), F32)] * 4
        + [vmem((d, HALF), F32)] * 2
        + [vmem((inner, TILE), BF)]
        + [vmem((inner, HALF), BF)] * 2
        + [vmem((d, HALF), BF)] * 4
        + [vmem((inner, HALF), BF)] * 2
        + [vmem((inner, LANES), BF), sem((1,)), sem((1,))]
        + Summing.scratch(plan.first),
        compiler_params=params(2),
        name="decoder_back",
    )(starts, ends, evr_d, evr_d, evr_d, *ins, *stash, packed_first)

    late = fixed((2, plan.late.pieces, 16, LANES), BF)
    early_sum = fixed((plan.early.pieces, 16, LANES), BF)
    ins = [kb_e, wr_e, g2_e, g1_e]
    stash = [h2e, z2e, d2e, r2e, h1e, z1e, d1e, r1e, ey]
    vecs = [dg3_e, db3_e, dg1_d, db1_d, dg2_d, db2_d, dg3_d, db3_d]
    grad_low, packed_late, summed, first_whole = pl.pallas_call(
        functools.partial(enc_back_kernel, plan),
        grid=(steps,),
        out_shape=[wide(d), late, early_sum, first],
        in_specs=[later.cols(1), later.cols(1), later.before(inner), later.cols(inner), later.after(inner)]
        + [head(inner), tail(inner)]
        + [spec(a) for a in ins]
        + [later.cols(a.shape[0]) for a in stash]
        + [anywhere] * (2 + len(vecs)),
        out_specs=[later.cols(d), whole(late.shape), whole(early_sum.shape), whole(first.shape)],
        scratch_shapes=[
            vmem((i1, ENCODER_TAPS * inner), F32),
            vmem((inner, d1), F32),
            vmem((inner, LANES), F32),
            vmem((inner, LANES), F32),
            vmem((d, LANES), F32),
            vmem((d, LANES), F32),
            vmem((ENCODER_TAPS * inner, TILE), BF),
            vmem((inner, LANES), BF),
            vmem((inner, LANES), BF),
        ]
        + [vmem((inner, HALF), F32)] * 2
        + [vmem((d, HALF), F32)] * 2
        + [vmem((inner, TILE), BF)]
        + [vmem((inner, HALF), BF)] * 2
        + [vmem((d, HALF), BF)] * 2
        + [vmem((inner, HALF), BF)] * 2
        + [vmem((inner, LANES), BF)] * 2
        + [sem((2,)), sem((2,)), vmem(first.shape, BF)]
        + Summing.spread_scratch(plan.first)
        + [sem((8,))]
        + [vmem(a.shape, F32) for a in vecs]
        + Summing.scratch(plan.early),
        compiler_params=params(3),
        name="encoder_back",
    )(starts, ends, evr_e, evr_e, evr_e, evr_e, evr_e, *ins, *stash, packed, first_share, *vecs)

    vm = pl.BlockSpec(memory_space=pltpu.VMEM)
    early_whole, late_whole = pl.pallas_call(
        functools.partial(sum_kernel, plan),
        out_shape=[early_sum, fixed((plan.late.pieces, 16, LANES), BF)],
        in_specs=[anywhere, anywhere],
        out_specs=[vm, vm],
        scratch_shapes=Summing.scratch(plan.late)
        + Summing.spread_scratch(plan.late)
        + Summing.spread_scratch(plan.early),
        compiler_params=params(4),
        name="sum_gradients",
    )(packed_late, summed)

    grad, *shares = pl.pallas_call(
        functools.partial(finish_kernel, plan),
        grid=(steps,),
        out_shape=[wide(d, F32)] + [fixed(w.shape) for w in weights],
        in_specs=[plain.cols(d), whole(first_whole.shape), whole(early_whole.shape), whole(late_whole.shape)],
        out_specs=[plain.cols(d)]
        + [pl.BlockSpec(memory_space=pl.ANY) if at in LARGE else whole(w.shape) for at, w in enumerate(weights)],
        scratch_shapes=[vmem(weights[at].shape, F32) for at in LARGE] + [sem((len(LARGE),))],
        compiler_params=params(),
        name="finish",
    )(grad_low, first_whole, early_whole, late_whole)
    shares = [w.T if at % 12 == 2 else w for at, w in enumerate(shares)]
    return (out.T[None], grad.T[None], *shares)


def solution(mesh):
    rows = P("wa", "seq", None)
    block = (
        P("wa"), P("wa"), P(None, "wa"), P("wa"), P("wa"), P("wa"),
        P(None, "wa", None), P("wa"), P("wa"), P("wa"), P("wa", None), P("wa"),
    )
    return jax.shard_map(
        functools.partial(local, mesh.shape["seq"]),
        mesh=mesh,
        in_specs=(rows, P("wa", "seq"), P("wa", "seq"), rows, *block, *block),
        out_specs=(rows, rows, *block, *block),
        check_vma=False,
    )
```

```python
import functools

import jax
import jax.numpy as jnp
from jax import lax
from jax.experimental import pallas as pl
from jax.experimental.pallas import tpu as pltpu
from jax.sharding import PartitionSpec as P

ENCODER_TAPS = 5
ENCODER_DILATION = 8
DECODER_TAPS = 3
DECODER_DILATION = 16
EPS = 1e-05

MESH = pl.DeviceIdType.MESH
BF = jnp.bfloat16
F32 = jnp.float32
LANES = 128
TILE = 512
HALF = 256
AUG = 16
VMEM_LIMIT = 56 * 1024 * 1024
GELU_1 = 2.0 * 0.7978845608028654
GELU_3 = 8.0 * 0.7978845608028654 * 0.044715

ENCODER_SHIFTS = tuple(ENCODER_DILATION * (j - ENCODER_TAPS // 2) for j in range(ENCODER_TAPS))
DECODER_SHIFTS = tuple(-DECODER_DILATION * (DECODER_TAPS - 1 - j) for j in range(DECODER_TAPS))


def params(collective=None):
    if collective is None:
        return pltpu.CompilerParams(vmem_limit_bytes=VMEM_LIMIT)
    return pltpu.CompilerParams(
        vmem_limit_bytes=VMEM_LIMIT, collective_id=collective, has_side_effects=True
    )


def whole(shape):
    return pl.BlockSpec(shape, lambda *_: (0,) * len(shape))


def nt_dot(left, right):
    return lax.dot_general(left, right, (((1,), (1,)), ((), ())), preferred_element_type=F32)


def nn_dot(left, right):
    return jnp.dot(left, right, preferred_element_type=F32)


def product(out, left, right, extra=None):
    rows = out.shape[0]
    middle = (rows // 2 + 15) // 16 * 16
    for a, b in ((0, middle), (middle, rows)):
        value = nn_dot(left[a:b, :], right)
        out[a:b, :] = value if extra is None else value + extra[a:b, :].astype(F32)


def lanes_of(column, width):
    return jnp.concatenate([column] * (width // LANES), axis=1)


def fold(value):
    total = value[:, :LANES]
    for at in range(LANES, value.shape[1], LANES):
        total = total + value[:, at : at + LANES]
    return total


def weights_kernel(dims, *refs):
    d, inner, taps = dims
    n_in = 24
    ins, refs = refs[:n_in], refs[n_in:]
    results, refs = refs[:30], refs[30:]
    outs, refs = refs[:30], refs[30:]
    (small_own, small_got, k_own0, k_own1, e_own0, e_own1, r_own0, r_own1, *rest) = refs
    (r_got0, r_got1, k_got0, k_got1, e_got0, e_got1, k_all, send, recv, store) = rest
    me = lax.axis_index("wa")
    other = 1 - me
    barrier = pltpu.get_barrier_semaphore()
    pl.semaphore_signal(barrier, inc=1, device_id={"wa": other}, device_id_type=MESH)
    pl.semaphore_wait(barrier, 1)

    half = inner // 2
    pad = k_own0.shape[1]
    small_own[...] = jnp.zeros_like(small_own)
    small_at = []
    for side in range(2):
        for at in (0, 1, 3, 4, 5, 7, 8, 9, 11):
            small_at.append(12 * side + at)
    for row, at in enumerate(small_at):
        n = ins[at].shape[0]
        small_own[row : row + 1, 0:n] = ins[at][...].astype(F32).reshape(1, n)
    owns, gots = [], []
    for side, (k_own, e_own, r_own) in enumerate(((k_own0, e_own0, r_own0), (k_own1, e_own1, r_own1))):
        base = 12 * side
        k_own[:, half - 8 : pad, :] = jnp.zeros((taps[side], pad - half + 8, inner), BF)
        k_own[:, 0:half, :] = ins[base + 6][...]
        e_own[half - 8 : pad, :] = jnp.zeros((pad - half + 8, d), BF)
        e_own[0:half, :] = ins[base + 10][...]
        r_own[half - 8 : pad, :] = jnp.zeros((pad - half + 8, d), BF)
        r_own[0:half, :] = ins[base + 2][...]
        owns += [r_own, k_own, e_own]
    owns.append(small_own)
    gots = [r_got0, k_got0, e_got0, r_got1, k_got1, e_got1, small_got]
    copies = []
    pairs = list(zip(owns, gots))
    for at in (6, 0, 2, 1, 3, 5, 4):
        own, got = pairs[at]
        copies.append(
            pltpu.make_async_remote_copy(
                src_ref=own,
                dst_ref=got,
                send_sem=send.at[at],
                recv_sem=recv.at[at],
                device_id={"wa": other},
                device_id_type=MESH,
            )
        )
        copies[-1].start()
    arrival = dict(zip((6, 0, 2, 1, 3, 5, 4), copies))
    stores = []

    def keep(at):
        stores.append(pltpu.make_async_copy(outs[at], results[at], store.at[at]))
        stores[-1].start()

    first_core = me == 0
    square = (HALF, HALF)
    unit = lax.broadcasted_iota(jnp.int32, square, 0) == lax.broadcasted_iota(jnp.int32, square, 1)
    unit = jnp.where(unit, 1.0, 0.0).astype(BF)

    def turn(out, columns, count, width=None):
        for a in range(0, count, HALF):
            b = min(a + HALF, count)
            piece = nt_dot(unit[0 : b - a, 0 : b - a], columns(a, b)).astype(BF)
            if width is None:
                out[a:b, :] = piece
            else:
                out[a:b, 0:width] = piece

    def ordered(own, got):
        own, got = own.astype(F32), got.astype(F32)
        return jnp.where(first_core, own, got), jnp.where(first_core, got, own)

    arrival[6].wait()
    small0, small1 = ordered(small_own[...], small_got[...])

    def column(row, n):
        line = jnp.concatenate([small0[row : row + 1, 0 : n // 2], small1[row : row + 1, 0 : n // 2]], axis=1)
        return jnp.broadcast_to(line, (LANES, n)).T

    def bias_columns(value):
        where = lax.broadcasted_iota(jnp.int32, (value.shape[0], AUG), 1) == 0
        return jnp.where(where, value[:, :AUG], 0.0).astype(BF)

    for side in range(2):
        o = outs[15 * side : 15 * side + 15]
        wrt, kt, wet, we, kb, wr, *vectors = o
        base = 9 * side
        for at, (row, n) in enumerate(((0, d), (3, inner), (6, inner))):
            gain, half_gain, half_bias = vectors[3 * at : 3 * at + 3]
            gain[...] = column(base + row, n)
            half_gain[...] = gain[...] * 0.5
            half_bias[...] = column(base + row + 1, n) * 0.5
        n = taps[side]
        first = 15 * side
        for at in range(6, 15):
            keep(first + at)
        arrival[3 * side].wait()
        r0, r1 = ordered(owns[3 * side][0:half, :], gots[3 * side][0:half, :])
        wrt[:, 0:d] = jnp.concatenate([r0, r1], axis=0).astype(BF)
        wrt[:, d : d + AUG] = bias_columns(column(base + 2, inner))
        keep(first)
        turn(wr, lambda a, b: wrt[:, a:b], d)
        keep(first + 5)
        arrival[3 * side + 2].wait()
        e0, e1 = ordered(owns[3 * side + 2][0:half, :], gots[3 * side + 2][0:half, :])
        we[...] = jnp.concatenate([e0, e1], axis=0).astype(BF)
        keep(first + 3)
        turn(wet, lambda a, b: we[:, a:b], d, inner)
        wet[:, inner : inner + AUG] = bias_columns(column(base + 8, d))
        keep(first + 2)
        arrival[3 * side + 1].wait()
        for j in range(n):
            k0, k1 = ordered(owns[3 * side + 1][j, 0:half, :], gots[3 * side + 1][j, 0:half, :])
            k = jnp.concatenate([k0, k1], axis=0).astype(BF)
            for channels, place in tap_pieces(j, n, inner):
                kb[:, place] = k[:, channels]
                k_all[place, :] = k[channels, :]
        keep(first + 4)
        turn(kt, lambda a, b: k_all[0 : n * inner, a:b], inner, n * inner)
        kt[:, n * inner : n * inner + AUG] = bias_columns(column(base + 5, inner))
        keep(first + 1)
    for copy in stores:
        copy.wait()


def gather_weights(args, d, inner):
    taps = (ENCODER_TAPS, DECODER_TAPS)
    half = inner // 2
    pad = -(-half // 16) * 16
    shapes = []
    for n in taps:
        shapes += [
            ((inner, d + AUG), BF),
            ((inner, n * inner + AUG), BF),
            ((d, inner + AUG), BF),
            ((inner, d), BF),
            ((inner, n * inner), BF),
            ((d, inner), BF),
        ]
        for c in (d, inner, inner):
            shapes += [((c, LANES), F32)] * 3
    vm = pl.BlockSpec(memory_space=pltpu.VMEM)
    small = pltpu.VMEM((24, 512), F32)
    kk = [pltpu.VMEM((n, pad, inner), BF) for n in taps]
    ee = [pltpu.VMEM((pad, d), BF)] * 2
    outs = pl.pallas_call(
        functools.partial(weights_kernel, (d, inner, taps)),
        out_shape=[jax.ShapeDtypeStruct(*s) for s in shapes],
        in_specs=[vm] * 24,
        out_specs=[pl.BlockSpec(memory_space=pl.ANY)] * 30,
        scratch_shapes=[pltpu.VMEM(*shape) for shape in shapes]
        + [small, small, *kk, *ee, *ee, *ee, *kk, *ee]
        + [pltpu.VMEM((taps[0] * inner, inner), BF)]
        + [pltpu.SemaphoreType.DMA((7,)), pltpu.SemaphoreType.DMA((7,)), pltpu.SemaphoreType.DMA((30,))],
        compiler_params=params(0),
        name="gather_weights",
    )(*args)
    return outs[:15], outs[15:]


def pacing(thunks, slots):
    state = [0, 0]
    thunks = list(thunks)

    def between():
        while state[1] < len(thunks) and state[0] * len(thunks) >= state[1] * slots:
            thunks[state[1]]()
            state[1] += 1
        state[0] += 1

    return between


def add_product(total, left, right):
    def piece(at, stop):
        total[:, at:stop] += nt_dot(left[...], right[at:stop, :])

    columns = right.shape[0]
    return [functools.partial(piece, at, min(at + HALF, columns)) for at in range(0, columns, HALF)]


def norm_forward(src, lanes, channels, gain, bias, h_out, z_out, d_out, r_out, keep=None, fill=(), at=None, h_copy=None):
    width = lanes.stop - lanes.start
    between = pacing(fill, 3 * (channels // 16))
    total = [jnp.zeros((8, width), F32) for _ in range(4)]
    for c in range(0, channels, 16):
        between()
        x = src[c : c + 16, at or lanes].astype(F32)
        if keep is not None:
            keep[c : c + 16, at or lanes] = x
        k = (c // 8) % 4
        total[k] = total[k] + x[0:8]
        total[k + 1] = total[k + 1] + x[8:16]
    mean = jnp.sum((total[0] + total[1]) + (total[2] + total[3]), axis=0, keepdims=True) * (1.0 / channels)
    wide = jnp.broadcast_to(mean, (16, width))
    values = src if keep is None else keep
    total = [jnp.zeros((8, width), F32) for _ in range(4)]
    for c in range(0, channels, 16):
        between()
        centre = values[c : c + 16, at or lanes] - wide
        square = centre * centre
        k = (c // 8) % 4
        total[k] = total[k] + square[0:8]
        total[k + 1] = total[k + 1] + square[8:16]
    spread = jnp.sum((total[0] + total[1]) + (total[2] + total[3]), axis=0, keepdims=True) * (1.0 / channels)
    r = lax.rsqrt(spread + EPS)
    if r_out is not None:
        r_out[:, lanes] = jnp.broadcast_to(r, (8, width))
    rw = jnp.broadcast_to(r, (16, width))
    mw = jnp.broadcast_to(mean * r, (16, width))
    one, point = BF(1.0), BF(0.5)
    for c in range(0, channels, 16):
        between()
        rows = slice(c, c + 16)
        z = values[rows, at or lanes] * rw - mw
        half = (z * lanes_of(gain[rows, :], width) + lanes_of(bias[rows, :], width)).astype(BF)
        sq = half * half
        t = jnp.tanh(half * (sq * BF(GELU_3) + BF(GELU_1)))
        up = one + t
        h = half * up
        h_out[rows, lanes] = h
        if h_copy is not None:
            h_copy[rows, :] = h
        d_out[rows, lanes] = point * up + h * ((one - t) * (sq * BF(1.5 * GELU_3) + BF(0.5 * GELU_1)))
        z_out[rows, lanes] = z.astype(BF)


def norm_backward(grad, lanes, channels, gain, z_in, d_in, r_in, gain_sum, bias_sum, keep, emit, fill=(), at=None):
    width = lanes.stop - lanes.start
    between = pacing(fill, 2 * (channels // 16))
    one = [jnp.zeros((8, width), F32) for _ in range(2)]
    two = [jnp.zeros((8, width), F32) for _ in range(2)]
    r = r_in[0:1, lanes]
    rw = jnp.broadcast_to(r, (16, width))
    for c in range(0, channels, 16):
        between()
        rows = slice(c, c + 16)
        da = grad[rows, at or lanes] * d_in[rows, lanes].astype(F32)
        p = da * z_in[rows, lanes].astype(F32)
        bias_sum[rows, :] += fold(da)
        gain_sum[rows, :] += fold(p)
        wide = lanes_of(gain[rows, :], width)
        dz = da * wide
        q = p * wide
        keep[rows, at or lanes] = (dz * rw).astype(BF)
        for k in range(2):
            one[k] = one[k] + dz[8 * k : 8 * k + 8]
            two[k] = two[k] + q[8 * k : 8 * k + 8]
    scale = r * (1.0 / channels)
    m1 = jnp.broadcast_to(jnp.sum(one[0] + one[1], axis=0, keepdims=True) * scale, (16, width)).astype(BF)
    m2 = jnp.broadcast_to(jnp.sum(two[0] + two[1], axis=0, keepdims=True) * scale, (16, width)).astype(BF)
    for c in range(0, channels, 16):
        between()
        rows = slice(c, c + 16)
        emit(rows, keep[rows, at or lanes] - (z_in[rows, lanes] * m2 + m1))


def tap_mask(starts, ends, first, shift):
    place = first + shift + lax.broadcasted_iota(jnp.int32, (8, TILE), 1)
    usable = (place >= jnp.broadcast_to(starts[...], (8, TILE))) & (place < jnp.broadcast_to(ends[...], (8, TILE)))
    one = jnp.where(usable, 1.0, 0.0)
    return jnp.concatenate([one, one], axis=0).astype(BF)


def tap_row(j, c, taps, inner):
    aligned = inner // LANES * LANES
    return j * aligned + c if c < aligned else taps * aligned + j * (inner - aligned) + c - aligned


def tap_pieces(j, taps, inner):
    aligned = inner // LANES * LANES
    for a, b in ((0, aligned), (aligned, inner)):
        at = tap_row(j, a, taps, inner)
        yield slice(a, b), slice(at, at + b - a)


def stack_taps(stack, shifts, before, main, after, starts, ends, first, inner):
    for j, shift in enumerate(shifts):
        if not shift:
            for channels, place in tap_pieces(j, len(shifts), inner):
                stack[place, :] = main[channels, :]
            continue
        mask = tap_mask(starts, ends, first, shift)
        for c in range(0, inner, 16):
            rows = slice(c, c + 16)
            if shift < 0:
                span = jnp.concatenate([before[rows, :], main[rows, :]], axis=1)
                span = pltpu.roll(span, -shift, 1)[:, LANES:]
            else:
                span = jnp.concatenate([main[rows, :], after[rows, :]], axis=1)
                span = pltpu.roll(span, TILE + LANES - shift, 1)[:, :TILE]
            at = tap_row(j, c, len(shifts), inner)
            stack[at : at + 16, :] = span * mask


def ones_rows(width):
    where = lax.broadcasted_iota(jnp.int32, (AUG, width), 0) == 0
    return jnp.where(where, 1.0, 0.0).astype(BF)


def neighbours():
    me = lax.axis_index("seq")
    n = lax.axis_size("seq")
    return lax.rem(me + n - 1, n), lax.rem(me + 1, n)


def greet(others):
    barrier = pltpu.get_barrier_semaphore()
    for device in others:
        pl.semaphore_signal(barrier, inc=1, device_id=device, device_id_type=MESH)
    pl.semaphore_wait(barrier, len(others))


def send_copy(src, dst, send_sem, recv_sem, device):
    return pltpu.make_async_remote_copy(
        src_ref=src, dst_ref=dst, send_sem=send_sem, recv_sem=recv_sem, device_id=device, device_id_type=MESH
    )


def later_tile(step, steps):
    return lax.rem(step + 1, steps)


def first_place(tile, steps):
    return lax.axis_index("seq") * (steps * TILE) + tile * TILE


CHAINS = (slice(0, HALF), slice(HALF, TILE))
EVERY = slice(0, HALF)


def enc_in_kernel(x, wrt, g1, b1, g2, b2, h1, z1, d1, r1, h2, z2, d2, r2, xt, u0, u1, h_wide0, h_wide1):
    d, inner = x.shape[0], wrt.shape[0]
    h1[d : d + AUG, :] = ones_rows(TILE)
    h2[inner : inner + AUG, :] = ones_rows(TILE)
    u, h_wide = (u0, u1), (h_wide0, h_wide1)
    for k in range(2):
        h_wide[k][d : d + AUG, :] = ones_rows(HALF)
        norm_forward(x, CHAINS[k], d, g1, b1, h1, z1, d1, r1, xt, h_copy=h_wide[k])
        product(u[k], wrt, h_wide[k][...])
    for k in range(2):
        norm_forward(u[k], CHAINS[k], inner, g2, b2, h2, z2, d2, r2, at=EVERY)


def choose_edge(window, block, edge, at_end):
    window[...] = block[0 : window.shape[0], :]

    @pl.when(at_end)
    def _():
        window[...] = edge[0 : window.shape[0], :]


def trade_edges(step, steps, head, tail, got_l, got_r, send, recv, others=()):
    left, right = neighbours()
    to_left = send_copy(head, got_r, send.at[0], recv.at[0], {"seq": left})
    to_right = send_copy(tail, got_l, send.at[1], recv.at[1], {"seq": right})

    @pl.when(step == 0)
    def _():
        greet([{"seq": left}, {"seq": right}, *others])
        to_left.start()
        to_right.start()

    @pl.when(step == steps - 2)
    def _():
        to_left.wait()
        to_right.wait()


def enc_out_kernel(
    steps, starts, ends, before, main, after, head, tail, xt, kt, wet, wrt, g3, b3, g1, b1, g2, b2,
    h3, z3, d3, r3, x1, h1, z1, d1, r1, h2, z2, d2, r2, edge_o,
    stack, win_b, win_a, v0, v1, y0, y1, u0, u1, h_in0, h_in1, h_wide0, h_wide1, got_l, got_r, own, got, send, recv,
):
    step = pl.program_id(0)
    d, inner = xt.shape[0], v0.shape[0]
    v, y, u, h_in, h_wide = (v0, v1), (y0, y1), (u0, u1), (h_in0, h_in1), (h_wide0, h_wide1)
    trade_edges(step, steps, head, tail, got_l, got_r, send, recv)
    choose_edge(win_b, before, got_l, step == steps - 1)
    choose_edge(win_a, after, got_r, step == steps - 2)
    stack_taps(stack, ENCODER_SHIFTS, win_b, main, win_a, starts, ends, first_place(later_tile(step, steps), steps), inner)
    stack[len(ENCODER_SHIFTS) * inner :, :] = ones_rows(TILE)
    h3[inner : inner + AUG, :] = ones_rows(TILE)
    h1[d : d + AUG, :] = ones_rows(TILE)
    h2[inner : inner + AUG, :] = ones_rows(TILE)
    one, two = CHAINS

    def make_v(k):
        product(v[k], kt, stack[:, CHAINS[k]])

    def make_y(k):
        product(y[k], wet, h_in[k][...], xt[:, CHAINS[k]])

    def make_u(k):
        product(u[k], wrt, h_wide[k][...])

    def norm_last(k):
        norm_forward(v[k], CHAINS[k], inner, g3, b3, h3, z3, d3, r3, at=EVERY, h_copy=h_in[k])

    def norm_first(k):
        for c in range(0, d, 16):
            x1[c : c + 16, CHAINS[k]] = y[k][c : c + 16, :].astype(BF)
        norm_forward(y[k], CHAINS[k], d, g1, b1, h1, z1, d1, r1, at=EVERY, h_copy=h_wide[k])

    def norm_mid(k):
        norm_forward(u[k], CHAINS[k], inner, g2, b2, h2, z2, d2, r2, at=EVERY)

    for k in range(2):
        h_in[k][inner : inner + AUG, :] = ones_rows(HALF)
        h_wide[k][d : d + AUG, :] = ones_rows(HALF)
    make_v(0)
    make_v(1)
    norm_last(0)
    make_y(0)
    norm_last(1)
    make_y(1)
    norm_first(0)
    make_u(0)
    norm_first(1)
    make_u(1)
    norm_mid(0)
    norm_mid(1)

    def give():
        return send_copy(own, got, send.at[2], recv.at[2], {"seq": neighbours()[1]})

    @pl.when(step == steps - 2)
    def _():
        own[...] = h2[:, TILE - LANES : TILE]
        give().start()

    @pl.when(step == steps - 1)
    def _():
        give().wait()
        edge_o[...] = got[...]


def dec_out_kernel(
    plan, starts, ends, before, main, e_l, cot_t, x1, kt, we, wet, f3, b3, g3,
    out, evr, packed, dg3, db3,
    dwe, stack, win_b, v0, v1, h3, z3, d3, r3, g0, g1, kept0, kept1, h_in0, h_in1,
):
    steps = plan.steps
    step = pl.program_id(0)
    inner = v0.shape[0]
    v, g, kept, h_in = (v0, v1), (g0, g1), (kept0, kept1), (h_in0, h_in1)

    @pl.when(step == 0)
    def _():
        dwe[...] = jnp.zeros_like(dwe)
        dg3[...] = jnp.zeros_like(dg3)
        db3[...] = jnp.zeros_like(db3)

    choose_edge(win_b, before, e_l, step == 0)
    stack_taps(stack, DECODER_SHIFTS, win_b, main, None, starts, ends, first_place(step, steps), inner)
    stack[len(DECODER_SHIFTS) * inner :, :] = ones_rows(TILE)
    h3[inner : inner + AUG, :] = ones_rows(TILE)

    def make_out(k):
        out[:, CHAINS[k]] = nn_dot(wet[...], h_in[k][...]) + x1[:, CHAINS[k]].astype(F32)

    def back(k, fill):
        def emit(rows, value):
            evr[rows, CHAINS[k]] = value

        norm_backward(g[k], CHAINS[k], inner, g3, z3, d3, r3, dg3, db3, kept[k], emit, fill, EVERY)

    for k in range(2):
        h_in[k][inner : inner + AUG, :] = ones_rows(HALF)
        g[k][...] = nn_dot(we[...], cot_t[:, CHAINS[k]])
    for k in range(2):
        product(v[k], kt, stack[:, CHAINS[k]])
    for k in range(2):
        norm_forward(v[k], CHAINS[k], inner, f3, b3, h3, z3, d3, r3, at=EVERY, h_copy=h_in[k])
    products = add_product(dwe, h3, cot_t)
    back(0, [lambda: make_out(0), *products[:2]])
    back(1, [lambda: make_out(1), *products[2:]])

    @pl.when(step == steps - 1)
    def _():
        pack_gradients(packed, plan, ((dwe, dwe.shape[1]),), ())


def dec_back_kernel(
    plan, starts, ends, main, after, head, kb, wr, we, g2, g1, g3,
    h2, z2, d2, r2, h1, z1, d1, r1, cot_t, h3, z3, d3, r3, given,
    ey, evr, packed, first, dg2, db2, dg1, db1, dg3, db3,
    dk, dwrt, dwe, stack, win_a, ga0, ga1, gb0, gb1, big0, big1, eur, eur0, eur1, ey0, ey1,
    kept0, kept1, keeps0, keeps1, got, send, recv, *traffic,
):
    steps = plan.steps
    sum_over = Summing(plan.first, given, first, traffic)
    k = sum_over.steps
    due = [0, 1] + [2 + (i * (steps - 3)) // max(1, k - 1) for i in range(k)]
    hook = hooks(steps, [(place, functools.partial(sum_over.reduce_stage, at)) for at, place in enumerate(due)])
    step = pl.program_id(0)
    d, inner = cot_t.shape[0], ga0.shape[0]
    ga, gb, big, eurs, eys = (ga0, ga1), (gb0, gb1), (big0, big1), (eur0, eur1), (ey0, ey1)
    kept, keeps = (kept0, kept1), (keeps0, keeps1)

    @pl.when(step == 0)
    def _():
        for ref in (dk, dwrt, dwe, dg2, db2, dg1, db1, dg3, db3):
            ref[...] = jnp.zeros_like(ref)

    left, right = neighbours()
    to_left = send_copy(head, got, send.at[0], recv.at[0], {"seq": left})

    @pl.when(step == 0)
    def _():
        greet([{"seq": left}, {"seq": right}, *sum_over.partners()])
        to_left.start()

    @pl.when(step == steps - 1)
    def _():
        to_left.wait()

    hook(False)
    choose_edge(win_a, after, got, step == steps - 1)
    back = tuple(-s for s in DECODER_SHIFTS)
    stack_taps(stack, back, None, main, win_a, starts, ends, first_place(step, steps), inner)

    def back2(k, fill):
        def emit(rows, value):
            eur[rows, CHAINS[k]] = value
            eurs[k][rows, :] = value

        norm_backward(ga[k], CHAINS[k], inner, g2, z2, d2, r2, dg2, db2, keeps[k], emit, fill, EVERY)

    def back1(k, fill):
        def emit(rows, value):
            total = value + cot_t[rows, CHAINS[k]]
            ey[rows, CHAINS[k]] = total
            eys[k][rows, :] = total

        norm_backward(big[k], CHAINS[k], d, g1, z1, d1, r1, dg1, db1, kept[k], emit, fill, EVERY)

    def back3(k, fill):
        def emit(rows, value):
            evr[rows, CHAINS[k]] = value

        norm_backward(gb[k], CHAINS[k], inner, g3, z3, d3, r3, dg3, db3, keeps[k], emit, fill, EVERY)

    for k in range(2):
        product(ga[k], kb, stack[:, CHAINS[k]])
    by_k = add_product(dk, h2, stack)
    back2(0, by_k[:2])
    big[0][...] = nn_dot(wr[...], eur0[...])
    back2(1, by_k[2:])
    big[1][...] = nn_dot(wr[...], eur1[...])
    by_r = add_product(dwrt, eur, h1)
    back1(0, by_r[:2])
    gb[0][...] = nn_dot(we[...], ey0[...])
    back1(1, by_r[2:])
    gb[1][...] = nn_dot(we[...], ey1[...])
    by_e = add_product(dwe, h3, ey)
    back3(0, by_e[:2])
    back3(1, by_e[2:])

    @pl.when(step == steps - 1)
    def _():
        pack_gradients(packed, plan, ((dk, dk.shape[1]), (dwrt, d + AUG), (dwe, d)), ())

    hook(True)


def enc_back_kernel(
    plan, starts, ends, before, main, after, head, tail, kb, wr, g2, g1,
    h2, z2, d2, r2, h1, z1, d1, r1, ey, given, first_share, *rest,
):
    vecs, rest = rest[:8], rest[8:]
    (
        grad, packed, summed, first_whole,
        dk, dwrt, dg2, db2, dg1, db1,
        stack, win_b, win_a, ga0, ga1, big0, big1, eur, eur0, eur1, kept0, kept1, keeps0, keeps1,
        got_l, got_r, send, recv, result, first_up, first_sem, vec_sem,
    ), rest = rest[:32], rest[32:]
    held, traffic = rest[:8], rest[8:]
    loads = [pltpu.make_async_copy(vecs[at], held[at], vec_sem.at[at]) for at in range(8)]
    steps = plan.steps
    step = pl.program_id(0)
    d, inner = ey.shape[0], ga0.shape[0]
    ga, big, eurs = (ga0, ga1), (big0, big1), (eur0, eur1)
    kept, keeps = (kept0, kept1), (keeps0, keeps1)

    @pl.when(step == 0)
    def _():
        for load in loads:
            load.start()
        for ref in (dk, dwrt, dg2, db2, dg1, db1):
            ref[...] = jnp.zeros_like(ref)

    sum_over = Summing(plan.early, given, summed, traffic)
    trade_edges(step, steps, head, tail, got_l, got_r, send, recv, sum_over.partners())

    k = sum_over.steps
    due = [0, 1] + [3 + (i * (steps - 3)) // max(1, k - 1) for i in range(k)]
    actions = [(place, functools.partial(sum_over.reduce_stage, at)) for at, place in enumerate(due)]
    first = Summing(plan.first, None, result, (None,) * 8 + (first_up, first_sem))

    def begin():
        first.take_share(first_share)
        first.spread_stage(0)

    actions.append((0, begin))
    actions += [(1 + (steps - 2) * (at + 1) // k, functools.partial(first.spread_stage, at + 1)) for at in range(k)]
    hook = hooks(steps, actions)

    hook(False)
    choose_edge(win_b, before, got_l, step == steps - 1)
    choose_edge(win_a, after, got_r, step == steps - 2)
    back = tuple(-s for s in ENCODER_SHIFTS)
    stack_taps(stack, back, win_b, main, win_a, starts, ends, first_place(later_tile(step, steps), steps), inner)

    def back2(k, fill):
        def emit(rows, value):
            eur[rows, CHAINS[k]] = value
            eurs[k][rows, :] = value

        norm_backward(ga[k], CHAINS[k], inner, g2, z2, d2, r2, dg2, db2, keeps[k], emit, fill, EVERY)

    def back1(k, fill):
        def emit(rows, value):
            grad[rows, CHAINS[k]] = value + ey[rows, CHAINS[k]]

        norm_backward(big[k], CHAINS[k], d, g1, z1, d1, r1, dg1, db1, kept[k], emit, fill, EVERY)

    for k in range(2):
        product(ga[k], kb, stack[:, CHAINS[k]])
    by_k = add_product(dk, h2, stack)
    back2(0, by_k[:2])
    big[0][...] = nn_dot(wr[...], eur0[...])
    back2(1, by_k[2:4])
    big[1][...] = nn_dot(wr[...], eur1[...])
    by_r = add_product(dwrt, eur, h1)
    back1(0, by_k[4:])
    back1(1, by_r)

    @pl.when(step == steps - 1)
    def _():
        in_chunks(plan.first.pieces, lambda at, count: copy_pieces(first_whole, result, at, count))
        for load in loads:
            load.wait()
        sums = (dg1, db1, dg2, db2, *held)
        pack_gradients(packed, plan, ((dk, dk.shape[1]), (dwrt, d + AUG)), sums)

    hook(True)


LARGE = (2, 6, 10, 14, 18, 22)
ROWS_OF = 13


def blocks_of(used):
    return -(-used // LANES)


class Part:
    def __init__(self, sections, vectors, streams, n):
        self.starts, at = {}, 0
        for name, used in sections:
            self.starts[name] = (at, used)
            at += blocks_of(used)
        if vectors:
            self.starts["vec"] = (at, LANES)
            at += 1
        self.filled = at * ROWS_OF
        self.streams = streams
        self.per = -(-self.filled // (streams * n)) * n
        self.pieces = streams * self.per
        self.n = n
        self.rounds, base = [], 1
        while base < n:
            radix = 4 if n // base == 4 else 2
            self.rounds.append((base, radix))
            base *= radix


class Plan:
    def __init__(self, d, inner, steps, n):
        self.d, self.inner, self.steps, self.n = d, inner, steps, n
        self.first = Part((("d_we", d),), False, 2, n)
        early = (("d_k", DECODER_TAPS * inner), ("d_wr", d + AUG), ("e_we", d))
        self.early = Part(early, False, 2, n)
        self.late = Part((("e_k", ENCODER_TAPS * inner), ("e_wr", d + AUG)), True, 4, n)


def pack_gradients(packed, plan, mats, vecs):
    d, inner = plan.d, plan.inner
    half = inner // 2
    for w in range(2):
        at = 0
        for ref, used in mats:
            for b in range(blocks_of(used)):
                stop = min(used, LANES * (b + 1))
                lanes = slice(LANES * b, stop)
                for r in range(ROWS_OF):
                    base = half * w + 16 * r
                    if r < ROWS_OF - 1:
                        value = ref[base : base + 16, lanes]
                    else:
                        value = ref[base : base + 8, lanes]
                        low = ref[inner : inner + 8, lanes] if ref.shape[0] > inner else jnp.zeros_like(value)
                        value = jnp.concatenate([value, low], axis=0)
                    if stop - LANES * b < LANES:
                        blank = jnp.zeros((16, LANES * (b + 1) - stop), F32)
                        value = jnp.concatenate([value, blank], axis=1)
                    packed[w, at] = value.astype(BF)
                    at += 1
        if vecs:
            columns = []
            for ref in vecs:
                total = jnp.sum(ref[...], axis=1, keepdims=True)
                if ref.shape[0] == d:
                    columns.append(total[2 * half * w : 2 * half * w + half])
                    columns.append(total[2 * half * w + half : 2 * half * w + 2 * half])
                else:
                    columns.append(total[half * w : half * (w + 1)])
            lane = lax.broadcasted_iota(jnp.int32, (half, LANES), 1)
            value = jnp.zeros((half, LANES), F32)
            for lane_at, column in enumerate(columns):
                value = jnp.where(lane == lane_at, column, value)
            value = jnp.concatenate([value, jnp.zeros((ROWS_OF * 16 - half, LANES), F32)], axis=0)
            for r in range(ROWS_OF):
                packed[w, at] = value[16 * r : 16 * r + 16].astype(BF)
                at += 1
        left = packed.shape[1] - at
        if left:
            packed[w, at : packed.shape[1]] = jnp.zeros((left, 16, LANES), BF)


def in_chunks(count, body):
    size = max(c for c in range(1, 17) if count % c == 0)

    def step(i, _):
        body(i * size, size)
        return 0

    lax.fori_loop(0, count // size, step, 0)


def copy_pieces(dst, src, at, count):
    dst[pl.ds(at, count)] = src[pl.ds(at, count)]


def hooks(steps, actions):
    step = pl.program_id(0)

    def hook(end):
        for place, action in actions:
            if (place >= steps) == end:

                @pl.when(step == min(place, steps - 1))
                def _(action=action):
                    action()

    return hook


class Summing:
    def __init__(self, part, given, out, traffic):
        self.part, self.given, self.out = part, given, out
        self.got, self.total, self.leave, self.landed, self.core, self.down, self.own, self.own_sem, *up = traffic
        self.up, self.share_sem = up if up else (None, None)
        self.me = lax.axis_index("wa")
        self.seq = lax.axis_index("seq")
        self.steps = len(part.rounds)
        self.orders = []
        for s in range(part.streams):
            order = list(range(self.steps))
            if s % 2 and self.steps > 2:
                order[0], order[1] = order[1], order[0]
            if s % 4 > 1 and self.steps > 2:
                order.insert(1, order.pop())
            self.orders.append(order)

    @staticmethod
    def scratch(part):
        sem = pltpu.SemaphoreType.DMA
        steps = max(1, len(part.rounds))
        pieces = (part.pieces, 16, LANES)
        return [
            pltpu.VMEM(pieces, BF),
            pltpu.VMEM(pieces, F32),
            pltpu.VMEM(pieces, BF),
            pltpu.VMEM(pieces, BF),
            sem((2,)),
            sem((2, steps, part.streams, 3)),
            pltpu.VMEM(pieces, BF),
            sem((1,)),
        ]

    @staticmethod
    def spread_scratch(part):
        return [
            pltpu.SemaphoreType.DMA((2, max(1, len(part.rounds)), part.streams, 3)),
            pltpu.SemaphoreType.DMA((part.streams,)),
        ]

    def digit(self, which, by=0):
        base, radix = self.part.rounds[which]
        return lax.rem(lax.div(self.seq, base) + by, radix)

    def others(self, which):
        return range(1, self.part.rounds[which][1])

    def peer(self, which, by):
        base = self.part.rounds[which][0]
        return {"seq": self.seq + (self.digit(which, by) - self.digit(which)) * base}

    def partners(self):
        peers = [self.peer(which, by) for which in range(self.steps) for by in self.others(which)]
        return [{"wa": 1 - self.me}, *peers]

    def range_at(self, s, k):
        start, size, land = s * self.part.per, self.part.per, s * self.part.per
        for i in range(k):
            radix = self.part.rounds[self.orders[s][i]][1]
            size //= radix
            start = start + self.digit(self.orders[s][i]) * size
            if i < k - 1:
                land += (radix - 1) * size
        return start, size, land

    def core_copy(self):
        return send_copy(
            self.given.at[1 - self.me], self.got, self.core.at[0], self.core.at[1], {"wa": 1 - self.me}
        )

    def own_copy(self):
        return pltpu.make_async_copy(self.given.at[self.me], self.own, self.own_sem.at[0])

    def down_copy(self, s, k, by):
        start, _, _ = self.range_at(s, k)
        _, size, land = self.range_at(s, k + 1)
        which = self.orders[s][k]
        return send_copy(
            self.leave.at[pl.ds(start + self.digit(which, by) * size, size)],
            self.landed.at[pl.ds(land + (by - 1) * size, size)],
            self.down.at[0, k, s, by - 1],
            self.down.at[1, k, s, by - 1],
            self.peer(which, by),
        )

    def up_copy(self, s, k, by):
        start, size, _ = self.range_at(s, k + 1)
        ref = self.out.at[pl.ds(start, size)]
        which = self.orders[s][k]
        return send_copy(ref, ref, self.up.at[0, k, s, by - 1], self.up.at[1, k, s, by - 1], self.peer(which, by))

    def add(self, s, k):
        start, size, land = self.range_at(s, k)

        def summed(at, count):
            if k == 0:
                own = self.own[pl.ds(start + at, count)].astype(F32)
                return own + self.got[pl.ds(start + at, count)].astype(F32)
            total = self.total[pl.ds(start + at, count)]
            for by in self.others(self.orders[s][k - 1]):
                total = total + self.landed[pl.ds(land + (by - 1) * size + at, count)].astype(F32)
            return total

        if k == self.steps:

            def finish(at, count):
                self.out[pl.ds(start + at, count)] = summed(at, count).astype(BF)

            in_chunks(size, finish)
            return
        which = self.orders[s][k]
        part = size // self.part.rounds[which][1]
        for by in self.others(which):
            give = self.digit(which, by) * part

            def to_leave(at, count, give=give):
                self.leave[pl.ds(start + give + at, count)] = summed(give + at, count).astype(BF)

            in_chunks(part, to_leave)
            self.down_copy(s, k, by).start()
        own = self.digit(which) * part

        def to_keep(at, count):
            self.total[pl.ds(start + own + at, count)] = summed(own + at, count)

        in_chunks(part, to_keep)

    def reduce_stage(self, at):
        if at == 0:
            self.core_copy().start()
            self.own_copy().start()
            return
        if at == 1:
            self.core_copy().wait()
            self.own_copy().wait()
        for s in range(self.part.streams):
            if at > 1:
                for by in self.others(self.orders[s][at - 2]):
                    self.down_copy(s, at - 2, by).wait()
            self.add(s, at - 1)

    def spread_stage(self, at):
        for s in range(self.part.streams):
            if at > 0:
                for by in self.others(self.orders[s][self.steps - at]):
                    self.up_copy(s, self.steps - at, by).wait()
            if at < self.steps:
                for by in self.others(self.orders[s][self.steps - at - 1]):
                    self.up_copy(s, self.steps - at - 1, by).start()

    def take_share(self, source):
        copies = []
        for s in range(self.part.streams):
            start, size, _ = self.range_at(s, self.steps)
            where = pl.ds(start, size)
            copies.append(pltpu.make_async_copy(source.at[where], self.out.at[where], self.share_sem.at[s]))
            copies[-1].start()
        for copy in copies:
            copy.wait()


def sum_kernel(plan, late_given, early_share, early_out, late_out, *traffic):
    late = Summing(plan.late, late_given, late_out, traffic[:10])
    early = Summing(plan.early, None, early_out, (None,) * 8 + traffic[10:])
    steps = late.steps
    greet(late.partners())
    late.reduce_stage(0)
    early.take_share(early_share)
    early.spread_stage(0)
    late.reduce_stage(1)
    for at in range(steps):
        early.spread_stage(at + 1)
        late.reduce_stage(at + 2)
    for at in range(steps + 1):
        late.spread_stage(at)


def finish_kernel(plan, grad_low, first, early, late, grad, *rest):
    results, large, stored = list(rest[:24]), rest[24:30], rest[30]
    outs, copies = list(results), []
    for at, place in enumerate(LARGE):
        outs[place] = large[at]
        copies.append(pltpu.make_async_copy(large[at], results[place], stored.at[at]))
    d, inner = plan.d, plan.inner
    half = inner // 2
    grad[...] = grad_low[...].astype(F32)

    @pl.when(pl.program_id(0) == 0)
    def _():
        me = lax.axis_index("wa")

        def matrix(name):
            for part, ref in ((plan.first, first), (plan.early, early), (plan.late, late)):
                if name in part.starts:
                    break
            begin, used = part.starts[name]
            parts = []
            for b in range(begin, begin + blocks_of(used)):
                value = ref[b * ROWS_OF : (b + 1) * ROWS_OF].reshape(ROWS_OF * 16, LANES)
                parts.append(value.astype(F32))
            return jnp.concatenate(parts, axis=1)

        def my_half(line, size):
            return jnp.where(me == 0, line[:, 0:size], line[:, size : 2 * size])

        turned = matrix("vec")[0:half].T

        def write(ref, pieces):
            ref[...] = jnp.concatenate(pieces, axis=1).reshape(ref.shape)

        for side, taps in enumerate((ENCODER_TAPS, DECODER_TAPS)):
            tag = "ed"[side]
            first_g, first_b, red_w, red_b, mid_g, mid_b, ker, ker_b, last_g, last_b, exp_w, exp_b = outs[
                12 * side : 12 * side + 12
            ]
            at = 8 * side
            write(first_g, [turned[at : at + 1], turned[at + 1 : at + 2]])
            write(first_b, [turned[at + 2 : at + 3], turned[at + 3 : at + 4]])
            write(mid_g, [turned[at + 4 : at + 5]])
            write(mid_b, [turned[at + 5 : at + 6]])
            write(last_g, [turned[at + 6 : at + 7]])
            write(last_b, [turned[at + 7 : at + 8]])
            value = matrix(tag + "_we")
            exp_w[...] = value[0:half, 0:d]
            write(exp_b, [my_half(value[half : half + 1, 0:d], d // 2)])
            value = matrix(tag + "_k")
            for j in range(taps):
                ker[j] = jnp.concatenate([value[0:half, place] for _, place in tap_pieces(j, taps, inner)], axis=1)
            centre = (ENCODER_SHIFTS if side == 0 else DECODER_SHIFTS).index(0)
            sums = [value[half : half + 1, place] for _, place in tap_pieces(centre, taps, inner)]
            write(ker_b, [my_half(jnp.concatenate(sums, axis=1), half)])
            value = matrix(tag + "_wr")[0:half]
            red_w[...] = value[:, 0:d]
            write(red_b, [value[:, d:].T[0:1]])
            for copy in copies[3 * side : 3 * side + 3]:
                copy.start()

    @pl.when(pl.program_id(0) == plan.steps - 1)
    def _():
        for copy in copies:
            copy.wait()


def local(n, stream, doc_start, doc_end, cotangent, *weights):
    rows, d = stream.shape[1], stream.shape[2]
    inner = weights[6].shape[1] * 2
    steps = rows // TILE
    x, cot = stream[0].T, cotangent[0].T
    starts, ends = doc_start, doc_end
    weights = [w.T if at % 12 == 2 else w for at, w in enumerate(weights)]
    enc, dec = gather_weights(weights, d, inner)
    wrt_e, kt_e, wet_e, we_e, kb_e, wr_e, g1_e, f1_e, b1_e, g2_e, f2_e, b2_e, g3_e, f3_e, b3_e = enc
    wrt_d, kt_d, wet_d, we_d, kb_d, wr_d, g1_d, f1_d, b1_d, g2_d, f2_d, b2_d, g3_d, f3_d, b3_d = dec

    plan = Plan(d, inner, steps, n)
    blocks = rows // LANES
    per = TILE // LANES

    def spec(a):
        return whole(a.shape)

    def wide(channels, dtype=BF):
        return jax.ShapeDtypeStruct((channels, rows), dtype)

    def fixed(shape, dtype=F32):
        return jax.ShapeDtypeStruct(shape, dtype)

    class Order:
        def __init__(self, first):
            self.tile = lambda i: (i + first) % steps

        def cols(self, channels):
            return pl.BlockSpec((channels, TILE), lambda i: (0, self.tile(i)))

        def before(self, channels):
            return pl.BlockSpec((channels, LANES), lambda i: (0, (per * self.tile(i) + blocks - 1) % blocks))

        def after(self, channels):
            return pl.BlockSpec((channels, LANES), lambda i: (0, (per * self.tile(i) + per) % blocks))

    def head(channels):
        return pl.BlockSpec((channels, LANES), lambda i: (0, 0))

    def tail(channels):
        return pl.BlockSpec((channels, LANES), lambda i: (0, blocks - 1))

    plain, later = Order(0), Order(1)
    d1, i1 = d + AUG, inner + AUG
    norm_wide = [(d1, BF), (d, BF), (d, BF), (8, F32)]
    norm_in = [(i1, BF), (inner, BF), (inner, BF), (8, F32)]
    sem = pltpu.SemaphoreType.DMA
    vmem = pltpu.VMEM
    anywhere = pl.BlockSpec(memory_space=pl.ANY)

    def outs_of(order, items):
        return [wide(c, t) for c, t in items], [order.cols(c) for c, _ in items]

    shapes, specs = outs_of(plain, norm_wide + norm_in)
    ins = [wrt_e, f1_e, b1_e, f2_e, b2_e]
    h1e, z1e, d1e, r1e, h2e, z2e, d2e, r2e = pl.pallas_call(
        enc_in_kernel,
        grid=(steps,),
        out_shape=shapes,
        in_specs=[plain.cols(d)] + [spec(a) for a in ins],
        out_specs=specs,
        scratch_shapes=[vmem((d, TILE), F32)] + [vmem((inner, HALF), F32)] * 2 + [vmem((d1, HALF), BF)] * 2,
        compiler_params=params(),
        name="encoder_in",
    )(x, *ins)

    shapes, specs = outs_of(later, norm_in + [(d, BF)] + norm_wide + norm_in)
    ins = [kt_e, wet_e, wrt_d, f3_e, b3_e, f1_d, b1_d, f2_d, b2_d]
    h3e, z3e, d3e, r3e, x1, h1d, z1d, d1d, r1d, h2d, z2d, d2d, r2d, edge_d = pl.pallas_call(
        functools.partial(enc_out_kernel, steps),
        grid=(steps,),
        out_shape=shapes + [fixed((i1, LANES), BF)],
        in_specs=[later.cols(1), later.cols(1), later.before(i1), later.cols(i1), later.after(i1)]
        + [head(i1), tail(i1), later.cols(d)]
        + [spec(a) for a in ins],
        out_specs=specs + [whole((i1, LANES))],
        scratch_shapes=[
            vmem((ENCODER_TAPS * inner + AUG, TILE), BF),
            vmem((inner, LANES), BF),
            vmem((inner, LANES), BF),
        ]
        + [vmem((inner, HALF), F32)] * 2
        + [vmem((d, HALF), F32)] * 2
        + [vmem((inner, HALF), F32)] * 2
        + [vmem((i1, HALF), BF)] * 2
        + [vmem((d1, HALF), BF)] * 2
        + [vmem((i1, LANES), BF)] * 4
        + [sem((3,)), sem((3,))],
        compiler_params=params(1),
        name="encoder_out",
    )(starts, ends, h2e, h2e, h2e, h2e, h2e, x, *ins)

    small, large = fixed((inner, LANES)), fixed((d, LANES))
    sums = [fixed((2, plan.first.pieces, 16, LANES), BF), small, small]
    ins = [kt_d, we_d, wet_d, f3_d, b3_d, g3_d]
    out, evr_d, packed_first, dg3_d, db3_d = pl.pallas_call(
        functools.partial(dec_out_kernel, plan),
        grid=(steps,),
        out_shape=[wide(d, F32), wide(inner)] + sums,
        in_specs=[plain.cols(1), plain.cols(1), plain.before(i1), plain.cols(i1), spec(edge_d)]
        + [plain.cols(d), plain.cols(d)]
        + [spec(a) for a in ins],
        out_specs=[plain.cols(d), plain.cols(inner)] + [whole(s.shape) for s in sums],
        scratch_shapes=[
            vmem((i1, d), F32),
            vmem((DECODER_TAPS * inner + AUG, TILE), BF),
            vmem((inner, LANES), BF),
            vmem((inner, HALF), F32),
            vmem((inner, HALF), F32),
            vmem((i1, TILE), BF),
            vmem((inner, TILE), BF),
            vmem((inner, TILE), BF),
            vmem((8, TILE), F32),
        ]
        + [vmem((inner, HALF), F32)] * 2
        + [vmem((inner, HALF), BF)] * 2
        + [vmem((i1, HALF), BF)] * 2,
        compiler_params=params(),
        name="decoder_out",
    )(starts, ends, h2d, h2d, edge_d, cot, x1, *ins)

    shapes, specs = outs_of(plain, [(d, BF), (inner, BF)])
    early = fixed((2, plan.early.pieces, 16, LANES), BF)
    first = fixed((plan.first.pieces, 16, LANES), BF)
    sums = [small, small, large, large, small, small]
    ins = [kb_d, wr_d, we_e, g2_d, g1_d, g3_e]
    stash = [h2d, z2d, d2d, r2d, h1d, z1d, d1d, r1d, cot, h3e, z3e, d3e, r3e]
    ey, evr_e, packed, first_share, dg2_d, db2_d, dg1_d, db1_d, dg3_e, db3_e = pl.pallas_call(
        functools.partial(dec_back_kernel, plan),
        grid=(steps,),
        out_shape=shapes + [early, first] + sums,
        in_specs=[plain.cols(1), plain.cols(1), plain.cols(inner), plain.after(inner), head(inner)]
        + [spec(a) for a in ins]
        + [plain.cols(a.shape[0]) for a in stash]
        + [anywhere],
        out_specs=specs + [whole(early.shape), whole(first.shape)] + [whole(s.shape) for s in sums],
        scratch_shapes=[
            vmem((i1, DECODER_TAPS * inner), F32),
            vmem((inner, d1), F32),
            vmem((i1, d), F32),
            vmem((DECODER_TAPS * inner, TILE), BF),
            vmem((inner, LANES), BF),
        ]
        + [vmem((inner, HALF), F32)] * 4
        + [vmem((d, HALF), F32)] * 2
        + [vmem((inner, TILE), BF)]
        + [vmem((inner, HALF), BF)] * 2
        + [vmem((d, HALF), BF)] * 4
        + [vmem((inner, HALF), BF)] * 2
        + [vmem((inner, LANES), BF), sem((1,)), sem((1,))]
        + Summing.scratch(plan.first),
        compiler_params=params(2),
        name="decoder_back",
    )(starts, ends, evr_d, evr_d, evr_d, *ins, *stash, packed_first)

    late = fixed((2, plan.late.pieces, 16, LANES), BF)
    early_sum = fixed((plan.early.pieces, 16, LANES), BF)
    ins = [kb_e, wr_e, g2_e, g1_e]
    stash = [h2e, z2e, d2e, r2e, h1e, z1e, d1e, r1e, ey]
    vecs = [dg3_e, db3_e, dg1_d, db1_d, dg2_d, db2_d, dg3_d, db3_d]
    grad_low, packed_late, summed, first_whole = pl.pallas_call(
        functools.partial(enc_back_kernel, plan),
        grid=(steps,),
        out_shape=[wide(d), late, early_sum, first],
        in_specs=[later.cols(1), later.cols(1), later.before(inner), later.cols(inner), later.after(inner)]
        + [head(inner), tail(inner)]
        + [spec(a) for a in ins]
        + [later.cols(a.shape[0]) for a in stash]
        + [anywhere] * (2 + len(vecs)),
        out_specs=[later.cols(d), whole(late.shape), whole(early_sum.shape), whole(first.shape)],
        scratch_shapes=[
            vmem((i1, ENCODER_TAPS * inner), F32),
            vmem((inner, d1), F32),
            vmem((inner, LANES), F32),
            vmem((inner, LANES), F32),
            vmem((d, LANES), F32),
            vmem((d, LANES), F32),
            vmem((ENCODER_TAPS * inner, TILE), BF),
            vmem((inner, LANES), BF),
            vmem((inner, LANES), BF),
        ]
        + [vmem((inner, HALF), F32)] * 2
        + [vmem((d, HALF), F32)] * 2
        + [vmem((inner, TILE), BF)]
        + [vmem((inner, HALF), BF)] * 2
        + [vmem((d, HALF), BF)] * 2
        + [vmem((inner, HALF), BF)] * 2
        + [vmem((inner, LANES), BF)] * 2
        + [sem((2,)), sem((2,)), vmem(first.shape, BF)]
        + Summing.spread_scratch(plan.first)
        + [sem((8,))]
        + [vmem(a.shape, F32) for a in vecs]
        + Summing.scratch(plan.early),
        compiler_params=params(3),
        name="encoder_back",
    )(starts, ends, evr_e, evr_e, evr_e, evr_e, evr_e, *ins, *stash, packed, first_share, *vecs)

    vm = pl.BlockSpec(memory_space=pltpu.VMEM)
    early_whole, late_whole = pl.pallas_call(
        functools.partial(sum_kernel, plan),
        out_shape=[early_sum, fixed((plan.late.pieces, 16, LANES), BF)],
        in_specs=[anywhere, anywhere],
        out_specs=[vm, vm],
        scratch_shapes=Summing.scratch(plan.late)
        + Summing.spread_scratch(plan.late)
        + Summing.spread_scratch(plan.early),
        compiler_params=params(4),
        name="sum_gradients",
    )(packed_late, summed)

    grad, *shares = pl.pallas_call(
        functools.partial(finish_kernel, plan),
        grid=(steps,),
        out_shape=[wide(d, F32)] + [fixed(w.shape) for w in weights],
        in_specs=[plain.cols(d), whole(first_whole.shape), whole(early_whole.shape), whole(late_whole.shape)],
        out_specs=[plain.cols(d)]
        + [pl.BlockSpec(memory_space=pl.ANY) if at in LARGE else whole(w.shape) for at, w in enumerate(weights)],
        scratch_shapes=[vmem(weights[at].shape, F32) for at in LARGE] + [sem((len(LARGE),))],
        compiler_params=params(),
        name="finish",
    )(grad_low, first_whole, early_whole, late_whole)
    shares = [w.T if at % 12 == 2 else w for at, w in enumerate(shares)]
    return (out.T[None], grad.T[None], *shares)


def solution(mesh):
    rows = P("wa", "seq", None)
    block = (
        P("wa"), P("wa"), P(None, "wa"), P("wa"), P("wa"), P("wa"),
        P(None, "wa", None), P("wa"), P("wa"), P("wa"), P("wa", None), P("wa"),
    )
    return jax.shard_map(
        functools.partial(local, mesh.shape["seq"]),
        mesh=mesh,
        in_specs=(rows, P("wa", "seq"), P("wa", "seq"), rows, *block, *block),
        out_specs=(rows, rows, *block, *block),
        check_vma=False,
    )
```
